32 devices in a mesh: dp: 8 (over y, x, core), mp: 4 (over z).
Axes of the slice: x: 2, y: 2, z: 4, core: 2. Of those that a mesh axis runs over, the one named last changes fastest.
Arguments:
- hidden: bfloat16 [128, 64, 768], P('dp'), may hold values from -6 to 6
- images: bfloat16 [128, 257, 1408], P('dp'), may hold values from -6 to 6
- caption_len: int32 [128], P('dp'), may hold values from 5 to 32, as said below
- cotangent: bfloat16 [128, 64, 768], P('dp'), may hold values from -6 to 6
- attn_in: float32 [4, 768, 768], P(None, 'dp', 'mp'), may hold values from -0.21875 to 0.21875
- attn_in_first: float32 [4, 768, 768], P(None, 'dp', 'mp'), may hold values from -24 to 24
- attn_in_second: float32 [4, 768, 768], P(None, 'dp', 'mp'), may hold values from 1.31072 to 5.24288
- attn_out: float32 [2, 768, 768], P(None, 'mp', 'dp'), may hold values from -0.625 to 0.625
- attn_out_first: float32 [2, 768, 768], P(None, 'mp', 'dp'), may hold values from -12 to 12
- attn_out_second: float32 [2, 768, 768], P(None, 'mp', 'dp'), may hold values from 0.32768 to 1.31072
- cross_key_value_maps: float32 [2, 1408, 768], P(None, 'dp', 'mp'), may hold values from -0.15625 to 0.15625
- cross_kv_first: float32 [2, 1408, 768], P(None, 'dp', 'mp'), may hold values from -6 to 6
- cross_kv_second: float32 [2, 1408, 768], P(None, 'dp', 'mp'), may hold values from 0.08224 to 0.32896
- ffn_up: float32 [2, 768, 3072], P(None, 'dp', 'mp'), may hold values from -0.21875 to 0.21875
- ffn_up_first: float32 [2, 768, 3072], P(None, 'dp', 'mp'), may hold values from -8 to 8
- ffn_up_second: float32 [2, 768, 3072], P(None, 'dp', 'mp'), may hold values from 0.16384 to 0.65536
- ffn_down: float32 [2, 3072, 768], P(None, 'mp', 'dp'), may hold values from -0.109375 to 0.109375
- ffn_down_first: float32 [2, 3072, 768], P(None, 'mp', 'dp'), may hold values from -20 to 20
- ffn_down_second: float32 [2, 3072, 768], P(None, 'mp', 'dp'), may hold values from 1.024 to 4.096
- vec_rep: float32 [12, 768], replicated
- vec_rep_first: float32 [12, 768], replicated, may hold values from -40 to 40
- vec_rep_second: float32 [12, 768], replicated, may hold values from 4.01408 to 16.05632
- query_value_bias_rows: float32 [4, 768], P(None, 'mp'), may hold values from -1.25 to 1.25
- vec_head_first: float32 [4, 768], P(None, 'mp'), may hold values from -24 to 24
- vec_head_second: float32 [4, 768], P(None, 'mp'), may hold values from 1.31072 to 5.24288
- bias_up: float32 [2, 3072], P(None, 'mp'), may hold values from -1.25 to 1.25
- bias_up_first: float32 [2, 3072], P(None, 'mp'), may hold values from -8 to 8
- bias_up_second: float32 [2, 3072], P(None, 'mp'), may hold values from 0.16384 to 0.65536
Outputs:
- layer_out: bfloat16 [128, 64, 768], P('dp')
- grad_hidden: float32 [128, 64, 768], P('dp')
- attn_in_moment: float32 [4, 768, 768], P(None, 'dp', 'mp')
- attn_in_square: float32 [4, 768, 768], P(None, 'dp', 'mp')
- attn_in_next: float32 [4, 768, 768], P(None, 'dp', 'mp')
- attn_out_moment: float32 [2, 768, 768], P(None, 'mp', 'dp')
- attn_out_square: float32 [2, 768, 768], P(None, 'mp', 'dp')
- attn_out_next: float32 [2, 768, 768], P(None, 'mp', 'dp')
- cross_kv_moment: float32 [2, 1408, 768], P(None, 'dp', 'mp')
- cross_kv_square: float32 [2, 1408, 768], P(None, 'dp', 'mp')
- cross_kv_next: float32 [2, 1408, 768], P(None, 'dp', 'mp')
- ffn_up_moment: float32 [2, 768, 3072], P(None, 'dp', 'mp')
- ffn_up_square: float32 [2, 768, 3072], P(None, 'dp', 'mp')
- ffn_up_next: float32 [2, 768, 3072], P(None, 'dp', 'mp')
- ffn_down_moment: float32 [2, 3072, 768], P(None, 'mp', 'dp')
- ffn_down_square: float32 [2, 3072, 768], P(None, 'mp', 'dp')
- ffn_down_next: float32 [2, 3072, 768], P(None, 'mp', 'dp')
- vec_rep_moment: float32 [12, 768], replicated
- vec_rep_square: float32 [12, 768], replicated
- vec_rep_next: float32 [12, 768], replicated
- vec_head_moment: float32 [4, 768], P(None, 'mp')
- vec_head_square: float32 [4, 768], P(None, 'mp')
- vec_head_next: float32 [4, 768], P(None, 'mp')
- bias_up_moment: float32 [2, 3072], P(None, 'mp')
- bias_up_square: float32 [2, 3072], P(None, 'mp')
- bias_up_next: float32 [2, 3072], P(None, 'mp')
The draws below stay inside these ranges and needn't reach their ends.
Inputs may be any that keep to these rules, and one draw needn't show every extreme that they name: `caption_len`: in the items of one index of dp some item has 32 caption tokens.
All inputs are finite; a program needn't handle non-finite values.
Results may differ from the reference program's by a relative error of at most 0.02.
Values may be sent and summed in bfloat16 or wider, within the bound.
No kernel may reach another device: no remote copies, remote signals or barrier semaphores. Data moves between devices by JAX's collectives and lax.ppermute only.
A program may use at most 192 MiB of HBM per device.

```python
import math
import jax
import jax.numpy as jnp
from jax import lax

D = 768
HEADS = 12
HEAD_DIM = 64
F = 3072
E = 1408
IMG = 257
NQ = 32
NT = 32
ITEMS_DEV = 16
STEP_COUNT = 10
ROWS = 64
ITEMS = 128
ROWS_ALL = 8192
KEYS_ALL = 32896


def draw_caption_len(key, part):
    key = jax.random.fold_in(key, 11)
    first_key, second_key = jax.random.split(key)
    lengths = jax.random.randint(first_key, (ITEMS,), 5, NT + 1)
    chosen = jax.random.randint(second_key, (ITEMS // ITEMS_DEV, 1), 0, ITEMS_DEV)
    longest = jnp.arange(ITEMS_DEV)[None, :] == chosen
    return jnp.where(longest, NT, lengths.reshape(ITEMS // ITEMS_DEV, ITEMS_DEV)).reshape(ITEMS).astype(jnp.int32)


def draw_vec_rep(key, part):
    key = jax.random.fold_in(key, 7)
    rows = jnp.arange(12)[:, None]
    is_gain = (rows == 4) | (rows == 6) | (rows == 8) | (rows == 10)
    noise = jax.random.normal(key, (12, D), jnp.float32)
    return jnp.where(is_gain, 1.0 + 0.1 * noise, 0.2 * noise).astype(jnp.float32)


def levels(key, extent, cuts, least, largest):
    def one(dim, parts):
        steps = jax.random.uniform(jax.random.fold_in(jax.random.fold_in(key, 6), dim), (parts,), jnp.float32, least / len(cuts), largest / len(cuts))
        return jnp.repeat(jnp.exp(steps), extent[dim] // parts).reshape((-1,) + (1,) * (len(extent) - dim - 1))

    factor_of = one(*cuts[0])
    for cut in cuts[1:]:
        factor_of = factor_of * one(*cut)
    return factor_of


def normal_values(own_key, extent, scale, bound, cuts=(), held_as=jnp.bfloat16):
    entries = jax.random.normal(own_key, extent, jnp.float32) * scale
    if len(cuts) > 0:
        entries = levels(own_key, extent, cuts, -0.22, 0.18) * entries
    return jnp.clip(entries, min=-bound, max=bound).astype(held_as)


def setup_inputs(seed: int = 0) -> dict:
    streams_of = jax.random.split(jax.random.key(seed), 29)
    return {
        "hidden": normal_values(streams_of[0], (ITEMS, ROWS, D), 1.0, 6.0, ((0, 8),)),
        "images": normal_values(streams_of[1], (ITEMS, IMG, E), 1.0, 6.0, ((0, 8),)),
        "caption_len": draw_caption_len(jax.random.fold_in(streams_of[28], 71), 0),
        "cotangent": normal_values(streams_of[3], (ITEMS, ROWS, D), 1.0, 6.0, ((0, 8),)),
        "attn_in": normal_values(streams_of[4], (4, D, D), D ** -0.5, 0.21875, ((1, 8), (2, 4)), jnp.float32),
        "attn_in_first": normal_values(streams_of[5], (4, D, D), (0.044 * ROWS_ALL ** 0.5), 24.0, ((1, 8), (2, 4)), jnp.float32),
        "attn_in_second": jnp.clip(jnp.exp(math.log(5.24288) - 1.3862944 * jax.random.uniform(streams_of[6], (4, D, D), jnp.float32) ** levels(streams_of[6], (4, D, D), ((1, 8), (2, 4)), -0.2, 0.2)), 1.31072, 5.24288),
        "attn_out": normal_values(streams_of[7], (2, D, D), (max(D // 8, 1)) ** -0.5, 0.625, ((1, 4), (2, 8)), jnp.float32),
        "attn_out_first": normal_values(streams_of[8], (2, D, D), (0.022 * ROWS_ALL ** 0.5), 12.0, ((1, 4), (2, 8)), jnp.float32),
        "attn_out_second": jnp.clip(jnp.exp(math.log(1.31072) - 1.3862944 * jax.random.uniform(streams_of[9], (2, D, D), jnp.float32) ** levels(streams_of[9], (2, D, D), ((1, 4), (2, 8)), -0.2, 0.2)), 0.32768, 1.31072),
        "cross_key_value_maps": normal_values(streams_of[10], (2, E, D), E ** -0.5, 0.15625, ((1, 8), (2, 4)), jnp.float32),
        "cross_kv_first": normal_values(streams_of[11], (2, E, D), (0.0056 * KEYS_ALL ** 0.5), 6.0, ((1, 8), (2, 4)), jnp.float32),
        "cross_kv_second": jnp.clip(jnp.exp(math.log(0.32896) - 1.3862944 * jax.random.uniform(streams_of[12], (2, E, D), jnp.float32) ** levels(streams_of[12], (2, E, D), ((1, 8), (2, 4)), -0.2, 0.2)), 0.08224, 0.32896),
        "ffn_up": normal_values(streams_of[13], (2, D, F), D ** -0.5, 0.21875, ((1, 8), (2, 4)), jnp.float32),
        "ffn_up_first": normal_values(streams_of[14], (2, D, F), (0.022 * (ITEMS * NQ) ** 0.5), 8.0, ((1, 8), (2, 4)), jnp.float32),
        "ffn_up_second": jnp.clip(jnp.exp(math.log(0.65536) - 1.3862944 * jax.random.uniform(streams_of[15], (2, D, F), jnp.float32) ** levels(streams_of[15], (2, D, F), ((1, 8), (2, 4)), -0.2, 0.2)), 0.16384, 0.65536),
        "ffn_down": normal_values(streams_of[16], (2, F, D), F ** -0.5, 0.109375, ((1, 4), (2, 8)), jnp.float32),
        "ffn_down_first": normal_values(streams_of[17], (2, F, D), (0.056 * (ITEMS * NQ) ** 0.5), 20.0, ((1, 4), (2, 8)), jnp.float32),
        "ffn_down_second": jnp.clip(jnp.exp(math.log(4.096) - 1.3862944 * jax.random.uniform(streams_of[18], (2, F, D), jnp.float32) ** levels(streams_of[18], (2, F, D), ((1, 4), (2, 8)), -0.2, 0.2)), 1.024, 4.096),
        "vec_rep": draw_vec_rep(jax.random.fold_in(streams_of[28], 71), 0),
        "vec_rep_first": normal_values(streams_of[20], (12, D), (0.078 * ROWS_ALL ** 0.5), 40.0, (), jnp.float32),
        "vec_rep_second": jnp.clip(jnp.exp(jax.random.uniform(streams_of[21], (12, D), jnp.float32, math.log(4.01408), math.log(16.05632))), 4.01408, 16.05632),
        "query_value_bias_rows": normal_values(streams_of[22], (4, D), 0.2, 1.25, ((1, 4),), jnp.float32),
        "vec_head_first": normal_values(streams_of[23], (4, D), (0.044 * ROWS_ALL ** 0.5), 24.0, ((1, 4),), jnp.float32),
        "vec_head_second": jnp.clip(jnp.exp(math.log(5.24288) - 1.3862944 * jax.random.uniform(streams_of[24], (4, D), jnp.float32) ** levels(streams_of[24], (4, D), ((1, 4),), -0.2, 0.2)), 1.31072, 5.24288),
        "bias_up": normal_values(streams_of[25], (2, F), 0.2, 1.25, ((1, 4),), jnp.float32),
        "bias_up_first": normal_values(streams_of[26], (2, F), (0.022 * (ITEMS * NQ) ** 0.5), 8.0, ((1, 4),), jnp.float32),
        "bias_up_second": jnp.clip(jnp.exp(math.log(0.65536) - 1.3862944 * jax.random.uniform(streams_of[27], (2, F), jnp.float32) ** levels(streams_of[27], (2, F), ((1, 4),), -0.2, 0.2)), 0.16384, 0.65536),
    }


PRECISION_MAXIMUM = lax.Precision.HIGHEST
NORM_EPS = 1e-06
BETA_ONE = 0.9
BETA_TWO = 0.999
ADAM_EPS = 1e-08
WEIGHT_DECAY = 0.01
MASKED = -1000000000.0

@jax.custom_vjp
def reduced_precision(v):
    return lax.optimization_barrier(v.astype(jnp.bfloat16)).astype(jnp.float32)

@jax.custom_vjp
def low_back(v):
    return v

def low_keep(v):
    return (reduced_precision(v), None)

def low_pass(kept, grad):
    return (grad,)

def back_keep(v):
    return (v, None)

def back_low(kept, grad):
    return (reduced_precision(grad),)
reduced_precision.defvjp(low_keep, low_pass)
low_back.defvjp(back_keep, back_low)

def forward_and_backward(values):
    return reduced_precision(low_back(values))

def layer_norm(values, gain, shift):
    center = values - lax.optimization_barrier(jnp.mean(values, axis=-1, keepdims=True))
    spread = lax.optimization_barrier(jnp.mean(center * center, axis=-1, keepdims=True))
    return center * lax.rsqrt(spread + NORM_EPS) * gain + shift

def project(values, weight):
    return jnp.einsum('nrd,de->nre', values, weight, precision=PRECISION_MAXIMUM)

def attention(query_rows, key_rows, value_rows, mask_add):
    count = query_rows.shape[0]
    length = query_rows.shape[1]
    query_heads = query_rows.reshape(count, length, HEADS, HEAD_DIM)
    key_heads = key_rows.reshape(count, key_rows.shape[1], HEADS, HEAD_DIM)
    value_heads = value_rows.reshape(count, value_rows.shape[1], HEADS, HEAD_DIM)
    scores = jnp.einsum('nqhc,nkhc->nhqk', query_heads, key_heads, precision=PRECISION_MAXIMUM) * HEAD_DIM ** (-0.5) + mask_add
    scores = low_back(scores)
    top = lax.optimization_barrier(jnp.max(scores, axis=-1, keepdims=True))
    expo = jnp.exp(scores - top)
    probs = reduced_precision(expo / lax.optimization_barrier(jnp.sum(expo, axis=-1, keepdims=True)))
    context = jnp.einsum('nhqk,nkhc->nqhc', probs, value_heads, precision=PRECISION_MAXIMUM)
    return context.reshape(count, length, HEADS * HEAD_DIM)

def ffn_group(values, up_weight, up_bias, down_weight, down_bias, gain, shift):
    up_pre = low_back(jnp.einsum('nrd,df->nrf', reduced_precision(values), reduced_precision(up_weight), precision=PRECISION_MAXIMUM) + up_bias)
    up_act = reduced_precision(jax.nn.gelu(up_pre, approximate=False))
    down_branch = low_back(jnp.einsum('nrf,fd->nrd', up_act, reduced_precision(down_weight), precision=PRECISION_MAXIMUM) + down_bias)
    return layer_norm(values + down_branch, gain, shift)

def forward(tokens, image_feature_rows, lengths, attn_in, attn_out, cross_key_value_maps, ffn_up, ffn_down, vec_rep, query_value_bias_rows, bias_up):
    positions = jnp.arange(ROWS)
    valid = (positions[None, :] < NQ) | (positions[None, :] - NQ < lengths[:, None])
    mask_add = jnp.where(valid, 0.0, MASKED).astype(jnp.float32)[:, None, None, :]
    self_query = forward_and_backward(project(tokens, reduced_precision(attn_in[0])) + query_value_bias_rows[0])
    self_key = forward_and_backward(project(tokens, reduced_precision(attn_in[1])))
    self_value = forward_and_backward(project(tokens, reduced_precision(attn_in[2])) + query_value_bias_rows[1])
    self_context = forward_and_backward(attention(self_query, self_key, self_value, mask_add))
    self_branch = low_back(project(self_context, reduced_precision(attn_out[0])) + vec_rep[0])
    first_out = layer_norm(tokens + self_branch, vec_rep[4], vec_rep[5])
    query_part = first_out[:, :NQ]
    cross_query = forward_and_backward(project(reduced_precision(query_part), reduced_precision(attn_in[3])) + query_value_bias_rows[2])
    cross_attention_key = forward_and_backward(jnp.einsum('jkw,wr->jkr', image_feature_rows, reduced_precision(cross_key_value_maps[0]), precision=PRECISION_MAXIMUM))
    cross_attention_value = forward_and_backward(jnp.einsum('jkw,wr->jkr', image_feature_rows, reduced_precision(cross_key_value_maps[1]), precision=PRECISION_MAXIMUM) + query_value_bias_rows[3])
    cross_context = forward_and_backward(attention(cross_query, cross_attention_key, cross_attention_value, jnp.float32(0.0)))
    cross_branch = low_back(project(cross_context, reduced_precision(attn_out[1])) + vec_rep[1])
    second_query = layer_norm(query_part + cross_branch, vec_rep[6], vec_rep[7])
    query_final = ffn_group(second_query, ffn_up[0], bias_up[0], ffn_down[0], vec_rep[2], vec_rep[8], vec_rep[9])
    caption_final = ffn_group(first_out[:, NQ:], ffn_up[1], bias_up[1], ffn_down[1], vec_rep[3], vec_rep[10], vec_rep[11])
    return jnp.concatenate([query_final, caption_final], axis=1)

def adam_update(weight, first, second, grad, rate):
    first_new = BETA_ONE * first + (1.0 - BETA_ONE) * grad
    second_new = BETA_TWO * second + (1.0 - BETA_TWO) * grad * grad
    first_hat = first_new / (1.0 - BETA_ONE ** STEP_COUNT)
    second_hat = second_new / (1.0 - BETA_TWO ** STEP_COUNT)
    weight_new = weight - rate * (first_hat / (jnp.sqrt(second_hat) + ADAM_EPS) + WEIGHT_DECAY * weight)
    return (first_new, second_new, weight_new)

def learning_rates():
    return (2.0 / math.sqrt(D), 2.0 / math.sqrt(max(D // 8, 1)), 2.0 / math.sqrt(E), 2.0 / math.sqrt(D), 2.0 / math.sqrt(F), 0.3, 0.3, 0.3)

def reference(hidden, images, caption_len, cotangent, attn_in, attn_in_first, attn_in_second, attn_out, attn_out_first, attn_out_second, cross_key_value_maps, cross_kv_first, cross_kv_second, ffn_up, ffn_up_first, ffn_up_second, ffn_down, ffn_down_first, ffn_down_second, vec_rep, vec_rep_first, vec_rep_second, query_value_bias_rows, vec_head_first, vec_head_second, bias_up, bias_up_first, bias_up_second):
    params = (attn_in, attn_out, cross_key_value_maps, ffn_up, ffn_down, vec_rep, query_value_bias_rows, bias_up)
    firsts = (attn_in_first, attn_out_first, cross_kv_first, ffn_up_first, ffn_down_first, vec_rep_first, vec_head_first, bias_up_first)
    seconds = (attn_in_second, attn_out_second, cross_kv_second, ffn_up_second, ffn_down_second, vec_rep_second, vec_head_second, bias_up_second)
    block = math.gcd(ITEMS, 64)
    groups = ITEMS // block

    def one_block(carry, pieces):
        tokens, image_feature_rows, lengths, grad_top = pieces
        image_float = image_feature_rows.astype(jnp.float32)

        def local(token_values, *weights):
            return forward(token_values, image_float, lengths, *weights)
        result, pull = jax.vjp(local, tokens.astype(jnp.float32), *params)
        grads = pull(grad_top.astype(jnp.float32))
        totals = tuple((total + grad for total, grad in zip(carry, grads[1:])))
        return (totals, (result.astype(jnp.bfloat16), grads[0]))
    start = tuple((jnp.zeros_like(weight) for weight in params))
    pieces = (hidden.reshape(groups, block, ROWS, D), images.reshape(groups, block, IMG, E), caption_len.reshape(groups, block).astype(jnp.int32), cotangent.reshape(groups, block, ROWS, D))
    totals, (mixed_rows, grad_rows) = lax.scan(one_block, start, pieces)
    layer_out = mixed_rows.reshape(ITEMS, ROWS, D)
    grad_hidden = grad_rows.reshape(ITEMS, ROWS, D)
    results = []
    for weight, first, second, grad, rate in zip(params, firsts, seconds, totals, learning_rates()):
        results.extend(adam_update(weight, first, second, grad, rate))
    return (layer_out, grad_hidden, results[0], results[1], results[2], results[3], results[4], results[5], results[6], results[7], results[8], results[9], results[10], results[11], results[12], results[13], results[14], results[15], results[16], results[17], results[18], results[19], results[20], results[21], results[22], results[23])
```

```python
import math

import jax
import jax.numpy as jnp
from jax import lax
from jax.sharding import Mesh
from jax.sharding import PartitionSpec as P

D = 768
HEAD_DIM = 64
F = 3072
E = 1408
NQ = 32
STEP_COUNT = 10

NORM_EPS = 1e-06
BETA_ONE = 0.9
BETA_TWO = 0.999
ADAM_EPS = 1e-08
WEIGHT_DECAY = 0.01
MASKED = -1000000000.0

BF = jnp.bfloat16
F32 = jnp.float32


def swap(values, axis):
    return lax.ppermute(values, axis, [(0, 1), (1, 0)])


def mp_swap(values, distance):
    count = lax.axis_size("mp")
    return lax.ppermute(values, "mp", [(i, i ^ distance) for i in range(count)])


def pick(values, place):
    return lax.dynamic_index_in_dim(values, place, 0, keepdims=False)


def mp_place(pieces):
    me = lax.axis_index("mp")
    total = jnp.zeros((len(pieces),) + pieces[0].shape, pieces[0].dtype)
    for distance, piece in enumerate(pieces):
        total = lax.dynamic_update_index_in_dim(total, piece, me ^ distance, 0)
    return total


def mp_gather(values):
    count = lax.axis_size("mp")
    return mp_place([values] + [mp_swap(values, j) for j in range(1, count)])


def grow(values, axis):
    other = swap(values, axis)
    first = lax.axis_index(axis) == 0
    return jnp.stack([jnp.where(first, values, other), jnp.where(first, other, values)])


def shrink(values, axis):
    me = lax.axis_index(axis)
    sent = pick(values, 1 - me).astype(BF)
    return pick(values, me).astype(F32) + swap(sent, axis).astype(F32)


def tree_gather(values, order):
    for axis in order + ("core",):
        values = grow(values, axis)
    return values


def tree_reduce(values, order):
    for axis in (order + ("core",))[::-1]:
        values = shrink(values, axis)
    return values


def mp_reduce(values):
    count = lax.axis_size("mp")
    me = lax.axis_index("mp")
    total = pick(values, me)
    for j in range(1, count):
        total = total + mp_swap(pick(values, me ^ j).astype(BF), j).astype(F32)
    return total


def axes_to_rows(order):
    bits = len(order)
    natural = [bits - order.index(f"b{k}") for k in range(bits)] + [0]
    return natural


def to_rows(values, order):
    bits = len(order)
    natural = axes_to_rows(order)
    moved = values.transpose(natural + [bits + 2, bits + 1, bits + 3])
    rows = math.prod(moved.shape[: bits + 2])
    return moved.reshape((rows,) + moved.shape[bits + 2 :])


def from_rows(values, order):
    bits = len(order)
    natural = axes_to_rows(order)
    rows = values.shape[0] // 2 ** (bits + 1)
    split = values.reshape((2,) * (bits + 1) + (rows,) + values.shape[1:])
    back = [0] * (bits + 1)
    for place, axis in enumerate(natural):
        back[axis] = place
    return split.transpose(back + [bits + 2, bits + 1, bits + 3])


def split_two(rows):
    width = rows.shape[2] // 2
    halves = rows.reshape(rows.shape[0], rows.shape[1], 2, width)
    return tuple(halves[:, :, i].reshape(rows.shape[0], rows.shape[1] * width) for i in range(2))


def join_two(first, second, count):
    parts = [v.reshape(v.shape[0], count, v.shape[1] // count) for v in (first, second)]
    return jnp.concatenate(parts, axis=2)


def norm_forward(values, gain, shift):
    center = values - jnp.mean(values, axis=-1, keepdims=True)
    spread = jnp.mean(center * center, axis=-1, keepdims=True)
    inverse = lax.rsqrt(spread + NORM_EPS)
    normed = center * inverse
    return (normed * gain + shift, normed, inverse)


def norm_backward(grad_out, normed, inverse, gain):
    scaled = grad_out * gain
    inner = (
        scaled
        - jnp.mean(scaled, axis=-1, keepdims=True)
        - normed * jnp.mean(scaled * normed, axis=-1, keepdims=True)
    )
    grad_gain = jnp.sum(grad_out * normed, axis=0)
    grad_shift = jnp.sum(grad_out, axis=0)
    return (inner * inverse, grad_gain, grad_shift)


def dot(a, b):
    return lax.dot_general(a, b, (((1,), (0,)), ((), ())), preferred_element_type=F32)


def dot_t(a, b):
    return lax.dot_general(a, b, (((1,), (1,)), ((), ())), preferred_element_type=F32)


def t_dot(a, b):
    return lax.dot_general(a, b, (((0,), (0,)), ((), ())), preferred_element_type=F32)


def scores_of(query_heads, key_heads, mask_add):
    raw = jnp.einsum("nqhc,nkhc->nhqk", query_heads, key_heads, preferred_element_type=F32)
    return raw * HEAD_DIM ** (-0.5) + mask_add


def attend_forward(query_heads, key_heads, value_heads, mask_add):
    scores = scores_of(query_heads, key_heads, mask_add)
    top = jnp.max(scores, axis=-1, keepdims=True)
    expo = jnp.exp(scores - top)
    total = jnp.sum(expo, axis=-1, keepdims=True)
    probs = expo / total
    context = jnp.einsum(
        "nhqk,nkhc->nqhc", probs.astype(BF), value_heads, preferred_element_type=F32
    )
    return (context.astype(BF), probs)


def attend_backward(query_heads, key_heads, value_heads, probs, grad_context):
    grad_probs = jnp.einsum(
        "nqhc,nkhc->nhqk", grad_context, value_heads, preferred_element_type=F32
    )
    grad_value = jnp.einsum(
        "nhqk,nqhc->nkhc", probs.astype(BF), grad_context, preferred_element_type=F32
    )
    grad_scores = probs * (grad_probs - jnp.sum(probs * grad_probs, axis=-1, keepdims=True))
    grad_scores = grad_scores.astype(BF)
    scale = HEAD_DIM ** (-0.5)
    grad_query = (
        jnp.einsum("nhqk,nkhc->nqhc", grad_scores, key_heads, preferred_element_type=F32) * scale
    )
    grad_key = (
        jnp.einsum("nhqk,nqhc->nkhc", grad_scores, query_heads, preferred_element_type=F32) * scale
    )
    return (grad_query.astype(BF), grad_key.astype(BF), grad_value.astype(BF))


def column_sum(values):
    return jnp.sum(values.astype(F32), axis=0)


def adam_update(weight, first, second, grad, rate):
    first_new = BETA_ONE * first + (1.0 - BETA_ONE) * grad
    second_new = BETA_TWO * second + (1.0 - BETA_TWO) * grad * grad
    first_hat = first_new / (1.0 - BETA_ONE**STEP_COUNT)
    second_hat = second_new / (1.0 - BETA_TWO**STEP_COUNT)
    weight_new = weight - rate * (
        first_hat / (jnp.sqrt(second_hat) + ADAM_EPS) + WEIGHT_DECAY * weight
    )
    return (first_new, second_new, weight_new)


def local(
    bits,
    hidden,
    images,
    caption_len,
    cotangent,
    attn_in,
    attn_in_first,
    attn_in_second,
    attn_out,
    attn_out_first,
    attn_out_second,
    cross_key_value_maps,
    cross_kv_first,
    cross_kv_second,
    ffn_up,
    ffn_up_first,
    ffn_up_second,
    ffn_down,
    ffn_down_first,
    ffn_down_second,
    vec_rep,
    vec_rep_first,
    vec_rep_second,
    query_value_bias_rows,
    vec_head_first,
    vec_head_second,
    bias_up,
    bias_up_first,
    bias_up_second,
):
    forth = tuple(f"b{k}" for k in range(bits))
    back = forth[::-1]
    every = forth + ("core", "mp")
    mp = lax.axis_size("mp")
    me = lax.axis_index("mp")
    group = me & 1
    pair = me - group
    items = hidden.shape[0] // mp
    row_count = hidden.shape[1]
    rows = items * NQ

    def side(values):
        return jnp.concatenate([values[0], values[1]], axis=1)

    low_in = attn_in.astype(BF)
    low_out = attn_out.astype(BF).transpose(0, 2, 1)
    low_kv = cross_key_value_maps.astype(BF)
    low_up = ffn_up.astype(BF)
    low_down = ffn_down.astype(BF).transpose(0, 2, 1)
    qk_all = mp_gather(side(low_in[:2]))
    vc_all = mp_gather(side(low_in[2:]))
    kv_all = mp_gather(side(low_kv))
    oo_all = mp_gather(side(low_out))

    def group_gather(values):
        mine, other = pick(values, group), pick(values, 1 - group)
        pieces = [mine] + [mp_swap(other if j % 2 else mine, j) for j in range(1, mp)]
        return mp_place(pieces)

    up_all = group_gather(low_up)
    down_all = group_gather(low_down)
    w_query, w_key = split_two(to_rows(tree_gather(qk_all, forth), forth))
    w_value, w_cross = split_two(to_rows(tree_gather(vc_all, back), back))
    w_ck, w_cv = split_two(to_rows(tree_gather(kv_all, forth), forth))
    w_out, w_cout = split_two(to_rows(tree_gather(oo_all, back), back))
    up_rows = to_rows(tree_gather(up_all, forth), forth)
    w_up = up_rows.reshape(up_rows.shape[0], -1)
    down_rows = to_rows(tree_gather(down_all, back), back)
    w_down = down_rows.reshape(down_rows.shape[0], -1)

    head_all = lax.all_gather(query_value_bias_rows, "mp", axis=1, tiled=True)
    bias_all = lax.all_gather(bias_up, "mp", axis=1, tiled=True)

    tokens = lax.dynamic_slice_in_dim(hidden, me * items, items, 0)
    image_rows = lax.dynamic_slice_in_dim(images, me * items, items, 0)
    lengths = lax.dynamic_slice_in_dim(caption_len, me * items, items, 0)
    image_flat = image_rows.reshape(items * image_rows.shape[1], image_rows.shape[2])
    tokens_flat = tokens.reshape(items * row_count, D)
    heads = D // HEAD_DIM

    def split_heads(values, length):
        return values.reshape(items, length, heads, HEAD_DIM)

    def merge(values):
        return values.reshape(-1, D)

    positions = jnp.arange(row_count)
    valid = (positions[None, :] < NQ) | (positions[None, :] - NQ < lengths[:, None])
    mask_add = jnp.where(valid, 0.0, MASKED).astype(F32)[:, None, None, :]
    query = split_heads((dot(tokens_flat, w_query) + head_all[0]).astype(BF), row_count)
    key = split_heads(dot(tokens_flat, w_key).astype(BF), row_count)
    value = split_heads((dot(tokens_flat, w_value) + head_all[1]).astype(BF), row_count)
    context, probs = attend_forward(query, key, value, mask_add)
    context_flat = merge(context)
    first_out, first_normed, first_inverse = norm_forward(
        tokens_flat.astype(F32) + dot_t(context_flat, w_out) + vec_rep[0], vec_rep[4], vec_rep[5]
    )
    first_items = first_out.reshape(items, 2, NQ, D)
    first_query = first_items[:, 0].reshape(rows, D)
    first_low = first_query.astype(BF)
    keys = image_rows.shape[1]
    cross_query = split_heads((dot(first_low, w_cross) + head_all[2]).astype(BF), NQ)
    cross_key = split_heads(dot(image_flat, w_ck).astype(BF), keys)
    cross_value = split_heads((dot(image_flat, w_cv) + head_all[3]).astype(BF), keys)
    cross_context, cross_probs = attend_forward(cross_query, cross_key, cross_value, F32(0.0))
    cross_flat = merge(cross_context)
    second_out, second_normed, second_inverse = norm_forward(
        first_query + dot_t(cross_flat, w_cout) + vec_rep[1], vec_rep[6], vec_rep[7]
    )

    caption_rows = first_items[:, 1].reshape(rows, D)
    is_low = group == 0
    kept = jnp.where(is_low, second_out, caption_rows)
    given = mp_swap(jnp.where(is_low, caption_rows, second_out).astype(BF), 1).astype(F32)
    ffn_rows = jnp.concatenate(
        [jnp.where(is_low, kept, given), jnp.where(is_low, given, kept)], axis=0
    )
    top = lax.dynamic_slice_in_dim(cotangent, pair * items, 2 * items, 0)
    top = top.reshape(2 * items, 2, NQ, D)
    top = lax.dynamic_index_in_dim(top, group, 1, keepdims=False)
    top = top.reshape(2 * rows, D).astype(F32)
    third_bias = pick(vec_rep[2:4], group)
    third_gain = jnp.where(is_low, vec_rep[8], vec_rep[10])
    third_shift = jnp.where(is_low, vec_rep[9], vec_rep[11])
    ffn_low = ffn_rows.astype(BF)
    up_pre = dot(ffn_low, w_up) + pick(bias_all, group)
    gelu_value, gelu_pull = jax.vjp(lambda v: jax.nn.gelu(v, approximate=False), up_pre)
    up_act = gelu_value.astype(BF)
    third_out, third_normed, third_inverse = norm_forward(
        ffn_rows + dot_t(up_act, w_down) + third_bias, third_gain, third_shift
    )
    out_all = mp_gather(third_out.astype(BF))
    layer_out = (
        out_all.reshape(mp // 2, 2, 2, items, NQ, D)
        .transpose(0, 2, 3, 1, 4, 5)
        .reshape(mp * items, row_count, D)
    )
    grad_third, gain_third, shift_third = norm_backward(
        top, third_normed, third_inverse, third_gain
    )
    grad_ffn = grad_third.astype(BF)
    third_bias_sum = column_sum(grad_ffn)
    grad_down = t_dot(grad_ffn, up_act)
    grad_act = dot(grad_ffn, w_down)
    grad_pre = gelu_pull(grad_act)[0].astype(BF)
    bias_sum = column_sum(grad_pre)
    grad_up = t_dot(ffn_low, grad_pre)
    grad_rows = grad_third + dot_t(grad_pre, w_up)
    mine = jnp.where(is_low, grad_rows[:rows], grad_rows[rows:])
    theirs = jnp.where(is_low, grad_rows[rows:], grad_rows[:rows])
    got = mp_swap(theirs.astype(BF), 1).astype(F32)
    grad_second = jnp.where(is_low, mine, got)
    grad_caption = jnp.where(is_low, got, mine)

    grad_cross, gain_second, shift_second = norm_backward(
        grad_second, second_normed, second_inverse, vec_rep[6]
    )
    grad_cross_low = grad_cross.astype(BF)
    second_bias_sum = column_sum(grad_cross_low)
    grad_cout = t_dot(grad_cross_low, cross_flat)
    cross_back = split_heads(dot(grad_cross_low, w_cout).astype(BF), NQ)
    cross_gq, cross_gk, cross_gv = attend_backward(
        cross_query, cross_key, cross_value, cross_probs, cross_back
    )
    cross_gq, cross_gk, cross_gv = merge(cross_gq), merge(cross_gk), merge(cross_gv)
    grad_wcross = t_dot(first_low, cross_gq)
    grad_ck = t_dot(image_flat, cross_gk)
    grad_cv = t_dot(image_flat, cross_gv)
    grad_first_query = grad_cross + dot_t(cross_gq, w_cross)

    grad_first = jnp.stack(
        [grad_first_query.reshape(items, NQ, D), grad_caption.reshape(items, NQ, D)], axis=1
    ).reshape(items * row_count, D)
    grad_self, gain_first, shift_first = norm_backward(
        grad_first, first_normed, first_inverse, vec_rep[4]
    )
    grad_self_low = grad_self.astype(BF)
    first_bias_sum = column_sum(grad_self_low)
    grad_out = t_dot(grad_self_low, context_flat)
    self_back = split_heads(dot(grad_self_low, w_out).astype(BF), row_count)
    self_gq, self_gk, self_gv = attend_backward(query, key, value, probs, self_back)
    self_gq, self_gk, self_gv = merge(self_gq), merge(self_gk), merge(self_gv)
    grad_query = t_dot(tokens_flat, self_gq)
    grad_key = t_dot(tokens_flat, self_gk)
    grad_value = t_dot(tokens_flat, self_gv)
    grad_tokens = (
        grad_self + dot_t(self_gq, w_query) + dot_t(self_gk, w_key) + dot_t(self_gv, w_value)
    )
    grad_hidden = (
        mp_gather(grad_tokens.astype(BF)).reshape(mp * items, row_count, D).astype(F32)
    )

    none = jnp.zeros_like(third_bias_sum)

    def of_group(values):
        return jnp.where(is_low, values, none), jnp.where(is_low, none, values)

    bias_low, bias_high = of_group(third_bias_sum)
    gain_low, gain_high = of_group(gain_third)
    shift_low, shift_high = of_group(shift_third)
    shared = jnp.stack(
        [
            first_bias_sum,
            second_bias_sum,
            bias_low,
            bias_high,
            gain_first,
            shift_first,
            gain_second,
            shift_second,
            gain_low,
            shift_low,
            gain_high,
            shift_high,
        ]
    )
    headwise = jnp.stack(
        [column_sum(self_gq), column_sum(self_gv), column_sum(cross_gq), column_sum(cross_gv)]
    )
    hidden_bias = jnp.stack(
        [
            jnp.where(is_low, bias_sum, jnp.zeros_like(bias_sum)),
            jnp.where(is_low, jnp.zeros_like(bias_sum), bias_sum),
        ]
    )
    reduced_rep, head_total, bias_total = lax.psum((shared, headwise, hidden_bias), every)
    head_width = query_value_bias_rows.shape[1]
    bias_width = bias_up.shape[1]
    reduced_head = lax.dynamic_slice_in_dim(head_total, me * head_width, head_width, 1)
    reduced_bias = lax.dynamic_slice_in_dim(bias_total, me * bias_width, bias_width, 1)

    def reduce_two(first, second, order):
        pieces = from_rows(join_two(first, second, mp), order)
        total = mp_reduce(tree_reduce(pieces, order))
        width = total.shape[1] // 2
        return jnp.stack([total[:, :width], total[:, width:]])

    def reduce_group(values, order):
        pieces = from_rows(values.reshape(values.shape[0], mp, -1), order)
        local_sum = tree_reduce(pieces, order)
        mine = pick(local_sum, me)
        other = jnp.zeros_like(mine)
        for j in range(1, mp):
            got = mp_swap(pick(local_sum, me ^ j).astype(BF), j).astype(F32)
            if j % 2:
                other = other + got
            else:
                mine = mine + got
        return jnp.stack([jnp.where(is_low, mine, other), jnp.where(is_low, other, mine)])

    reduced_down = reduce_group(grad_down, back).transpose(0, 2, 1)
    reduced_up = reduce_group(grad_up, forth)
    reduced_kv = reduce_two(grad_ck, grad_cv, forth)
    reduced_out = reduce_two(grad_out, grad_cout, back).transpose(0, 2, 1)
    reduced_in = jnp.concatenate(
        [reduce_two(grad_query, grad_key, forth), reduce_two(grad_value, grad_wcross, back)]
    )
    rates = (
        2.0 / math.sqrt(D),
        2.0 / math.sqrt(max(D // 8, 1)),
        2.0 / math.sqrt(E),
        2.0 / math.sqrt(D),
        2.0 / math.sqrt(F),
        0.3,
        0.3,
        0.3,
    )
    weights = (
        attn_in,
        attn_out,
        cross_key_value_maps,
        ffn_up,
        ffn_down,
        vec_rep,
        query_value_bias_rows,
        bias_up,
    )
    firsts = (
        attn_in_first,
        attn_out_first,
        cross_kv_first,
        ffn_up_first,
        ffn_down_first,
        vec_rep_first,
        vec_head_first,
        bias_up_first,
    )
    seconds = (
        attn_in_second,
        attn_out_second,
        cross_kv_second,
        ffn_up_second,
        ffn_down_second,
        vec_rep_second,
        vec_head_second,
        bias_up_second,
    )
    reduced = (
        reduced_in,
        reduced_out,
        reduced_kv,
        reduced_up,
        reduced_down,
        reduced_rep,
        reduced_head,
        reduced_bias,
    )
    results = []
    for weight, first, second, grad, rate in zip(weights, firsts, seconds, reduced, rates):
        results.extend(adam_update(weight, first, second, grad, rate))
    return (layer_out, grad_hidden, *results)


def solution(mesh):
    dp, mp = mesh.devices.shape
    bits = (dp // 2).bit_length() - 1
    names = tuple(f"b{k}" for k in range(bits)) + ("core",)
    fine = Mesh(mesh.devices.reshape((2,) * (bits + 1) + (mp,)), names + ("mp",))
    split = P(names)
    inward = P(None, names, "mp")
    outward = P(None, "mp", names)
    head = P(None, "mp")
    placed = (
        (split,) * 4
        + (inward,) * 3
        + (outward,) * 3
        + (inward,) * 6
        + (outward,) * 3
        + (P(),) * 3
        + (head,) * 6
    )
    out_placed = (
        (split,) * 2
        + (inward,) * 3
        + (outward,) * 3
        + (inward,) * 6
        + (outward,) * 3
        + (P(),) * 3
        + (head,) * 6
    )
    return jax.shard_map(
        lambda *arrays: local(bits, *arrays),
        mesh=fine,
        in_specs=placed,
        out_specs=out_placed,
        check_vma=False,
    )
```

```python
import functools
import math

import jax
import jax.numpy as jnp
from jax import lax
from jax.experimental import pallas as pl
from jax.experimental.pallas import tpu as pltpu
from jax.sharding import Mesh
from jax.sharding import PartitionSpec as P

D = 768
HEAD_DIM = 64
F = 3072
E = 1408
NQ = 32
STEP_COUNT = 10

NORM_EPS = 1e-06
BETA_ONE = 0.9
BETA_TWO = 0.999
ADAM_EPS = 1e-08
WEIGHT_DECAY = 0.01
MASKED = -1000000000.0

BF = jnp.bfloat16
F32 = jnp.float32
SCALE = HEAD_DIM ** (-0.5)
MIB = 1 << 20


def dot(a, b):
    return lax.dot_general(a, b, (((1,), (0,)), ((), ())), preferred_element_type=F32)


def dot_t(a, b):
    return lax.dot_general(a, b, (((1,), (1,)), ((), ())), preferred_element_type=F32)


def t_dot(a, b):
    return lax.dot_general(a, b, (((0,), (0,)), ((), ())), preferred_element_type=F32)


def swap(values, axis):
    return lax.ppermute(values, axis, [(0, 1), (1, 0)])


def mp_swap(values, distance):
    count = lax.axis_size("mp")
    return lax.ppermute(values, "mp", [(i, i ^ distance) for i in range(count)])


class Plan:
    def __init__(self, bits, mp, items, dp):
        self.bits = bits
        self.mp = mp
        self.dp = dp
        self.items = items
        self.rows = items * 2 * NQ
        self.half = items * NQ
        self.width = D // mp
        self.forth = tuple(f"b{k}" for k in range(bits))
        self.back = self.forth[::-1]

    def direct(self, rows):
        return rows % 16 == 0

    def bit(self, axis):
        return 1 if axis == "core" else 2 << (self.bits - 1 - int(axis[1:]))

    def masks(self, order):
        found = [0]
        for axis in order + ("core",):
            found = found + [m | self.bit(axis) for m in found]
        return found

    def dp_index(self):
        place = lax.axis_index("core")
        for axis in self.forth:
            place = place + self.bit(axis) * lax.axis_index(axis)
        return place


def mp_collect(own, sent):
    return [own] + [mp_swap(sent(j), j) for j in range(1, lax.axis_size("mp"))]


def tree_gather(plan, stacked, order):
    if plan.direct(stacked.shape[1]):
        pieces = [stacked]
        for axis in order + ("core",):
            pieces = pieces + [swap(p, axis) for p in pieces]
        return pieces
    near = jnp.arange(plan.mp) ^ lax.axis_index("mp")
    values = jnp.take(stacked, near, axis=0)[None]
    for axis in order + ("core",):
        values = jnp.concatenate([values, swap(values, axis)])
    back = [0] * plan.dp
    for k, mask in enumerate(plan.masks(order)):
        back[mask] = k
    natural = jnp.take(jnp.array(back), jnp.arange(plan.dp) ^ plan.dp_index())
    values = jnp.take(values, natural, axis=0).transpose(1, 0, 2, 3)
    return [values.reshape(plan.mp, -1, values.shape[-1])]


def tree_halves(plan, grads, rows, order):
    if plan.direct(rows):
        return grads
    (natural,) = grads
    blocks = natural.reshape(plan.mp, plan.dp, rows, natural.shape[-1])
    near = jnp.arange(plan.mp) ^ lax.axis_index("mp")
    places = jnp.array(plan.masks(order)) ^ plan.dp_index()
    blocks = jnp.take(jnp.take(blocks, near, axis=0), places, axis=1).transpose(1, 0, 2, 3)
    return blocks[: plan.dp // 2], blocks[plan.dp // 2 :]


def tree_reduce(halves, order):
    kept, sent = halves
    for axis in (order + ("core",))[::-1]:
        got = swap(sent, axis)
        half = got.shape[0] // 2
        if half == 0:
            return (kept.astype(F32) + got.astype(F32))[0]
        kept, sent = (
            (kept[:half].astype(F32) + got[:half].astype(F32)).astype(BF),
            (kept[half:].astype(F32) + got[half:].astype(F32)).astype(BF),
        )


def norm_parts(values):
    center = values - jnp.mean(values, axis=-1, keepdims=True)
    spread = jnp.mean(center * center, axis=-1, keepdims=True)
    inverse = lax.rsqrt(spread + NORM_EPS)
    return center * inverse, inverse


def norm_backward(grad_out, normed, inverse, gain):
    scaled = grad_out * gain
    inner = (
        scaled
        - jnp.mean(scaled, axis=-1, keepdims=True)
        - normed * jnp.mean(scaled * normed, axis=-1, keepdims=True)
    )
    return inner * inverse


def column_sum(values):
    return jnp.sum(values.astype(F32), axis=0, keepdims=True)


def halves_of(values, items):
    split = values.reshape(items, 2 * NQ, values.shape[-1])
    parts = split[:, :NQ], split[:, NQ:]
    return tuple(p.reshape(items * NQ, values.shape[-1]) for p in parts)


def join_halves(query, caption, items):
    width = query.shape[-1]
    parts = [v.reshape(items, NQ, width) for v in (query, caption)]
    return jnp.concatenate(parts, axis=1).reshape(items * 2 * NQ, width)


def wide(first, second):
    return jnp.concatenate([first, second], axis=1)


def after(values, width):
    return jnp.concatenate([jnp.zeros_like(values), values], axis=1)


def before(values, width):
    return jnp.concatenate([values, jnp.zeros_like(values)], axis=1)


def head_lanes(width):
    lane = lax.broadcasted_iota(jnp.int32, (1, width), 1)
    return [lane // HEAD_DIM == h for h in range(width // HEAD_DIM)]


def only(values, lanes):
    return jnp.where(lanes, values, jnp.zeros_like(values))


def softmax(scores):
    expo = jnp.exp(scores - jnp.max(scores, axis=-1, keepdims=True))
    return expo * (1.0 / jnp.sum(expo, axis=-1, keepdims=True))


def fetch(plan, pieces, order, target, sem):
    if len(pieces) == 1:
        pltpu.make_async_copy(pieces[0], target, sem).start()
        return
    rows = pieces[0].shape[1]
    me, place = lax.axis_index("mp"), plan.dp_index()
    for mask, piece in zip(plan.masks(order), pieces):
        begin = pl.multiple_of((place ^ mask) * rows, 16)
        for j in range(plan.mp):
            pltpu.make_async_copy(
                piece.at[j], target.at[me ^ j, pl.ds(begin, rows), :], sem
            ).start()


def settle(target, sem):
    pltpu.make_async_copy(target, target, sem).wait()


def spread(plan, source, outs, order, sem):
    if len(outs) == 1:
        pltpu.make_async_copy(source, outs[0], sem).start()
        return
    rows = outs[0].shape[2]
    me, place = lax.axis_index("mp"), plan.dp_index()
    half = plan.dp // 2
    for k, mask in enumerate(plan.masks(order)):
        begin = pl.multiple_of((place ^ mask) * rows, 16)
        for j in range(plan.mp):
            pltpu.make_async_copy(
                source.at[me ^ j, pl.ds(begin, rows), :], outs[k // half].at[k % half, j], sem
            ).start()


def gradient_shapes(plan, rows, total, width):
    if plan.direct(rows):
        return [jax.ShapeDtypeStruct((plan.dp // 2, plan.mp, rows, width), BF)] * 2
    return [jax.ShapeDtypeStruct((plan.mp, total, width), BF)]


def call(kernel, ins, places, outs, out_places, scratch, limit, flops, moved):
    return pl.pallas_call(
        kernel,
        out_shape=outs,
        in_specs=[pl.BlockSpec(memory_space=p) for p in places],
        out_specs=[pl.BlockSpec(memory_space=p) for p in out_places],
        scratch_shapes=scratch,
        compiler_params=pltpu.CompilerParams(vmem_limit_bytes=limit * MIB),
        cost_estimate=pl.CostEstimate(flops=flops, bytes_accessed=moved, transcendentals=0),
    )(*ins)


ANY, VMEM, SMEM = pl.ANY, pltpu.VMEM, pltpu.SMEM
DMA = pltpu.SemaphoreType.DMA


def self_mask(plan, lengths, me):
    count = plan.rows
    row = lax.broadcasted_iota(jnp.int32, (count, count), 0)
    col = lax.broadcasted_iota(jnp.int32, (count, count), 1)
    span = 2 * NQ
    limit = jnp.zeros((count, count), jnp.int32)
    for i in range(plan.items):
        limit = jnp.where(col // span == i, lengths[me * plan.items + i], limit)
    inside = col % span
    valid = (row // span == col // span) & ((inside < NQ) | (inside - NQ < limit))
    return jnp.where(valid, 0.0, MASKED).astype(F32)


def load_tokens(plan, hidden, target, sem):
    me = lax.axis_index("mp")
    return pltpu.make_async_copy(hidden.at[pl.ds(me * plan.items, plan.items)], target, sem)


def self_forward(plan, lengths, hidden, vec, heads, qk, vc, oo):
    counts = len(qk), len(vc), len(oo)
    mp, rows, half, width = plan.mp, plan.rows, plan.half, plan.width

    def kernel(lengths, hidden, vec, heads, *rest):
        qk = rest[: counts[0]]
        vc = rest[counts[0] : counts[0] + counts[1]]
        oo = rest[counts[0] + counts[1] : sum(counts)]
        qk_out, v_out, context_out, z_out, cross_out = rest[sum(counts) : sum(counts) + 5]
        tokens, w_qk, w_vc, w_oo, sems = rest[sum(counts) + 5 :]
        me = lax.axis_index("mp")
        loaded = load_tokens(plan, hidden, tokens, sems.at[0])
        loaded.start()
        fetch(plan, qk, plan.forth, w_qk, sems.at[1])
        fetch(plan, vc, plan.back, w_vc, sems.at[2])
        fetch(plan, oo, plan.back, w_oo, sems.at[3])
        mask = self_mask(plan, lengths, me)
        lanes = head_lanes(width)
        loaded.wait()
        x = tokens[...].reshape(rows, D)
        settle(w_qk, sems.at[1])
        settle(w_vc, sems.at[2])
        settle(w_oo, sems.at[3])
        total = x.astype(F32) + vec[0:1, :]
        for z in range(mp):
            both = (dot(x, w_qk[z]) + heads[me ^ z, 0:1, :]).astype(BF)
            qk_out[z] = both
            q, k = both[:, :width], both[:, width:]
            v = (dot(x, w_vc[z]) + heads[me ^ z, 1:2, :]).astype(BF)[:, :width]
            v_out[z] = v
            context = jnp.zeros((rows, width), F32)
            for lane in lanes:
                probs = softmax(dot_t(only(q, lane), k) * SCALE + mask)
                context = context + only(dot(probs.astype(BF), v), lane)
            context = context.astype(BF)
            context_out[z] = context
            total = total + dot_t(before(context, width), w_oo[z])
        z_out[...] = total
        normed, _ = norm_parts(total)
        first = normed * vec[4:5, :] + vec[5:6, :]
        u = halves_of(first, plan.items)[0].astype(BF)
        for z in range(mp):
            cross = (dot(u, w_vc[z]) + heads[me ^ z, 1:2, :]).astype(BF)
            cross_out[z] = cross[:, width:]

    outs = [
        jax.ShapeDtypeStruct((mp, rows, 2 * width), BF),
        jax.ShapeDtypeStruct((mp, rows, width), BF),
        jax.ShapeDtypeStruct((mp, rows, width), BF),
        jax.ShapeDtypeStruct((rows, D), F32),
        jax.ShapeDtypeStruct((mp, half, width), BF),
    ]
    return call(
        kernel,
        (lengths, hidden, vec, heads, *qk, *vc, *oo),
        [SMEM, ANY, VMEM, VMEM] + [ANY] * sum(counts),
        outs,
        [VMEM] * 5,
        [
            pltpu.VMEM((plan.items, 2 * NQ, D), BF),
            pltpu.VMEM((mp, D, 2 * width), BF),
            pltpu.VMEM((mp, D, 2 * width), BF),
            pltpu.VMEM((mp, D, 2 * width), BF),
            DMA((4,)),
        ],
        32,
        3 * 10**9,
        9 * 10**6,
    )


def image_maps(plan, images, heads, kv):
    count = len(kv)
    mp, items, width = plan.mp, plan.items, plan.width
    keys = images.shape[1]
    padded = -(-keys // 128) * 128

    def kernel(images, heads, *rest):
        kv = rest[:count]
        out = rest[count]
        held, w_kv, sems = rest[count + 1 :]
        me = lax.axis_index("mp")
        loaded = load_tokens(plan, images, held, sems.at[0])
        loaded.start()
        fetch(plan, kv, plan.forth, w_kv, sems.at[1])
        loaded.wait()
        settle(w_kv, sems.at[1])
        for i in range(items):
            for z in range(mp):
                both = (dot(held[i], w_kv[z]) + heads[me ^ z, 2:3, :]).astype(BF)
                out[i, z, 0:keys, :] = both
                out[i, z, keys:padded, :] = jnp.zeros((padded - keys, 2 * width), BF)

    return call(
        kernel,
        (images, heads, *kv),
        [ANY, VMEM] + [ANY] * count,
        [jax.ShapeDtypeStruct((items, mp, padded, 2 * width), BF)],
        [VMEM],
        [
            pltpu.VMEM((items, keys, images.shape[2]), BF),
            pltpu.VMEM((mp, images.shape[2], 2 * width), BF),
            DMA((2,)),
        ],
        32,
        5 * 10**9,
        12 * 10**6,
    )[0]


def key_mask(plan, keys, padded):
    lane = lax.broadcasted_iota(jnp.int32, (1, padded), 1)
    return jnp.where(lane < keys, 0.0, MASKED).astype(F32)


def spread_heads(values, lanes):
    return jnp.concatenate([only(values, lane) for lane in lanes], axis=0)


def gather_heads(values, lanes):
    total = None
    for h, lane in enumerate(lanes):
        part = only(values[h * NQ : (h + 1) * NQ], lane)
        total = part if total is None else total + part
    return total


def cross_forward(plan, keys, vec, z_first, cross, kv, oo):
    count = len(oo)
    mp, rows, half, width, items = plan.mp, plan.rows, plan.half, plan.width, plan.items
    padded = kv.shape[2]

    def kernel(vec, z_first, cross, kv, *rest):
        oo = rest[:count]
        context_out, z_out, kept, given = rest[count : count + 4]
        w_oo, sems = rest[count + 4 :]
        group = lax.axis_index("mp") & 1
        fetch(plan, oo, plan.back, w_oo, sems.at[0])
        lanes = head_lanes(width)
        mask = key_mask(plan, keys, padded)
        normed, _ = norm_parts(z_first[...])
        u, caption = halves_of(normed * vec[4:5, :] + vec[5:6, :], items)
        for z in range(mp):
            for i in range(items):
                span = slice(i * NQ, (i + 1) * NQ)
                q = spread_heads(cross[z, span, :], lanes)
                both = kv[i, z]
                probs = softmax(dot_t(q, both[:, :width]) * SCALE + mask)
                context = gather_heads(dot(probs.astype(BF), both[:, width:]), lanes)
                context_out[z, span, :] = context.astype(BF)
        settle(w_oo, sems.at[0])
        total = u + vec[1:2, :]
        for z in range(mp):
            total = total + dot_t(after(context_out[z], width), w_oo[z])
        z_out[...] = total
        normed, _ = norm_parts(total)
        second = normed * vec[6:7, :] + vec[7:8, :]
        low = group == 0
        kept[...] = jnp.where(low, second, caption)
        given[...] = jnp.where(low, caption, second).astype(BF)

    outs = [
        jax.ShapeDtypeStruct((mp, half, width), BF),
        jax.ShapeDtypeStruct((half, D), F32),
        jax.ShapeDtypeStruct((half, D), F32),
        jax.ShapeDtypeStruct((half, D), BF),
    ]
    return call(
        kernel,
        (vec, z_first, cross, kv, *oo),
        [VMEM] * 4 + [ANY] * count,
        outs,
        [VMEM] * 4,
        [pltpu.VMEM((mp, D, 2 * width), BF), DMA((1,))],
        32,
        2 * 10**9,
        8 * 10**6,
    )


def feed_forward(plan, vec, heads, kept, got, cotangent, up, down, shard_rows):
    counts = len(up), len(down)
    mp, half, items = plan.mp, plan.half, plan.items
    hidden_width = F // mp
    shapes = gradient_shapes(plan, shard_rows, D, hidden_width)
    grads = len(shapes)

    def kernel(vec, heads, kept, got, cotangent, *rest):
        up, down = rest[: counts[0]], rest[counts[0] : sum(counts)]
        rest = rest[sum(counts) :]
        layer, kept_back, given_back, sums, bias_sums = rest[:5]
        up_out, down_out = rest[5 : 5 + grads], rest[5 + grads : 5 + 2 * grads]
        (top, w_up, w_down, act, up_grad, down_grad, sems) = rest[5 + 2 * grads :]
        me = lax.axis_index("mp")
        group = me & 1
        fetch(plan, up, plan.forth, w_up, sems.at[0])
        fetch(plan, down, plan.back, w_down, sems.at[1])
        tops = []
        for s in range(2):
            first = (me ^ s) * items
            tops.append(
                pltpu.make_async_copy(
                    cotangent.at[
                        pl.ds(first, items), pl.ds(pl.multiple_of(group * NQ, NQ), NQ), :
                    ],
                    top.at[s],
                    sems.at[2 + s],
                )
            )
            tops[-1].start()
        x = jnp.concatenate([kept[...], got[...].astype(F32)], axis=0)
        low = x.astype(BF)
        settle(w_up, sems.at[0])
        settle(w_down, sems.at[1])
        total = x + vec[pl.ds(2 + group, 1), :]
        for z in range(mp):
            bias = wide(
                heads[me ^ z, pl.ds(3 + 2 * group, 1), :], heads[me ^ z, pl.ds(4 + 2 * group, 1), :]
            )
            pre = dot(low, w_up[z]) + bias
            act[z] = pre
            value = 0.5 * pre * (1.0 + lax.erf(pre * (0.5**0.5)))
            total = total + dot_t(value.astype(BF), w_down[z])
        normed, inverse = norm_parts(total)
        gain = vec[pl.ds(8 + 2 * group, 1), :]
        third = normed * gain + vec[pl.ds(9 + 2 * group, 1), :]
        layer[...] = third.astype(BF).reshape(2, items, NQ, D)
        for t in tops:
            t.wait()
        grad = top[...].reshape(2 * half, D).astype(F32)
        back = norm_backward(grad, normed, inverse, gain)
        branch = back.astype(BF)
        sums[0:1, :] = column_sum(branch)
        sums[1:2, :] = column_sum(grad * normed)
        sums[2:3, :] = column_sum(grad)
        low_t = low.T
        branch_t = branch.T
        for z in range(mp):
            pre = act[z]
            cdf = 0.5 * (1.0 + lax.erf(pre * (0.5**0.5)))
            value = (pre * cdf).astype(BF)
            slope = cdf + pre * jnp.exp(-0.5 * pre * pre) * (1.0 / math.sqrt(2.0 * math.pi))
            pull = (dot(branch, w_down[z]) * slope).astype(BF)
            bias_sums[pl.ds(z, 1), :] = column_sum(pull)
            down_grad[z] = dot(branch_t, value).astype(BF)
            up_grad[z] = dot(low_t, pull).astype(BF)
            back = back + dot_t(pull, w_up[z])
        spread(plan, down_grad, down_out, plan.back, sems.at[4])
        spread(plan, up_grad, up_out, plan.forth, sems.at[5])
        kept_back[...] = back[:half]
        given_back[...] = back[half:].astype(BF)
        settle(down_grad, sems.at[4])
        settle(up_grad, sems.at[5])

    outs = [
        jax.ShapeDtypeStruct((2, items, NQ, D), BF),
        jax.ShapeDtypeStruct((half, D), F32),
        jax.ShapeDtypeStruct((half, D), BF),
        jax.ShapeDtypeStruct((3, D), F32),
        jax.ShapeDtypeStruct((mp, hidden_width), F32),
        *shapes,
        *shapes,
    ]
    found = call(
        kernel,
        (vec, heads, kept, got, cotangent, *up, *down),
        [VMEM] * 4 + [ANY] * (1 + sum(counts)),
        outs,
        [VMEM] * 5 + [ANY] * (2 * grads),
        [
            pltpu.VMEM((2, items, NQ, D), BF),
            pltpu.VMEM((mp, D, hidden_width), BF),
            pltpu.VMEM((mp, D, hidden_width), BF),
            pltpu.VMEM((mp, 2 * half, hidden_width), F32),
            pltpu.VMEM((mp, D, hidden_width), BF),
            pltpu.VMEM((mp, D, hidden_width), BF),
            DMA((6,)),
        ],
        48,
        8 * 10**9,
        20 * 10**6,
    )
    return (*found[:5], found[5 : 5 + grads], found[5 + grads :])


def cross_backward(plan, keys, vec, z_first, z_second, kept, got, cross, kv, vc, oo):
    counts = len(vc), len(oo)
    mp, rows, half, width, items = plan.mp, plan.rows, plan.half, plan.width, plan.items
    padded = kv.shape[2]

    def kernel(vec, z_first, z_second, kept, got, cross, kv, *rest):
        vc, oo = rest[: counts[0]], rest[counts[0] : sum(counts)]
        kv_back, query_back, branch_out, first_back, sums = rest[sum(counts) : sum(counts) + 5]
        w_vc, w_oo, sems = rest[sum(counts) + 5 :]
        low = (lax.axis_index("mp") & 1) == 0
        fetch(plan, oo, plan.back, w_oo, sems.at[0])
        fetch(plan, vc, plan.back, w_vc, sems.at[1])
        lanes = head_lanes(width)
        mask = key_mask(plan, keys, padded)
        other = got[...].astype(F32)
        grad = jnp.where(low, kept[...], other)
        caption = jnp.where(low, other, kept[...])
        normed, inverse = norm_parts(z_second[...])
        back = norm_backward(grad, normed, inverse, vec[6:7, :])
        branch = back.astype(BF)
        branch_out[...] = branch
        sums[0:1, :] = column_sum(branch)
        sums[1:2, :] = column_sum(grad * normed)
        sums[2:3, :] = column_sum(grad)
        settle(w_oo, sems.at[0])
        settle(w_vc, sems.at[1])
        for z in range(mp):
            context_back = dot(branch, w_oo[z]).astype(BF)[:, width:]
            value_sum = jnp.zeros((1, width), F32)
            for i in range(items):
                span = slice(i * NQ, (i + 1) * NQ)
                q = spread_heads(cross[z, span, :], lanes)
                g = spread_heads(context_back[span], lanes)
                both = kv[i, z]
                k, v = both[:, :width], both[:, width:]
                probs = softmax(dot_t(q, k) * SCALE + mask)
                pulled = dot_t(g, v)
                scored = probs * (pulled - jnp.sum(probs * pulled, axis=-1, keepdims=True))
                scored = scored.astype(BF)
                value_back = t_dot(probs.astype(BF), g).astype(BF)
                key_back = (t_dot(scored, q) * SCALE).astype(BF)
                kv_back[i, z] = wide(key_back, value_back)
                value_sum = value_sum + column_sum(value_back)
                query_back[z, span, :] = (gather_heads(dot(scored, k), lanes) * SCALE).astype(BF)
            sums[6:7, z * width : (z + 1) * width] = column_sum(query_back[z])
            sums[7:8, z * width : (z + 1) * width] = value_sum
            back = back + dot_t(after(query_back[z], width), w_vc[z])
        first_grad = join_halves(back, caption, items)
        normed, inverse = norm_parts(z_first[...])
        first = norm_backward(first_grad, normed, inverse, vec[4:5, :])
        first_back[...] = first
        sums[3:4, :] = column_sum(first_grad * normed)
        sums[4:5, :] = column_sum(first_grad)
        sums[5:6, :] = column_sum(first.astype(BF))

    outs = [
        jax.ShapeDtypeStruct((items, mp, padded, 2 * width), BF),
        jax.ShapeDtypeStruct((mp, half, width), BF),
        jax.ShapeDtypeStruct((half, D), BF),
        jax.ShapeDtypeStruct((rows, D), F32),
        jax.ShapeDtypeStruct((8, D), F32),
    ]
    return call(
        kernel,
        (vec, z_first, z_second, kept, got, cross, kv, *vc, *oo),
        [VMEM] * 7 + [ANY] * sum(counts),
        outs,
        [VMEM] * 5,
        [
            pltpu.VMEM((mp, D, 2 * width), BF),
            pltpu.VMEM((mp, D, 2 * width), BF),
            DMA((2,)),
        ],
        40,
        4 * 10**9,
        16 * 10**6,
    )


def image_gradient(plan, images, kv_back, shard_rows):
    mp, items, width = plan.mp, plan.items, plan.width
    keys, features = images.shape[1:]
    shapes = gradient_shapes(plan, shard_rows, features, 2 * width)
    even = keys // 128 * 128

    def kernel(images, kv_back, *rest):
        outs = rest[: len(shapes)]
        held, turned, grad, sems = rest[len(shapes) :]
        loaded = load_tokens(plan, images, held, sems.at[0])
        loaded.start()
        loaded.wait()
        for i in range(items):
            turned[:, i * even : (i + 1) * even] = held[i, 0:even, :].T
        for z in range(mp):
            total = jnp.zeros((features, 2 * width), F32)
            for i in range(items):
                total = total + dot(
                    turned[:, i * even : (i + 1) * even], kv_back[i, z, 0:even, :]
                )
            for i in range(items):
                if keys > even:
                    total = total + t_dot(held[i, even:keys, :], kv_back[i, z, even:keys, :])
            grad[z] = total.astype(BF)
        spread(plan, grad, outs, plan.forth, sems.at[1])
        settle(grad, sems.at[1])

    return call(
        kernel,
        (images, kv_back),
        [ANY, VMEM],
        shapes,
        [ANY] * len(shapes),
        [
            pltpu.VMEM((items, keys, features), BF),
            pltpu.VMEM((features, items * even), BF),
            pltpu.VMEM((mp, features, 2 * width), BF),
            DMA((2,)),
        ],
        48,
        5 * 10**9,
        12 * 10**6,
    )


def self_backward(plan, lengths, hidden, vec, z_first, first_back, branch, cross_context, query_back, qk_all, v_all, context_all, qk, vc, oo, shard_rows):
    counts = len(qk), len(vc), len(oo)
    mp, rows, half, width, items = plan.mp, plan.rows, plan.half, plan.width, plan.items
    shapes = gradient_shapes(plan, shard_rows, D, 2 * width)
    grads = len(shapes)

    def kernel(lengths, hidden, vec, z_first, first_back, branch, cross_context, query_back, qk_all, v_all, context_all, *rest):
        qk = rest[: counts[0]]
        vc = rest[counts[0] : counts[0] + counts[1]]
        oo = rest[counts[0] + counts[1] : sum(counts)]
        rest = rest[sum(counts) :]
        token_back, sums = rest[:2]
        qk_out = rest[2 : 2 + grads]
        vc_out = rest[2 + grads : 2 + 2 * grads]
        oo_out = rest[2 + 2 * grads : 2 + 3 * grads]
        tokens, w_qk, w_vc, w_oo, g_qk, g_vc, g_oo, sems = rest[2 + 3 * grads :]
        me = lax.axis_index("mp")
        loaded = load_tokens(plan, hidden, tokens, sems.at[0])
        loaded.start()
        fetch(plan, oo, plan.back, w_oo, sems.at[3])
        fetch(plan, qk, plan.forth, w_qk, sems.at[1])
        fetch(plan, vc, plan.back, w_vc, sems.at[2])
        mask = self_mask(plan, lengths, me)
        lanes = head_lanes(width)
        total = first_back[...]
        self_branch = total.astype(BF)
        branches_t = jnp.concatenate([self_branch, branch[...]], axis=0).T
        normed, _ = norm_parts(z_first[...])
        u = halves_of(normed * vec[4:5, :] + vec[5:6, :], items)[0].astype(BF)
        loaded.wait()
        inputs_t = jnp.concatenate([tokens[...].reshape(rows, D), u], axis=0).T
        settle(w_oo, sems.at[3])
        settle(w_qk, sems.at[1])
        settle(w_vc, sems.at[2])
        for z in range(mp):
            contexts = jnp.concatenate(
                [before(context_all[z], width), after(cross_context[z], width)], axis=0
            )
            g_oo[z] = dot(branches_t, contexts).astype(BF)
            pulled = dot(self_branch, w_oo[z]).astype(BF)[:, :width]
            q, k, v = qk_all[z][:, :width], qk_all[z][:, width:], v_all[z]
            query_grad = jnp.zeros((rows, width), F32)
            key_grad = jnp.zeros((rows, width), F32)
            value_grad = jnp.zeros((rows, width), F32)
            for lane in lanes:
                q_h, g_h = only(q, lane), only(pulled, lane)
                probs = softmax(dot_t(q_h, k) * SCALE + mask)
                wanted = dot_t(g_h, v)
                scored = probs * (wanted - jnp.sum(probs * wanted, axis=-1, keepdims=True))
                scored = scored.astype(BF)
                value_grad = value_grad + t_dot(probs.astype(BF), g_h)
                query_grad = query_grad + only(dot(scored, k), lane)
                key_grad = key_grad + t_dot(scored, q_h)
            query_grad = (query_grad * SCALE).astype(BF)
            value_grad = value_grad.astype(BF)
            sums[0:1, z * width : (z + 1) * width] = column_sum(query_grad)
            sums[1:2, z * width : (z + 1) * width] = column_sum(value_grad)
            both = wide(query_grad, (key_grad * SCALE).astype(BF))
            value_wide = before(value_grad, width)
            total = total + dot_t(both, w_qk[z]) + dot_t(value_wide, w_vc[z])
            g_qk[z] = dot(inputs_t[:, :rows], both).astype(BF)
            maps = jnp.concatenate([value_wide, after(query_back[z], width)], axis=0)
            g_vc[z] = dot(inputs_t, maps).astype(BF)
        token_back[...] = total.astype(BF)
        spread(plan, g_oo, oo_out, plan.back, sems.at[4])
        spread(plan, g_qk, qk_out, plan.forth, sems.at[5])
        spread(plan, g_vc, vc_out, plan.back, sems.at[6])
        settle(g_oo, sems.at[4])
        settle(g_qk, sems.at[5])
        settle(g_vc, sems.at[6])

    outs = [
        jax.ShapeDtypeStruct((rows, D), BF),
        jax.ShapeDtypeStruct((2, D), F32),
        *shapes,
        *shapes,
        *shapes,
    ]
    found = call(
        kernel,
        (lengths, hidden, vec, z_first, first_back, branch, cross_context, query_back, qk_all, v_all, context_all, *qk, *vc, *oo),
        [SMEM, ANY] + [VMEM] * 9 + [ANY] * sum(counts),
        outs,
        [VMEM] * 2 + [ANY] * (3 * grads),
        [pltpu.VMEM((items, 2 * NQ, D), BF)]
        + [pltpu.VMEM((mp, D, 2 * width), BF)] * 6
        + [DMA((7,))],
        48,
        6 * 10**9,
        24 * 10**6,
    )
    return (
        found[0],
        found[1],
        found[2 : 2 + grads],
        found[2 + grads : 2 + 2 * grads],
        found[2 + 2 * grads :],
    )


def place_layer(plan, pieces):
    mp, items = plan.mp, plan.items

    def kernel(*refs):
        out, sems = refs[mp], refs[mp + 1]
        me = lax.axis_index("mp")
        copies = []
        for j in range(mp):
            source = me ^ j
            group = source & 1
            for s in range(2):
                copies.append(
                    pltpu.make_async_copy(
                        refs[j].at[s],
                        out.at[
                            pl.ds((source ^ s) * items, items),
                            pl.ds(pl.multiple_of(group * NQ, NQ), NQ),
                            :,
                        ],
                        sems.at[2 * j + s],
                    )
                )
                copies[-1].start()
        for c in copies:
            c.wait()

    return call(
        kernel,
        pieces,
        [VMEM] * mp,
        [jax.ShapeDtypeStruct((mp * items, 2 * NQ, D), BF)],
        [ANY],
        [DMA((2 * mp,))],
        16,
        0,
        4 * 10**6,
    )[0]


def place_gradient(plan, pieces):
    mp, items = plan.mp, plan.items

    def kernel(*refs):
        out = refs[mp]
        me = lax.axis_index("mp")
        for j in range(mp):
            values = refs[j][...].astype(F32).reshape(items, 2 * NQ, D)
            out[pl.ds((me ^ j) * items, items)] = values

    return call(
        kernel,
        pieces,
        [VMEM] * mp,
        [jax.ShapeDtypeStruct((mp * items, 2 * NQ, D), F32)],
        [VMEM],
        [],
        24,
        0,
        6 * 10**6,
    )[0]


def adam_update(weight, first, second, grad, rate):
    first_new = BETA_ONE * first + (1.0 - BETA_ONE) * grad
    second_new = BETA_TWO * second + (1.0 - BETA_TWO) * grad * grad
    first_hat = first_new / (1.0 - BETA_ONE**STEP_COUNT)
    second_hat = second_new / (1.0 - BETA_TWO**STEP_COUNT)
    weight_new = weight - rate * (
        first_hat / (jnp.sqrt(second_hat) + ADAM_EPS) + WEIGHT_DECAY * weight
    )
    return (first_new, second_new, weight_new)


def local(
    bits,
    hidden,
    images,
    caption_len,
    cotangent,
    attn_in,
    attn_in_first,
    attn_in_second,
    attn_out,
    attn_out_first,
    attn_out_second,
    cross_key_value_maps,
    cross_kv_first,
    cross_kv_second,
    ffn_up,
    ffn_up_first,
    ffn_up_second,
    ffn_down,
    ffn_down_first,
    ffn_down_second,
    vec_rep,
    vec_rep_first,
    vec_rep_second,
    query_value_bias_rows,
    vec_head_first,
    vec_head_second,
    bias_up,
    bias_up_first,
    bias_up_second,
):
    mp = lax.axis_size("mp")
    me = lax.axis_index("mp")
    plan = Plan(bits, mp, hidden.shape[0] // mp, 2 ** (bits + 1))
    forth, back = plan.forth, plan.back
    group = me & 1
    low = group == 0
    keys = images.shape[1]

    def side(values):
        return jnp.concatenate([values[0], values[1]], axis=1)

    none = jnp.zeros_like(query_value_bias_rows[0])
    bias_rows = query_value_bias_rows
    packed = jnp.concatenate(
        [
            jnp.concatenate([bias_rows[0], none])[None],
            jnp.concatenate([bias_rows[1], bias_rows[2]])[None],
            jnp.concatenate([none, bias_rows[3]])[None],
            bias_up.reshape(-1, 2 * plan.width),
            jnp.zeros((1, 2 * plan.width), F32),
        ]
    )
    heads = jnp.stack(mp_collect(packed, lambda j: packed))

    low_in = attn_in.astype(BF)
    first_shard = jnp.stack([side(low_in[:2]), side(low_in[2:])])
    first_set = mp_collect(first_shard, lambda j: first_shard)
    qk = tree_gather(plan, jnp.stack([p[0] for p in first_set]), forth)
    vc = tree_gather(plan, jnp.stack([p[1] for p in first_set]), back)

    kv_rows = cross_key_value_maps.shape[1]
    second_shard = jnp.concatenate(
        [
            side(cross_key_value_maps.astype(BF)),
            side(attn_out.astype(BF).transpose(0, 2, 1)),
        ]
    )
    second_set = mp_collect(second_shard, lambda j: second_shard)
    oo = tree_gather(plan, jnp.stack([p[kv_rows:] for p in second_set]), back)
    kv = tree_gather(plan, jnp.stack([p[:kv_rows] for p in second_set]), forth)

    third_shard = jnp.stack(
        [ffn_up.astype(BF), ffn_down.astype(BF).transpose(0, 2, 1)], axis=1
    )
    own = lax.dynamic_index_in_dim(third_shard, group, 0, keepdims=False)
    other = lax.dynamic_index_in_dim(third_shard, 1 - group, 0, keepdims=False)
    third_set = mp_collect(own, lambda j: other if j % 2 else own)
    up = tree_gather(plan, jnp.stack([p[0] for p in third_set]), forth)
    down = tree_gather(plan, jnp.stack([p[1] for p in third_set]), back)

    qk_all, v_all, context_all, z_first, cross = self_forward(
        plan, caption_len, hidden, vec_rep, heads, qk, vc, oo
    )
    kv_all = image_maps(plan, images, heads, kv)
    cross_context, z_second, kept, given = cross_forward(
        plan, keys, vec_rep, z_first, cross, kv_all, oo
    )
    got = mp_swap(given, 1)
    layer, kept_back, given_back, third_sums, bias_sums, up_grad, down_grad = feed_forward(
        plan, vec_rep, heads, kept, got, cotangent, up, down, ffn_up.shape[1]
    )
    got_back = mp_swap(given_back, 1)
    layer_out = place_layer(plan, mp_collect(layer, lambda j: layer))
    kv_back, query_back, branch, first_back, cross_sums = cross_backward(
        plan, keys, vec_rep, z_first, z_second, kept_back, got_back, cross, kv_all, vc, oo
    )
    kv_grad = image_gradient(plan, images, kv_back, kv_rows)
    token_back, self_sums, qk_grad, vc_grad, oo_grad = self_backward(
        plan,
        caption_len,
        hidden,
        vec_rep,
        z_first,
        first_back,
        branch,
        cross_context,
        query_back,
        qk_all,
        v_all,
        context_all,
        qk,
        vc,
        oo,
        attn_in.shape[1],
    )
    grad_hidden = place_gradient(plan, mp_collect(token_back, lambda j: token_back))

    zero = jnp.zeros_like(third_sums)
    sums_low, sums_high = jnp.where(low, third_sums, zero), jnp.where(low, zero, third_sums)
    bias_flat = bias_sums.reshape(-1, D)
    bias_zero = jnp.zeros_like(bias_flat)
    vectors = jnp.concatenate(
        [
            cross_sums[5:6],
            cross_sums[0:1],
            sums_low[0:1],
            sums_high[0:1],
            cross_sums[3:5],
            cross_sums[1:3],
            sums_low[1:3],
            sums_high[1:3],
            self_sums,
            cross_sums[6:8],
            jnp.where(low, bias_flat, bias_zero),
            jnp.where(low, bias_zero, bias_flat),
        ]
    )
    for axis in ("core",) + forth:
        vectors = vectors + swap(vectors, axis)
    distance = 1
    while distance < mp:
        vectors = vectors + mp_swap(vectors, distance)
        distance *= 2
    reduced_rep = vectors[:12]
    head_width = query_value_bias_rows.shape[1]
    bias_width = bias_up.shape[1]
    reduced_head = lax.dynamic_slice_in_dim(vectors[12:16], me * head_width, head_width, 1)
    reduced_bias = lax.dynamic_slice_in_dim(
        vectors[16:].reshape(2, -1), me * bias_width, bias_width, 1
    )

    def finish(trees):
        totals = [
            tree_reduce(tree_halves(plan, grads, rows, order), order)
            for grads, rows, order in trees
        ]
        return mp_collect(
            [t[0] for t in totals],
            lambda j: jnp.concatenate([t[j].astype(BF) for t in totals]),
        )

    def split_columns(values):
        width = values.shape[1] // 2
        return jnp.stack([values[:, :width], values[:, width:]])

    def add_all(pieces, rows):
        own, rest = pieces[0], pieces[1:]
        bounds = [0]
        for r in rows:
            bounds.append(bounds[-1] + r)
        return [
            own[k] + sum(p[bounds[k] : bounds[k + 1]].astype(F32) for p in rest)
            for k in range(len(rows))
        ]

    ffn_rows = ffn_up.shape[1]
    attn_rows = attn_in.shape[1]
    third = finish([(up_grad, ffn_rows, forth), (down_grad, ffn_rows, back)])
    mine = [third[0][k] for k in range(2)]
    theirs = [jnp.zeros_like(m) for m in mine]
    for j in range(1, mp):
        for k in range(2):
            part = third[j][k * ffn_rows : (k + 1) * ffn_rows].astype(F32)
            if j % 2:
                theirs[k] = theirs[k] + part
            else:
                mine[k] = mine[k] + part
    reduced_up, reduced_down = (
        jnp.stack([jnp.where(low, m, t), jnp.where(low, t, m)]) for m, t in zip(mine, theirs)
    )
    reduced_down = reduced_down.transpose(0, 2, 1)
    kv_total = add_all(finish([(kv_grad, kv_rows, forth)]), [kv_rows])[0]
    reduced_kv = split_columns(kv_total)
    oo_total, qk_total, vc_total = add_all(
        finish(
            [
                (oo_grad, attn_rows, back),
                (qk_grad, attn_rows, forth),
                (vc_grad, attn_rows, back),
            ]
        ),
        [attn_rows] * 3,
    )
    reduced_out = split_columns(oo_total).transpose(0, 2, 1)
    reduced_in = jnp.concatenate([split_columns(qk_total), split_columns(vc_total)])
    rates = (
        2.0 / math.sqrt(D),
        2.0 / math.sqrt(max(D // 8, 1)),
        2.0 / math.sqrt(E),
        2.0 / math.sqrt(D),
        2.0 / math.sqrt(F),
        0.3,
        0.3,
        0.3,
    )
    weights = (
        attn_in,
        attn_out,
        cross_key_value_maps,
        ffn_up,
        ffn_down,
        vec_rep,
        query_value_bias_rows,
        bias_up,
    )
    firsts = (
        attn_in_first,
        attn_out_first,
        cross_kv_first,
        ffn_up_first,
        ffn_down_first,
        vec_rep_first,
        vec_head_first,
        bias_up_first,
    )
    seconds = (
        attn_in_second,
        attn_out_second,
        cross_kv_second,
        ffn_up_second,
        ffn_down_second,
        vec_rep_second,
        vec_head_second,
        bias_up_second,
    )
    reduced = (
        reduced_in,
        reduced_out,
        reduced_kv,
        reduced_up,
        reduced_down,
        reduced_rep,
        reduced_head,
        reduced_bias,
    )
    results = []
    for weight, first, second, grad, rate in zip(weights, firsts, seconds, reduced, rates):
        results.extend(adam_update(weight, first, second, grad, rate))
    return (layer_out, grad_hidden, *results)


def solution(mesh):
    dp, mp = mesh.devices.shape
    bits = (dp // 2).bit_length() - 1
    names = tuple(f"b{k}" for k in range(bits)) + ("core",)
    fine = Mesh(mesh.devices.reshape((2,) * (bits + 1) + (mp,)), names + ("mp",))
    split = P(names)
    inward = P(None, names, "mp")
    outward = P(None, "mp", names)
    head = P(None, "mp")
    stored = (inward,) * 3 + (outward,) * 3 + (inward,) * 6 + (outward,) * 3 + (P(),) * 3 + (head,) * 6
    return jax.shard_map(
        functools.partial(local, bits),
        mesh=fine,
        in_specs=(split,) * 4 + stored,
        out_specs=(split,) * 2 + stored,
        check_vma=False,
    )
```

```python
import functools
import math

import jax
import jax.numpy as jnp
from jax import lax
from jax.experimental import pallas as pl
from jax.experimental.layout import Layout, with_layout_constraint
from jax.experimental.pallas import tpu as pltpu
from jax.sharding import Mesh
from jax.sharding import PartitionSpec as P

D = 768
HEAD_DIM = 64
F = 3072
E = 1408
NQ = 32
STEP_COUNT = 10

NORM_EPS = 1e-06
BETA_ONE = 0.9
BETA_TWO = 0.999
ADAM_EPS = 1e-08
WEIGHT_DECAY = 0.01
MASKED = -1000000000.0

BF = jnp.bfloat16
F32 = jnp.float32
SCALE = HEAD_DIM ** (-0.5)
MIB = 1 << 20


def dot(a, b):
    return lax.dot_general(a, b, (((1,), (0,)), ((), ())), preferred_element_type=F32)


def dot_t(a, b):
    return lax.dot_general(a, b, (((1,), (1,)), ((), ())), preferred_element_type=F32)


def t_dot(a, b):
    return lax.dot_general(a, b, (((0,), (0,)), ((), ())), preferred_element_type=F32)


def swap(values, axis):
    return lax.ppermute(values, axis, [(0, 1), (1, 0)])


def mp_swap(values, distance):
    count = lax.axis_size("mp")
    return lax.ppermute(values, "mp", [(i, i ^ distance) for i in range(count)])


class Plan:
    def __init__(self, bits, mp, items, dp):
        self.bits = bits
        self.mp = mp
        self.dp = dp
        self.items = items
        self.rows = items * 2 * NQ
        self.half = items * NQ
        self.width = D // mp
        self.forth = tuple(f"b{k}" for k in range(bits))
        self.back = self.forth[::-1]
        self.distances = [1 << k for k in range(mp.bit_length() - 1)]

    def bit(self, axis):
        return 1 if axis == "core" else 2 << (self.bits - 1 - int(axis[1:]))

    def masks(self, order):
        found = [0]
        for axis in order + ("core",):
            found = found + [m | self.bit(axis) for m in found]
        return found

    def dp_index(self):
        place = lax.axis_index("core")
        for axis in self.forth:
            place = place + self.bit(axis) * lax.axis_index(axis)
        return place


class Part:
    def __init__(self, tree, low, count, place):
        self.tree, self.low, self.count, self.place = tree, low, count, place


def hold(*values):
    return lax.optimization_barrier(values)


def mp_double(values, distance):
    return jnp.concatenate([values, mp_swap(values, distance)])


def mp_direct(plan, own, sent):
    return [own] + [mp_swap(sent(j), j) for j in range(1, plan.mp)]


def two_trees(pieces, rows):
    return (
        jnp.concatenate([p[None, :rows] for p in pieces]),
        jnp.concatenate([p[None, rows:] for p in pieces]),
    )


def send_pair(plan, pair, k):
    return swap(pair[0], plan.forth[k]), swap(pair[1], plan.back[k])


def send_cores(pair):
    return tuple(swap(v, "core") for v in pair)


def join_pair(pair, got):
    return tuple(jnp.concatenate([v, g]) for v, g in zip(pair, got))


def as_quarters(pair, got, cores, got_cores):
    return tuple(zip(pair, got, cores, got_cores))


def as_trees(plan, cores):
    return {"a": (cores[0], plan.forth), "b": (cores[1], plan.back)}


def line_pairs(plan):
    return [(1, 2), (2, 1)], [(0, 1), (3, 2)], [(1, 0), (2, 3)]


def mp_middle(plan, values):
    if plan.mp != 4:
        return mp_swap(values, 2)
    return lax.ppermute(values, "mp", line_pairs(plan)[0])


def mp_outward(plan, got):
    if plan.mp != 4:
        return got
    return lax.ppermute(got, "mp", line_pairs(plan)[2])


def from_line(plan, across, far, j):
    if plan.mp != 4:
        return across[j - 2]
    me = lax.axis_index("mp")
    return jnp.where((me == 0) | (me == 3), far[j - 2], across[3 - j])


def mp_inward(plan, state):
    kept, sent = state
    if plan.mp != 4:
        return state
    got = lax.ppermute(sent, "mp", line_pairs(plan)[1])
    return kept, add_low(sent, got[::-1])


def mp_across(plan, state):
    kept, sent = state
    if plan.mp != 4:
        return mp_halve(state, 2)
    got = lax.ppermute(sent, "mp", line_pairs(plan)[0])
    return add_low(kept[:1], got[1:]), add_low(kept[1:], got[:1])


def natural_tree(plan, halves, order):
    values = jnp.concatenate(halves)
    values = values.reshape((plan.dp, values.shape[0] // plan.dp) + values.shape[1:])
    back = [0] * plan.dp
    for k, mask in enumerate(plan.masks(order)):
        back[mask] = k
    places = jnp.take(jnp.array(back), jnp.arange(plan.dp) ^ plan.dp_index())
    return jnp.take(values, places, axis=0)


def assemble(plan, trees, parts):
    found = []
    for part in parts:
        halves, order = trees[part.tree]
        natural = natural_tree(plan, halves, order)
        found.append(natural[:, :, part.low : part.low + part.count])
    whole = jnp.concatenate(found, axis=2).transpose(1, 0, 2, 3)
    return whole.reshape(whole.shape[0], -1, whole.shape[-1])


def by_distance(plan, matrices, segments, order):
    places = jnp.array(plan.masks(order)) ^ plan.dp_index()
    found = []
    for name, part in segments:
        blocks = matrices[name]
        blocks = blocks.reshape(blocks.shape[0], plan.dp, -1, blocks.shape[-1])
        blocks = jnp.take(blocks, places, axis=1).transpose(1, 0, 2, 3)
        found.append(blocks[:, :, part.place : part.place + part.count])
    whole = jnp.concatenate(found, axis=2)
    whole = whole.reshape((-1,) + whole.shape[2:])
    return whole[: whole.shape[0] // 2], whole[whole.shape[0] // 2 :]


def add_low(first, second):
    return (first.astype(F32) + second.astype(F32)).astype(BF)


def shrink_send(halves, axes):
    return tuple(swap(sent, axis) for (_, sent), axis in zip(halves, axes))


def shrink_add(halves, found):
    sums = []
    for (kept, _), got in zip(halves, found):
        half = got.shape[0] // 2
        sums.append((add_low(kept[:half], got[:half]), add_low(kept[half:], got[half:])))
    return tuple(sums)


def join_trees(halves):
    return tuple(jnp.concatenate([h[k] for h in halves], axis=1) for k in range(2))


def mp_halve(state, distance):
    kept, sent = state
    got = mp_swap(sent, distance)
    half = got.shape[0] // 2
    return add_low(kept[:half], got[:half]), add_low(kept[half:], got[half:])


def mp_scatter(plan, state):
    kept, sent = state
    pieces = [kept[0]]
    for j in range(1, plan.mp):
        values = kept if j < plan.mp // 2 else sent
        pieces.append(mp_swap(values[j % (plan.mp // 2)], j))
    return pieces


def mp_last(state):
    kept, sent = state
    return kept[0].astype(F32), mp_swap(sent[0], 1).astype(F32)


def norm_parts(values):
    center = values - jnp.mean(values, axis=-1, keepdims=True)
    spread = jnp.mean(center * center, axis=-1, keepdims=True)
    inverse = lax.rsqrt(spread + NORM_EPS)
    return center * inverse, inverse


def norm_backward(grad_out, normed, inverse, gain):
    scaled = grad_out * gain
    inner = (
        scaled
        - jnp.mean(scaled, axis=-1, keepdims=True)
        - normed * jnp.mean(scaled * normed, axis=-1, keepdims=True)
    )
    return inner * inverse


def column_sum(values):
    return jnp.sum(values.astype(F32), axis=0, keepdims=True)


def halves_of(values, items):
    split = values.reshape(items, 2 * NQ, values.shape[-1])
    parts = split[:, :NQ], split[:, NQ:]
    return tuple(p.reshape(items * NQ, values.shape[-1]) for p in parts)


def join_halves(query, caption, items):
    width = query.shape[-1]
    parts = [v.reshape(items, NQ, width) for v in (query, caption)]
    return jnp.concatenate(parts, axis=1).reshape(items * 2 * NQ, width)


def wide(first, second):
    return jnp.concatenate([first, second], axis=1)


def after(values, width):
    return jnp.concatenate([jnp.zeros_like(values), values], axis=1)


def before(values, width):
    return jnp.concatenate([values, jnp.zeros_like(values)], axis=1)


def head_lanes(width):
    lane = lax.broadcasted_iota(jnp.int32, (1, width), 1)
    return [lane // HEAD_DIM == h for h in range(width // HEAD_DIM)]


def only(values, lanes):
    return jnp.where(lanes, values, jnp.zeros_like(values))


def softmax(scores):
    expo = jnp.exp(scores - jnp.max(scores, axis=-1, keepdims=True))
    return expo * (1.0 / jnp.sum(expo, axis=-1, keepdims=True))


def fetch(plan, refs, parts, trees, target, sem):
    if trees is None:
        pltpu.make_async_copy(refs[0], target, sem).start()
        return
    place = plan.dp_index()
    block = sum(p.count for p in parts)
    for part in parts:
        found, order = trees[part.tree]
        for k, mask in enumerate(plan.masks(order)):
            quarter, index = divmod(k, plan.dp // len(found))
            begin = pl.multiple_of((place ^ mask) * block + part.place, 16)
            pieces = refs[found[quarter]].at[pl.ds(index * plan.mp, plan.mp)]
            pltpu.make_async_copy(
                pieces.at[:, pl.ds(part.low, part.count), :],
                target.at[:, pl.ds(begin, part.count), :],
                sem,
            ).start()


def fetch_whole(matrix, target, sem):
    pltpu.make_async_copy(matrix, target, sem).start()


def settle(target, sem):
    pltpu.make_async_copy(target, target, sem).wait()


def spread(plan, source, parts, outs, sem):
    if parts is None:
        pltpu.make_async_copy(source, outs, sem).start()
        return
    place = plan.dp_index()
    block = sum(p.count for p in parts)
    for part in parts:
        halves, order = outs[part.tree]
        for k, mask in enumerate(plan.masks(order)):
            half, index = divmod(k, plan.dp // 2)
            begin = pl.multiple_of((place ^ mask) * block + part.place, 16)
            pieces = halves[half].at[pl.ds(index * plan.mp, plan.mp)]
            pltpu.make_async_copy(
                source.at[:, pl.ds(begin, part.count), :],
                pieces.at[:, pl.ds(part.low, part.count), :],
                sem,
            ).start()


class Weights:
    def __init__(self, plan, trees, matrices):
        self.plan, self.matrices = plan, matrices
        self.direct = all(p.count % 16 == 0 for parts in matrices.values() for p in parts)
        if self.direct:
            self.trees = trees
        else:
            self.whole = {n: assemble(plan, trees, parts) for n, parts in matrices.items()}

    def operands(self, names):
        arrays, found = [], {}
        if not self.direct:
            for name in names:
                found[name] = (len(arrays), self.matrices[name], None)
                arrays.append(self.whole[name])
            return arrays, found
        seen = {}
        for name in names:
            for part in self.matrices[name]:
                if part.tree not in seen:
                    halves, order = self.trees[part.tree]
                    seen[part.tree] = (range(len(arrays), len(arrays) + len(halves)), order)
                    arrays.extend(halves)
            found[name] = (0, self.matrices[name], seen)
        return arrays, found


def gather_operands(sets):
    arrays, starts = [], {}
    for weights, names in sets:
        more, found = weights.operands(names)
        base = len(arrays)
        for name, (place, parts, trees) in found.items():
            starts[name] = functools.partial(
                lambda refs, target, sem, base, place, parts, trees, plan: fetch(
                    plan, refs[base + place :], parts, trees, target, sem
                )
                if trees is None
                else fetch(plan, refs[base:], parts, trees, target, sem),
                base=base,
                place=place,
                parts=parts,
                trees=trees,
                plan=weights.plan,
            )
        arrays.extend(more)
    return arrays, starts


class Gradients:
    def __init__(self, plan, trees, matrices, over):
        self.plan, self.trees, self.matrices, self.over = plan, trees, matrices, over
        self.direct = all(p.count % 16 == 0 for parts, _ in matrices.values() for p in parts)

    def shapes(self):
        found = []
        if self.direct:
            for _, rows, columns in self.trees.values():
                shape = (self.plan.dp // 2 * self.over, rows, columns)
                found += [jax.ShapeDtypeStruct(shape, BF)] * 2
            return found
        for parts, rows in self.matrices.values():
            columns = self.trees[parts[0].tree][2]
            found.append(jax.ShapeDtypeStruct((self.over, rows, columns), BF))
        return found

    def write(self, name, source, refs, sem):
        parts = self.matrices[name][0]
        if self.direct:
            outs = {
                tree: (refs[2 * k : 2 * k + 2], order)
                for k, (tree, (order, _, _)) in enumerate(self.trees.items())
            }
            spread(self.plan, source, parts, outs, sem)
        else:
            spread(self.plan, source, None, refs[list(self.matrices).index(name)], sem)

    def halves(self, arrays):
        if self.direct:
            return {t: tuple(arrays[2 * k : 2 * k + 2]) for k, t in enumerate(self.trees)}
        named = dict(zip(self.matrices, arrays))
        found = {}
        for tree, (order, _, _) in self.trees.items():
            segments = [
                (name, part)
                for name, (parts, _) in self.matrices.items()
                for part in parts
                if part.tree == tree
            ]
            segments.sort(key=lambda s: s[1].low)
            found[tree] = by_distance(self.plan, named, segments, order)
        return found


def call(kernel, ins, places, outs, out_places, scratch, limit):
    return pl.pallas_call(
        kernel,
        out_shape=outs,
        in_specs=[pl.BlockSpec(memory_space=p) for p in places],
        out_specs=[pl.BlockSpec(memory_space=p) for p in out_places],
        scratch_shapes=scratch,
        compiler_params=pltpu.CompilerParams(vmem_limit_bytes=limit * MIB),
        cost_estimate=pl.CostEstimate(flops=1000, bytes_accessed=1000, transcendentals=0),
    )(*ins)


ANY, HBM, VMEM, SMEM = pl.ANY, pltpu.HBM, pltpu.VMEM, pltpu.SMEM
DMA = pltpu.SemaphoreType.DMA


def self_mask(plan, lengths, me):
    count = plan.rows
    row = lax.broadcasted_iota(jnp.int32, (count, count), 0)
    col = lax.broadcasted_iota(jnp.int32, (count, count), 1)
    span = 2 * NQ
    limit = jnp.zeros((count, count), jnp.int32)
    for i in range(plan.items):
        limit = jnp.where(col // span == i, lengths[me * plan.items + i], limit)
    inside = col % span
    valid = (row // span == col // span) & ((inside < NQ) | (inside - NQ < limit))
    return jnp.where(valid, 0.0, MASKED).astype(F32)


def load_tokens(plan, hidden, target, sem):
    me = lax.axis_index("mp")
    return pltpu.make_async_copy(hidden.at[pl.ds(me * plan.items, plan.items)], target, sem)


def distance_shapes(plan):
    shape = (plan.half, plan.width)
    return [
        jax.ShapeDtypeStruct(shape, BF),
        jax.ShapeDtypeStruct(shape, BF),
        jax.ShapeDtypeStruct((plan.mp - 2,) + shape, BF),
    ]


def put_distance(refs, j, values):
    if j < 2:
        refs[j][...] = values
    else:
        refs[2][j - 2] = values


def get_distance(refs, j, span=slice(None)):
    return refs[j][span, :] if j < 2 else refs[2][j - 2, span, :]


def self_forward(plan, lengths, hidden, vec, heads, sets):
    arrays, starts = gather_operands(sets)
    count = len(arrays)
    mp, rows, half, width, items = plan.mp, plan.rows, plan.half, plan.width, plan.items

    def kernel(lengths, hidden, vec, heads, *rest):
        refs = rest[:count]
        qk_out, v_out, context_out, z_out = rest[count : count + 4]
        cross = rest[count + 4 : count + 7]
        wholes = rest[count + 7 : count + 10]
        tokens, w_qk, w_vc, w_oo, sems = rest[count + 10 :]
        me = lax.axis_index("mp")
        loaded = load_tokens(plan, hidden, tokens, sems.at[0])
        loaded.start()
        starts["qk"](refs, w_qk, sems.at[1])
        starts["vc"](refs, w_vc, sems.at[2])
        starts["oo"](refs, w_oo, sems.at[3])
        mask = self_mask(plan, lengths, me)
        lanes = head_lanes(width)
        loaded.wait()
        x = tokens[...].reshape(rows, D)
        total = x.astype(F32) + vec[0:1, :]
        kept = []
        for k, matrix in enumerate((w_qk, w_vc, w_oo)):
            settle(matrix, sems.at[1 + k])
            kept.append(pltpu.make_async_copy(matrix, wholes[k], sems.at[4 + k]))
            kept[-1].start()
        for j in range(mp):
            both = (dot(x, w_qk[j]) + heads[j, 0:1, :]).astype(BF)
            qk_out[j] = both
            q, k = both[:, :width], both[:, width:]
            v = (dot(x, w_vc[j]) + heads[j, 1:2, :]).astype(BF)[:, :width]
            v_out[j] = v
            context = jnp.zeros((rows, width), F32)
            for lane in lanes:
                probs = softmax(dot_t(only(q, lane), k) * SCALE + mask)
                context = context + only(dot(probs.astype(BF), v), lane)
            context = context.astype(BF)
            context_out[j] = context
            total = total + dot_t(before(context, width), w_oo[j])
        z_out[...] = total
        normed, _ = norm_parts(total)
        u = halves_of(normed * vec[4:5, :] + vec[5:6, :], items)[0].astype(BF)
        for j in range(mp):
            maps = (dot(u, w_vc[j]) + heads[j, 1:2, :]).astype(BF)
            put_distance(cross, j, maps[:, width:])
        for copy in kept:
            copy.wait()

    whole = jax.ShapeDtypeStruct((mp, D, 2 * width), BF)
    outs = [
        jax.ShapeDtypeStruct((mp, rows, 2 * width), BF),
        jax.ShapeDtypeStruct((mp, rows, width), BF),
        jax.ShapeDtypeStruct((mp, rows, width), BF),
        jax.ShapeDtypeStruct((rows, D), F32),
        *distance_shapes(plan),
        whole,
        whole,
        whole,
    ]
    found = call(
        kernel,
        (lengths, hidden, vec, heads, *arrays),
        [SMEM, HBM, VMEM, VMEM] + [ANY] * count,
        outs,
        [VMEM] * 7 + [HBM] * 3,
        [
            pltpu.VMEM((items, 2 * NQ, D), BF),
            *[pltpu.VMEM((mp, D, 2 * width), BF)] * 3,
            DMA((7,)),
        ],
        28,
    )
    return (*found[:4], found[4:7], found[7:])


def load_images(images, held, sems):
    count = images.shape[0]
    cut = -(-count // 4)
    found = []
    for k in range(0, count, cut):
        span = pl.ds(k, min(cut, count - k))
        found.append(pltpu.make_async_copy(images.at[span], held.at[span], sems.at[k // cut]))
        found[-1].start()
    return found, cut


def image_maps(plan, images, bias, maps):
    items, keys, features = images.shape
    width = plan.width
    padded = -(-keys // 128) * 128

    def kernel(images, bias, maps, out, held, w_kv, sems, w_sem):
        weights = pltpu.make_async_copy(maps, w_kv, w_sem.at[0])
        weights.start()
        loaded, cut = load_images(images, held, sems)
        weights.wait()
        for n, copy in enumerate(loaded):
            copy.wait()

            def step(i, carry):
                both = (dot(held[i], w_kv[...]) + bias[2:3, :]).astype(BF)
                out[i, 0:keys, :] = both
                out[i, keys:padded, :] = jnp.zeros((padded - keys, 2 * width), BF)
                return carry

            lax.fori_loop(n * cut, min(items, (n + 1) * cut), step, 0)

    return call(
        kernel,
        (images, bias, maps),
        [ANY, VMEM, ANY],
        [jax.ShapeDtypeStruct((items, padded, 2 * width), BF)],
        [VMEM],
        [
            pltpu.VMEM((items, keys, features), BF),
            pltpu.VMEM((features, 2 * width), BF),
            DMA((4,)),
            DMA((1,)),
        ],
        28,
    )[0]


def key_mask(plan, keys, padded):
    lane = lax.broadcasted_iota(jnp.int32, (1, padded), 1)
    return jnp.where(lane < keys, 0.0, MASKED).astype(F32)


def spread_heads(values, lanes):
    return jnp.concatenate([only(values, lane) for lane in lanes], axis=0)


def gather_heads(values, lanes):
    total = None
    for h, lane in enumerate(lanes):
        part = only(values[h * NQ : (h + 1) * NQ], lane)
        total = part if total is None else total + part
    return total


def cross_attend(plan, keys, queries, kv):
    mp, half, width, items = plan.mp, plan.half, plan.width, plan.items
    padded = kv.shape[1]

    def kernel(*refs):
        queries, kv, contexts = refs[:3], refs[3], refs[4:]
        me = lax.axis_index("mp")
        lanes = head_lanes(width)
        mask = key_mask(plan, keys, padded)
        for j in range(mp):
            rows = []
            for i in range(items):
                q = spread_heads(get_distance(queries, j, slice(i * NQ, (i + 1) * NQ)), lanes)
                both = kv[(me ^ j) * items + i]
                probs = softmax(dot_t(q, both[:, :width]) * SCALE + mask)
                rows.append(gather_heads(dot(probs.astype(BF), both[:, width:]), lanes))
            put_distance(contexts, j, jnp.concatenate(rows, axis=0).astype(BF))

    return call(
        kernel,
        (*queries, kv),
        [VMEM] * 4,
        distance_shapes(plan),
        [VMEM] * 3,
        [],
        24,
    )


def cross_output(plan, vec, z_first, contexts, whole_oo):
    mp, half, width, items = plan.mp, plan.half, plan.width, plan.items

    def kernel(vec, z_first, *rest):
        contexts, whole_oo = rest[:3], rest[3]
        z_out, kept, given, w_oo, sems = rest[4:]
        me = lax.axis_index("mp")
        fetch_whole(whole_oo, w_oo, sems.at[0])
        normed, _ = norm_parts(z_first[...])
        query, caption = halves_of(normed * vec[4:5, :] + vec[5:6, :], items)
        total = query + vec[1:2, :]
        settle(w_oo, sems.at[0])
        for j in range(mp):
            total = total + dot_t(after(get_distance(contexts, j), width), w_oo[j])
        z_out[...] = total
        normed, _ = norm_parts(total)
        second = normed * vec[6:7, :] + vec[7:8, :]
        low = (me & 1) == 0
        kept[...] = jnp.where(low, second, caption)
        given[...] = jnp.where(low, caption, second).astype(BF)

    return call(
        kernel,
        (vec, z_first, *contexts, whole_oo),
        [VMEM] * 5 + [HBM],
        [
            jax.ShapeDtypeStruct((half, D), F32),
            jax.ShapeDtypeStruct((half, D), F32),
            jax.ShapeDtypeStruct((half, D), BF),
        ],
        [VMEM] * 3,
        [pltpu.VMEM((mp, D, 2 * width), BF), DMA((1,))],
        16,
    )


def feed_forward(plan, vec, heads, kept, got, cotangent, sets, gradients):
    arrays, starts = gather_operands(sets)
    count = len(arrays)
    mp, half, items = plan.mp, plan.half, plan.items
    hidden_width = F // mp
    shapes = gradients.shapes()

    def kernel(vec, heads, kept, got, cotangent, *rest):
        refs, rest = rest[:count], rest[count:]
        layer, kept_back, given_back, sums, bias_sums = rest[:5]
        grad_out = rest[5 : 5 + len(shapes)]
        top, w_up, w_down, slope, act, up_grad, down_grad, w_sems, sems = rest[5 + len(shapes) :]
        me = lax.axis_index("mp")
        group = me & 1
        starts["up"](refs, w_up, w_sems.at[0])
        starts["down"](refs, w_down, w_sems.at[1])
        tops = []
        for s in range(2):
            first = (me ^ s) * items
            tops.append(
                pltpu.make_async_copy(
                    cotangent.at[
                        pl.ds(first, items), pl.ds(pl.multiple_of(group * NQ, NQ), NQ), :
                    ],
                    top.at[s],
                    sems.at[2 + s],
                )
            )
            tops[-1].start()
        x = jnp.concatenate([kept[...], got[...].astype(F32)], axis=0)
        low = x.astype(BF)
        low_t = low.T
        total = x + vec[pl.ds(2 + group, 1), :]
        settle(w_up, w_sems.at[0])
        for z in range(mp):
            bias = wide(
                heads[z, pl.ds(3 + 2 * group, 1), :], heads[z, pl.ds(4 + 2 * group, 1), :]
            )
            pre = dot(low, w_up[z]) + bias
            cdf = 0.5 + 0.5 * lax.erf(pre * (0.5**0.5))
            value = (pre * cdf).astype(BF)
            act[z] = value
            slope[z] = cdf + pre * jnp.exp(-0.5 * pre * pre) * (1.0 / math.sqrt(2.0 * math.pi))
            if z == 0:
                settle(w_down, w_sems.at[1])
            total = total + dot_t(value, w_down[z])
        normed, inverse = norm_parts(total)
        gain = vec[pl.ds(8 + 2 * group, 1), :]
        third = normed * gain + vec[pl.ds(9 + 2 * group, 1), :]
        layer[...] = third.astype(BF).reshape(2, items, NQ, D)
        for t in tops:
            t.wait()
        grad = top[...].reshape(2 * half, D).astype(F32)
        back = norm_backward(grad, normed, inverse, gain)
        branch = back.astype(BF)
        sums[0:1, :] = column_sum(branch)
        sums[1:2, :] = column_sum(grad * normed)
        sums[2:3, :] = column_sum(grad)
        branch_t = branch.T
        for z in range(mp):
            down_grad[z] = dot(branch_t, act[z]).astype(BF)
        gradients.write("down", down_grad, grad_out, sems.at[0])
        for z in range(mp):
            pull = (dot(branch, w_down[z]) * slope[z]).astype(BF)
            bias_sums[pl.ds(me ^ z, 1), :] = column_sum(pull)
            up_grad[z] = dot(low_t, pull).astype(BF)
            back = back + dot_t(pull, w_up[z])
        gradients.write("up", up_grad, grad_out, sems.at[1])
        kept_back[...] = back[:half]
        given_back[...] = back[half:].astype(BF)
        settle(down_grad, sems.at[0])
        settle(up_grad, sems.at[1])

    outs = [
        jax.ShapeDtypeStruct((2, items, NQ, D), BF),
        jax.ShapeDtypeStruct((half, D), F32),
        jax.ShapeDtypeStruct((half, D), BF),
        jax.ShapeDtypeStruct((3, D), F32),
        jax.ShapeDtypeStruct((mp, hidden_width), F32),
        *shapes,
    ]
    found = call(
        kernel,
        (vec, heads, kept, got, cotangent, *arrays),
        [VMEM] * 4 + [HBM] + [ANY] * count,
        outs,
        [VMEM] * 5 + [HBM] * len(shapes),
        [
            pltpu.VMEM((2, items, NQ, D), BF),
            pltpu.VMEM((mp, D, hidden_width), BF),
            pltpu.VMEM((mp, D, hidden_width), BF),
            pltpu.VMEM((mp, 2 * half, hidden_width), F32),
            pltpu.VMEM((mp, 2 * half, hidden_width), BF),
            pltpu.VMEM((mp, D, hidden_width), BF),
            pltpu.VMEM((mp, D, hidden_width), BF),
            DMA((2,)),
            DMA((4,)),
        ],
        48,
    )
    return (*found[:5], gradients.halves(found[5:]))


def cross_output_backward(plan, vec, z_second, kept, got, whole_oo):
    mp, half, width = plan.mp, plan.half, plan.width

    def kernel(vec, z_second, kept, got, whole_oo, *rest):
        back_out, branch_out, caption, sums = rest[:4]
        context_back = rest[4:7]
        w_oo, sems = rest[7:]
        low = (lax.axis_index("mp") & 1) == 0
        fetch_whole(whole_oo, w_oo, sems.at[0])
        other = got[...].astype(F32)
        grad = jnp.where(low, kept[...], other)
        caption[...] = jnp.where(low, other, kept[...])
        normed, inverse = norm_parts(z_second[...])
        back = norm_backward(grad, normed, inverse, vec[6:7, :])
        branch = back.astype(BF)
        back_out[...] = back
        branch_out[...] = branch
        sums[0:1, :] = column_sum(branch)
        sums[1:2, :] = column_sum(grad * normed)
        sums[2:3, :] = column_sum(grad)
        settle(w_oo, sems.at[0])
        for j in range(mp):
            put_distance(context_back, j, dot(branch, w_oo[j]).astype(BF)[:, width:])

    found = call(
        kernel,
        (vec, z_second, kept, got, whole_oo),
        [VMEM] * 4 + [HBM],
        [
            jax.ShapeDtypeStruct((half, D), F32),
            jax.ShapeDtypeStruct((half, D), BF),
            jax.ShapeDtypeStruct((half, D), F32),
            jax.ShapeDtypeStruct((3, D), F32),
            *distance_shapes(plan),
        ],
        [VMEM] * 7,
        [pltpu.VMEM((mp, D, 2 * width), BF), DMA((1,))],
        16,
    )
    return (*found[:4], found[4:])


def cross_attend_backward(plan, keys, queries, context_back, kv):
    mp, half, width, items = plan.mp, plan.half, plan.width, plan.items
    padded = kv.shape[1]

    def kernel(*refs):
        queries, context_back, kv = refs[:3], refs[3:6], refs[6]
        kv_back, value_sum, query_back = refs[7], refs[8], refs[9:]
        me = lax.axis_index("mp")
        lanes = head_lanes(width)
        mask = key_mask(plan, keys, padded)
        total = jnp.zeros((1, width), F32)
        for j in range(mp):
            rows = []
            for i in range(items):
                span = slice(i * NQ, (i + 1) * NQ)
                item = (me ^ j) * items + i
                q = spread_heads(get_distance(queries, j, span), lanes)
                g = spread_heads(get_distance(context_back, j, span), lanes)
                both = kv[item]
                k, v = both[:, :width], both[:, width:]
                probs = softmax(dot_t(q, k) * SCALE + mask)
                pulled = dot_t(g, v)
                scored = probs * (pulled - jnp.sum(probs * pulled, axis=-1, keepdims=True))
                scored = scored.astype(BF)
                value_back = t_dot(probs.astype(BF), g).astype(BF)
                key_back = (t_dot(scored, q) * SCALE).astype(BF)
                kv_back[item] = wide(key_back, value_back)
                total = total + column_sum(value_back)
                rows.append(gather_heads(dot(scored, k), lanes) * SCALE)
            put_distance(query_back, j, jnp.concatenate(rows, axis=0).astype(BF))
        value_sum[...] = total

    found = call(
        kernel,
        (*queries, *context_back, kv),
        [VMEM] * 7,
        [
            jax.ShapeDtypeStruct((mp * items, padded, 2 * width), BF),
            jax.ShapeDtypeStruct((1, width), F32),
            *distance_shapes(plan),
        ],
        [VMEM] * 5,
        [],
        28,
    )
    return found[0], found[1], found[2:]


def put_columns(target, row, found, me, width):
    for z in range(len(found)):
        total = jnp.zeros((1, width), F32)
        for j, values in enumerate(found):
            total = jnp.where((me ^ j) == z, values, total)
        target[row : row + 1, z * width : (z + 1) * width] = total


def cross_input_backward(plan, vec, z_first, back, caption, query_back, whole_vc):
    mp, rows, half, width, items = plan.mp, plan.rows, plan.half, plan.width, plan.items

    def kernel(vec, z_first, back, caption, *rest):
        query_back, whole_vc = rest[:3], rest[3]
        first_back, sums, w_vc, sems = rest[4:]
        me = lax.axis_index("mp")
        fetch_whole(whole_vc, w_vc, sems.at[0])
        total = back[...]
        found = [column_sum(get_distance(query_back, j)) for j in range(mp)]
        put_columns(sums, 3, found, me, width)
        settle(w_vc, sems.at[0])
        for j in range(mp):
            total = total + dot_t(after(get_distance(query_back, j), width), w_vc[j])
        first_grad = join_halves(total, caption[...], items)
        normed, inverse = norm_parts(z_first[...])
        first = norm_backward(first_grad, normed, inverse, vec[4:5, :])
        first_back[...] = first
        sums[0:1, :] = column_sum(first_grad * normed)
        sums[1:2, :] = column_sum(first_grad)
        sums[2:3, :] = column_sum(first.astype(BF))

    return call(
        kernel,
        (vec, z_first, back, caption, *query_back, whole_vc),
        [VMEM] * 7 + [HBM],
        [
            jax.ShapeDtypeStruct((rows, D), F32),
            jax.ShapeDtypeStruct((4, D), F32),
        ],
        [VMEM] * 2,
        [pltpu.VMEM((mp, D, 2 * width), BF), DMA((1,))],
        20,
    )


def image_gradient(plan, images, kv_back):
    items, keys, features = images.shape
    width = plan.width
    even = keys // 128 * 128

    def kernel(images, kv_back, out, held, turned, sems):
        loaded, cut = load_images(images, held, sems)
        total = jnp.zeros((2 * width, features), F32)
        for i in range(items):
            turned[i] = kv_back[i, 0:even, :].T
        for i in range(items):
            if i % cut == 0:
                loaded[i // cut].wait()
            total = total + dot(turned[i], held[i, 0:even, :])
        if keys > even:
            left = jnp.concatenate([held[i, even:keys, :] for i in range(items)], axis=0)
            right = jnp.concatenate([kv_back[i, even:keys, :] for i in range(items)], axis=0)
            total = total + t_dot(right, left)
        out[...] = total.astype(BF).T

    return call(
        kernel,
        (images, kv_back),
        [HBM, VMEM],
        [jax.ShapeDtypeStruct((features, 2 * width), BF)],
        [VMEM],
        [
            pltpu.VMEM((items, keys, features), BF),
            pltpu.VMEM((items, 2 * width, even), BF),
            DMA((4,)),
        ],
        40,
    )[0]


def self_backward(plan, lengths, saved, found_sums, wholes):
    mp, rows, width = plan.mp, plan.rows, plan.width
    count = len(saved) + len(found_sums)
    vectors_rows = 16 + 2 * mp * (F // mp // D)

    def kernel(lengths, *rest):
        vec, first_back, qk_all, v_all = rest[:4]
        first_sums, cross_sums, third_sums, bias_sums, value_sum = rest[4:count]
        wholes, rest = rest[count : count + 3], rest[count + 3 :]
        token_back, vectors, maps_back, value_maps = rest[:4]
        w_qk, w_vc, w_oo, w_sems = rest[4:]
        me = lax.axis_index("mp")
        for k, target in enumerate((w_qk, w_vc, w_oo)):
            fetch_whole(wholes[k], target, w_sems.at[k])
        mask = self_mask(plan, lengths, me)
        lanes = head_lanes(width)
        group = me & 1
        vectors[...] = jnp.zeros((vectors_rows, D), F32)
        vectors[0:1, :] = first_sums[2:3, :]
        vectors[1:2, :] = cross_sums[0:1, :]
        vectors[pl.ds(2 + group, 1), :] = third_sums[0:1, :]
        vectors[4:6, :] = first_sums[0:2, :]
        vectors[6:8, :] = cross_sums[1:3, :]
        vectors[pl.ds(8 + 2 * group, 1), :] = third_sums[1:2, :]
        vectors[pl.ds(9 + 2 * group, 1), :] = third_sums[2:3, :]
        vectors[14:15, :] = first_sums[3:4, :]
        for z in range(mp):
            span = slice(z * width, (z + 1) * width)
            vectors[15:16, span] = jnp.where(me == z, value_sum[...], 0.0)
        for g in range(2):
            vectors[16 + g * mp : 16 + (g + 1) * mp, :] = jnp.where(
                group == g, bias_sums[...], 0.0
            )
        total = first_back[...]
        self_branch = total.astype(BF)
        settle(w_oo, w_sems.at[2])
        query_sums, value_sums = [], []
        for z in range(mp):
            pulled = dot(self_branch, w_oo[z]).astype(BF)[:, :width]
            q, k, v = qk_all[z][:, :width], qk_all[z][:, width:], v_all[z]
            query_grad = jnp.zeros((rows, width), F32)
            key_grad = jnp.zeros((rows, width), F32)
            value_grad = jnp.zeros((rows, width), F32)
            for lane in lanes:
                q_h, g_h = only(q, lane), only(pulled, lane)
                probs = softmax(dot_t(q_h, k) * SCALE + mask)
                wanted = dot_t(g_h, v)
                scored = probs * (wanted - jnp.sum(probs * wanted, axis=-1, keepdims=True))
                scored = scored.astype(BF)
                value_grad = value_grad + t_dot(probs.astype(BF), g_h)
                query_grad = query_grad + only(dot(scored, k), lane)
                key_grad = key_grad + t_dot(scored, q_h)
            query_grad = (query_grad * SCALE).astype(BF)
            value_grad = value_grad.astype(BF)
            query_sums.append(column_sum(query_grad))
            value_sums.append(column_sum(value_grad))
            both = wide(query_grad, (key_grad * SCALE).astype(BF))
            maps_back[z] = both
            value_maps[z] = value_grad
            if z == 0:
                settle(w_qk, w_sems.at[0])
                settle(w_vc, w_sems.at[1])
            total = total + dot_t(both, w_qk[z]) + dot_t(before(value_grad, width), w_vc[z])
        put_columns(vectors, 12, query_sums, me, width)
        put_columns(vectors, 13, value_sums, me, width)
        token_back[...] = total.astype(BF)

    return call(
        kernel,
        (lengths, *saved, *found_sums, *wholes),
        [SMEM] + [VMEM] * count + [HBM] * 3,
        [
            jax.ShapeDtypeStruct((rows, D), BF),
            jax.ShapeDtypeStruct((vectors_rows, D), F32),
            jax.ShapeDtypeStruct((mp, rows, 2 * width), BF),
            jax.ShapeDtypeStruct((mp, rows, width), BF),
        ],
        [VMEM] * 4,
        [pltpu.VMEM((mp, D, 2 * width), BF)] * 3 + [DMA((3,))],
        32,
    )


def output_gradient(plan, first_back, branch, context_all, contexts, gradients):
    mp, width = plan.mp, plan.width
    shapes = gradients.shapes()

    def kernel(first_back, branch, context_all, *rest):
        cross_context, grad_out = rest[:3], rest[3 : 3 + len(shapes)]
        g_oo, sems = rest[3 + len(shapes) :]
        branches_t = jnp.concatenate([first_back[...].astype(BF), branch[...]], axis=0).T
        for z in range(mp):
            contexts = jnp.concatenate(
                [
                    before(context_all[z], width),
                    after(get_distance(cross_context, z), width),
                ],
                axis=0,
            )
            g_oo[z] = dot(branches_t, contexts).astype(BF)
        gradients.write("oo", g_oo, grad_out, sems.at[0])
        settle(g_oo, sems.at[0])

    found = call(
        kernel,
        (first_back, branch, context_all, *contexts),
        [VMEM] * 6,
        shapes,
        [HBM] * len(shapes),
        [pltpu.VMEM((mp, D, 2 * width), BF), DMA((1,))],
        24,
    )
    return gradients.halves(found)


def self_gradient(plan, hidden, saved, gradients):
    mp, rows, half, width, items = plan.mp, plan.rows, plan.half, plan.width, plan.items
    shapes = gradients.shapes()
    count = len(saved)

    def kernel(hidden, *rest):
        vec, z_first, maps_back, value_maps = rest[:4]
        query_back = rest[4:7]
        grad_out = rest[count : count + len(shapes)]
        tokens, g_qk, g_vc, sems = rest[count + len(shapes) :]
        loaded = load_tokens(plan, hidden, tokens, sems.at[0])
        loaded.start()
        normed, _ = norm_parts(z_first[...])
        u = halves_of(normed * vec[4:5, :] + vec[5:6, :], items)[0].astype(BF)
        loaded.wait()
        inputs_t = jnp.concatenate([tokens[...].reshape(rows, D), u], axis=0).T
        for z in range(mp):
            g_qk[z] = dot(inputs_t[:, :rows], maps_back[z]).astype(BF)
        gradients.write("qk", g_qk, grad_out, sems.at[1])
        for z in range(mp):
            maps = jnp.concatenate(
                [before(value_maps[z], width), after(get_distance(query_back, z), width)], axis=0
            )
            g_vc[z] = dot(inputs_t, maps).astype(BF)
        gradients.write("vc", g_vc, grad_out, sems.at[2])
        settle(g_qk, sems.at[1])
        settle(g_vc, sems.at[2])

    found = call(
        kernel,
        (hidden, *saved),
        [HBM] + [VMEM] * count,
        shapes,
        [HBM] * len(shapes),
        [pltpu.VMEM((items, 2 * NQ, D), BF)]
        + [pltpu.VMEM((mp, D, 2 * width), BF)] * 2
        + [DMA((3,))],
        24,
    )
    return gradients.halves(found)


def place_layer(plan, two, across, far):
    mp, items = plan.mp, plan.items

    def kernel(two, across, far, out):
        me = lax.axis_index("mp")
        for j in range(mp):
            source = me ^ j
            values = two[j] if j < 2 else from_line(plan, across, far, j)
            for s in range(2):
                out[
                    pl.ds((source ^ s) * items, items),
                    pl.ds(pl.multiple_of((source & 1) * NQ, NQ), NQ),
                    :,
                ] = values[s]

    return call(
        kernel,
        (two, across, far),
        [VMEM] * 3,
        [jax.ShapeDtypeStruct((mp * items, 2 * NQ, D), BF)],
        [VMEM],
        [],
        16,
    )[0]


def place_gradient(plan, two, across, far):
    mp, items = plan.mp, plan.items

    def kernel(two, across, far, out):
        me = lax.axis_index("mp")
        for j in range(mp):
            values = two[j] if j < 2 else from_line(plan, across, far, j)
            values = values.astype(F32).reshape(items, 2 * NQ, D)
            out[pl.ds((me ^ j) * items, items)] = values

    return call(
        kernel,
        (two, across, far),
        [VMEM] * 3,
        [jax.ShapeDtypeStruct((mp * items, 2 * NQ, D), F32)],
        [VMEM],
        [],
        24,
    )[0]


def adam_update(weight, first, second, grad, rate):
    first_new = BETA_ONE * first + (1.0 - BETA_ONE) * grad
    second_new = BETA_TWO * second + (1.0 - BETA_TWO) * grad * grad
    first_hat = first_new / (1.0 - BETA_ONE**STEP_COUNT)
    second_hat = second_new / (1.0 - BETA_TWO**STEP_COUNT)
    weight_new = weight - rate * (
        first_hat / (jnp.sqrt(second_hat) + ADAM_EPS) + WEIGHT_DECAY * weight
    )
    return (first_new, second_new, weight_new)


def local(
    bits,
    hidden,
    images,
    caption_len,
    cotangent,
    attn_in,
    attn_in_first,
    attn_in_second,
    attn_out,
    attn_out_first,
    attn_out_second,
    cross_key_value_maps,
    cross_kv_first,
    cross_kv_second,
    ffn_up,
    ffn_up_first,
    ffn_up_second,
    ffn_down,
    ffn_down_first,
    ffn_down_second,
    vec_rep,
    vec_rep_first,
    vec_rep_second,
    query_value_bias_rows,
    vec_head_first,
    vec_head_second,
    bias_up,
    bias_up_first,
    bias_up_second,
):
    mp = lax.axis_size("mp")
    me = lax.axis_index("mp")
    plan = Plan(bits, mp, hidden.shape[0] // mp, 2 ** (bits + 1))
    forth, back = plan.forth, plan.back
    low = (me & 1) == 0
    keys = images.shape[1]
    attn_rows, kv_rows, ffn_rows = attn_in.shape[1], cross_key_value_maps.shape[1], ffn_up.shape[1]
    oo_first = attn_rows // 32 * 16 or attn_rows // 2
    oo_second = attn_rows - oo_first

    def side(values):
        return jnp.concatenate([values[0], values[1]], axis=1)

    none = jnp.zeros_like(query_value_bias_rows[0])
    bias_rows = query_value_bias_rows
    packed = jnp.concatenate(
        [
            jnp.concatenate([bias_rows[0], none])[None],
            jnp.concatenate([bias_rows[1], bias_rows[2]])[None],
            jnp.concatenate([none, bias_rows[3]])[None],
            bias_up.reshape(-1, 2 * plan.width),
            jnp.zeros((1, 2 * plan.width), F32),
        ]
    )

    def three(values):
        found = []
        for _ in range(3):
            part = lax.reduce_precision(values, 8, 7)
            found.append(part.astype(BF))
            values = values - part
        return jnp.concatenate(found)

    low_in = attn_in.astype(BF)
    low_oo = side(attn_out.astype(BF).transpose(0, 2, 1))
    low_kv = side(cross_key_value_maps.astype(BF))
    attn_first, attn_second = attn_rows + oo_first, attn_rows + oo_second
    first_shard = jnp.concatenate(
        [
            side(low_in[:2]),
            low_oo[:oo_first],
            side(low_in[2:]),
            low_oo[oo_first:],
            three(packed),
        ]
    )
    group = me & 1
    low_ffn = jnp.concatenate([ffn_up.astype(BF), ffn_down.astype(BF).transpose(0, 2, 1)], axis=1)
    third_own = lax.dynamic_index_in_dim(low_ffn, group, 0, keepdims=False)
    third_other = lax.dynamic_index_in_dim(low_ffn, 1 - group, 0, keepdims=False)
    early, last = range(plan.bits - 1), range(plan.bits - 1, plan.bits)

    wide_columns, hidden_columns = 2 * plan.width, F // mp
    attn_parts = {
        "qk": [Part("a", 0, attn_rows, 0)],
        "vc": [Part("b", 0, attn_rows, 0)],
        "oo": [Part("a", attn_rows, oo_first, 0), Part("b", attn_rows, oo_second, oo_first)],
    }
    attn_gradients = Gradients(
        plan,
        {"a": (forth, attn_rows, wide_columns), "b": (back, attn_rows, wide_columns)},
        {"qk": (attn_parts["qk"], D), "vc": (attn_parts["vc"], D)},
        mp,
    )
    out_gradients = Gradients(
        plan,
        {"a": (forth, oo_first, wide_columns), "b": (back, oo_second, wide_columns)},
        {"oo": ([Part("a", 0, oo_first, 0), Part("b", 0, oo_second, oo_first)], D)},
        mp,
    )
    ffn_gradients = Gradients(
        plan,
        {"a": (forth, ffn_rows, hidden_columns), "b": (back, ffn_rows, hidden_columns)},
        {"up": ([Part("a", 0, ffn_rows, 0)], D), "down": ([Part("b", 0, ffn_rows, 0)], D)},
        mp,
    )

    first = mp_direct(plan, first_shard, lambda j: first_shard)
    maps = lax.all_gather(low_kv, forth + ("core",), axis=0, tiled=True)
    images = with_layout_constraint(images, Layout(major_to_minor=(0, 1, 2)))
    first, images, third_own, third_other = hold(first, images, third_own, third_other)
    packed_rows = packed.shape[0]
    heads = jnp.stack([p[attn_first + attn_second :].astype(F32) for p in first])
    heads = heads.reshape(mp, 3, packed_rows, heads.shape[-1]).sum(axis=1)
    first = (
        jnp.stack([p[:attn_first] for p in first]),
        jnp.stack([p[attn_first : attn_first + attn_second] for p in first]),
    )
    near = mp_swap(third_other, 1)
    for k in early:
        got = send_pair(plan, first, k)
        if k < plan.bits - 2:
            first = join_pair(first, got)
    got, near = hold(got, near)
    first = join_pair(first, got)
    third = jnp.stack([third_own, near])
    got = send_pair(plan, first, plan.bits - 1)
    first_cores = send_cores(first)
    for distance in plan.distances[1:]:
        if distance > 2:
            third = mp_double(third, distance)
    far_up = mp_swap(third[:, :ffn_rows], 2)
    kv_all = image_maps(plan, images, packed, maps)
    got, first_cores, kv_all, far_up = hold(got, first_cores, kv_all, far_up)
    got_cores = send_cores(got)
    far_down = mp_swap(third[:, ffn_rows:], 2)

    def before_last(values, order):
        for axis in order[:-2]:
            values = jnp.concatenate([values, swap(values, axis)])
        return values, swap(values, order[-2])

    up, up_got = before_last(jnp.concatenate([third[:, :ffn_rows], far_up]), forth)
    (got_cores,) = hold(got_cores)
    attn_set = Weights(
        plan, as_trees(plan, as_quarters(first, got, first_cores, got_cores)), attn_parts
    )
    qk_all, v_all, context_all, z_first, cross, wholes = self_forward(
        plan, caption_len, hidden, vec_rep, heads, [(attn_set, ["qk", "vc", "oo"])]
    )
    whole_qk, whole_vc, whole_oo = wholes

    def exchange(values):
        own, near, others = values
        got = mp_swap(others, 2)
        for distance in plan.distances[2:]:
            got = mp_swap(got, distance)
        passed = mp_swap(jnp.stack([near, got[1]]), 1)
        return own, passed[0], jnp.stack([got[0], passed[1]])

    far_down, cross, up_got = hold(far_down, cross, up_got)
    up = jnp.concatenate([up, up_got])
    down, down_got = before_last(jnp.concatenate([third[:, ffn_rows:], far_down]), back)
    queries = exchange(cross)
    (queries,) = hold(queries)
    contexts = cross_attend(plan, keys, queries, kv_all)
    contexts, down_got = hold(contexts, down_got)
    down = jnp.concatenate([down, down_got])
    half = up.shape[0] // 2
    up_last, down_last = swap(up[:half], forth[-1]), swap(down[:half], back[-1])
    contexts = exchange(contexts)
    contexts, down, up, up_last, down_last = hold(contexts, down, up, up_last, down_last)
    up_last = jnp.concatenate([up_last, swap(up[half:], forth[-1])])
    down_last = jnp.concatenate([down_last, swap(down[half:], back[-1])])
    up_core, down_core = send_cores((up, down))
    z_second, kept, given = cross_output(plan, vec_rep, z_first, contexts, whole_oo)
    kept, given = hold(kept, given)
    ffn_got = mp_swap(given, 1)
    up_last, down_last, up_core, down_core, ffn_got, kept = hold(
        up_last, down_last, up_core, down_core, ffn_got, kept
    )
    up_last_core, down_last_core = send_cores((up_last, down_last))
    up_last_core, down_last_core, ffn_got, kept = hold(
        up_last_core, down_last_core, ffn_got, kept
    )
    ffn_set = Weights(
        plan,
        as_trees(
            plan,
            (
                (up, up_last, up_core, up_last_core),
                (down, down_last, down_core, down_last_core),
            ),
        ),
        {"up": [Part("a", 0, ffn_rows, 0)], "down": [Part("b", 0, ffn_rows, 0)]},
    )
    layer, kept_back, given_back, third_sums, bias_sums, ffn_halves = feed_forward(
        plan,
        vec_rep,
        heads,
        kept,
        ffn_got,
        cotangent,
        [(ffn_set, ["up", "down"])],
        ffn_gradients,
    )
    cores = ("core", "core")
    ffn_state = ffn_halves["a"], ffn_halves["b"]
    got_back = mp_swap(given_back, 1)
    got = shrink_send(ffn_state, cores)
    got_back, got, kept_back, layer = hold(got_back, got, kept_back, layer)
    layer_near = mp_swap(layer, 1)
    ffn_state = shrink_add(ffn_state, got)
    for k in range(plan.bits - 1, 1, -1):
        ffn_state = shrink_add(ffn_state, shrink_send(ffn_state, (forth[k], back[k])))
    got = shrink_send(ffn_state, (forth[1], back[1]))
    cross_back, branch, caption_back, cross_sums, context_back = cross_output_backward(
        plan, vec_rep, z_second, kept_back, got_back, whole_oo
    )
    (context_back,) = hold(context_back)
    context_back = exchange(context_back)
    context_back, layer_near = hold(context_back, layer_near)
    layer_two = jnp.stack([layer, layer_near])
    layer_across = mp_middle(plan, layer_two)
    kv_back, value_sum, query_back = cross_attend_backward(
        plan, keys, queries, context_back, kv_all
    )
    query_back, got = hold(query_back, got)
    ffn_state = shrink_add(ffn_state, got)
    got = shrink_send(ffn_state, (forth[0], back[0]))
    query_back = exchange(query_back)
    query_back, got, layer_across = hold(query_back, got, layer_across)
    ffn_state = join_trees(shrink_add(ffn_state, got))
    for distance in plan.distances[:1:-1]:
        ffn_state = mp_halve(ffn_state, distance)
    first_back, first_sums = cross_input_backward(
        plan, vec_rep, z_first, cross_back, caption_back, query_back, whole_vc
    )
    out_halves = output_gradient(plan, first_back, branch, context_all, contexts, out_gradients)
    ffn_state, first_back, out_halves = hold(ffn_state, first_back, out_halves)
    middle = ffn_rows if ffn_state[1].shape[0] == 2 else 0
    ffn_got_up = mp_swap(ffn_state[1][:, :middle], 2)
    layer_far = mp_outward(plan, layer_across)
    out_state = out_halves["a"], out_halves["b"]
    out_got = shrink_send(out_state, cores)
    token_back, vectors, maps_back, value_maps = self_backward(
        plan,
        caption_len,
        (vec_rep, first_back, qk_all, v_all),
        (first_sums, cross_sums, third_sums, bias_sums, value_sum),
        wholes,
    )
    token_back, maps_back, vectors, ffn_got_up, out_got = hold(
        token_back, maps_back, vectors, ffn_got_up, out_got
    )
    near = mp_swap(token_back, 1)
    ffn_got_down = mp_swap(ffn_state[1][:, middle:], 2)
    out_state = shrink_add(out_state, out_got)
    for k in range(plan.bits - 1, 1, -1):
        out_state = shrink_add(out_state, shrink_send(out_state, (forth[k], back[k])))
    out_got = shrink_send(out_state, (forth[1], back[1]))
    attn_halves = self_gradient(
        plan,
        hidden,
        (vec_rep, z_first, maps_back, value_maps, *query_back),
        attn_gradients,
    )
    near, layer_far, vectors, attn_halves, kv_back, ffn_got_down, out_got = hold(
        near, layer_far, vectors, attn_halves, kv_back, ffn_got_down, out_got
    )
    attn_state = attn_halves["a"], attn_halves["b"]
    attn_got = shrink_send(attn_state, cores)
    vector_got = swap(vectors, "core")
    tokens_two = jnp.stack([token_back, near])
    across = mp_middle(plan, tokens_two)
    out_state = shrink_add(out_state, out_got)
    out_got = shrink_send(out_state, (forth[0], back[0]))
    attn_got, vector_got, kv_back, out_got = hold(attn_got, vector_got, kv_back, out_got)
    vectors = vectors + vector_got
    attn_state = shrink_add(attn_state, attn_got)
    for k in range(plan.bits - 1, 1, -1):
        attn_state = shrink_add(attn_state, shrink_send(attn_state, (forth[k], back[k])))
    attn_got = shrink_send(attn_state, (forth[1], back[1]))
    out_state = join_trees(shrink_add(out_state, out_got))
    for distance in plan.distances[:1:-1]:
        out_state = mp_halve(out_state, distance)
    out_got = mp_swap(out_state[1], 2)
    vector_got = mp_swap(vectors, 1)
    kv_grad = image_gradient(plan, images, kv_back)
    attn_got, kv_grad, vector_got, across, out_got = hold(
        attn_got, kv_grad, vector_got, across, out_got
    )
    kv_total = lax.psum_scatter(
        kv_grad, forth + ("core",), scatter_dimension=0, tiled=True
    ).astype(F32)
    vectors = vectors + vector_got
    vector_got = mp_swap(vectors, 2)
    tokens_far = mp_outward(plan, across)
    attn_state = shrink_add(attn_state, attn_got)
    attn_got = shrink_send(attn_state, (forth[0], back[0]))
    layer_out = place_layer(plan, layer_two, layer_across, layer_far)

    def add_halves(state, got):
        half = got.shape[0] // 2
        return add_low(state[0][:half], got[:half]), add_low(state[0][half:], got[half:])

    ffn_got = jnp.concatenate([ffn_got_up, ffn_got_down], axis=1)
    mine, theirs = mp_last(add_halves(ffn_state, ffn_got))
    out_state = add_halves(out_state, out_got)
    attn_got, vector_got, mine, theirs, tokens_far = hold(
        attn_got, vector_got, mine, theirs, tokens_far
    )
    vectors = vectors + vector_got
    for distance in plan.distances[2:]:
        vectors = vectors + mp_swap(vectors, distance)
    for axis in forth[1:]:
        vectors = vectors + swap(vectors, axis)
    attn_pieces = mp_scatter(plan, join_trees(shrink_add(attn_state, attn_got)))
    vector_got = swap(vectors, forth[0])
    out_total = sum(mp_last(out_state))
    attn_pieces, vector_got = hold(attn_pieces, vector_got)
    vectors = vectors + vector_got
    attn_total = sum(p.astype(F32) for p in attn_pieces)
    grad_hidden = place_gradient(plan, tokens_two, across, tokens_far)
    reduced_rep = vectors[:12]
    head_width = query_value_bias_rows.shape[1]
    bias_width = bias_up.shape[1]
    reduced_head = lax.dynamic_slice_in_dim(vectors[12:16], me * head_width, head_width, 1)
    reduced_bias = lax.dynamic_slice_in_dim(
        vectors[16:].reshape(2, -1), me * bias_width, bias_width, 1
    )

    def split_columns(values):
        width = values.shape[1] // 2
        return jnp.stack([values[:, :width], values[:, width:]])

    both = jnp.stack([jnp.where(low, mine, theirs), jnp.where(low, theirs, mine)])
    reduced_up, reduced_down = both[:, :ffn_rows], both[:, ffn_rows:].transpose(0, 2, 1)
    reduced_out = split_columns(out_total).transpose(0, 2, 1)
    reduced_in = jnp.concatenate(
        [split_columns(attn_total[:attn_rows]), split_columns(attn_total[attn_rows:])]
    )
    reduced_kv = split_columns(kv_total)
    rates = (
        2.0 / math.sqrt(D),
        2.0 / math.sqrt(max(D // 8, 1)),
        2.0 / math.sqrt(E),
        2.0 / math.sqrt(D),
        2.0 / math.sqrt(F),
        0.3,
        0.3,
        0.3,
    )
    weights = (
        attn_in,
        attn_out,
        cross_key_value_maps,
        ffn_up,
        ffn_down,
        vec_rep,
        query_value_bias_rows,
        bias_up,
    )
    firsts = (
        attn_in_first,
        attn_out_first,
        cross_kv_first,
        ffn_up_first,
        ffn_down_first,
        vec_rep_first,
        vec_head_first,
        bias_up_first,
    )
    seconds = (
        attn_in_second,
        attn_out_second,
        cross_kv_second,
        ffn_up_second,
        ffn_down_second,
        vec_rep_second,
        vec_head_second,
        bias_up_second,
    )
    reduced = (
        reduced_in,
        reduced_out,
        reduced_kv,
        reduced_up,
        reduced_down,
        reduced_rep,
        reduced_head,
        reduced_bias,
    )
    results = []
    for weight, first, second, grad, rate in zip(weights, firsts, seconds, reduced, rates):
        results.extend(adam_update(weight, first, second, grad, rate))
    return (layer_out, grad_hidden, *results)


def solution(mesh):
    dp, mp = mesh.devices.shape
    bits = (dp // 2).bit_length() - 1
    names = tuple(f"b{k}" for k in range(bits)) + ("core",)
    fine = Mesh(mesh.devices.reshape((2,) * (bits + 1) + (mp,)), names + ("mp",))
    split = P(names)
    inward = P(None, names, "mp")
    outward = P(None, "mp", names)
    head = P(None, "mp")
    stored = (inward,) * 3 + (outward,) * 3 + (inward,) * 6 + (outward,) * 3 + (P(),) * 3 + (head,) * 6
    return jax.shard_map(
        functools.partial(local, bits),
        mesh=fine,
        in_specs=(split,) * 4 + stored,
        out_specs=(split,) * 2 + stored,
        check_vma=False,
    )
```

```python
import functools
import math

import jax
import jax.numpy as jnp
from jax import lax
from jax.experimental import pallas as pl
from jax.experimental.layout import Layout, with_layout_constraint
from jax.experimental.pallas import tpu as pltpu
from jax.sharding import Mesh
from jax.sharding import PartitionSpec as P

D = 768
HEAD_DIM = 64
F = 3072
E = 1408
NQ = 32
STEP_COUNT = 10

NORM_EPS = 1e-06
BETA_ONE = 0.9
BETA_TWO = 0.999
ADAM_EPS = 1e-08
WEIGHT_DECAY = 0.01
MASKED = -1000000000.0

BF = jnp.bfloat16
F32 = jnp.float32
SCALE = HEAD_DIM ** (-0.5)
MIB = 1 << 20


def dot(a, b):
    return lax.dot_general(a, b, (((1,), (0,)), ((), ())), preferred_element_type=F32)


def dot_t(a, b):
    return lax.dot_general(a, b, (((1,), (1,)), ((), ())), preferred_element_type=F32)


def t_dot(a, b):
    return lax.dot_general(a, b, (((0,), (0,)), ((), ())), preferred_element_type=F32)


def swap(values, axis):
    return lax.ppermute(values, axis, [(0, 1), (1, 0)])


def mp_swap(values, distance):
    count = lax.axis_size("mp")
    return lax.ppermute(values, "mp", [(i, i ^ distance) for i in range(count)])


class Plan:
    def __init__(self, bits, mp, items, dp):
        self.bits = bits
        self.mp = mp
        self.dp = dp
        self.items = items
        self.rows = items * 2 * NQ
        self.half = items * NQ
        self.width = D // mp
        self.forth = tuple(f"b{k}" for k in range(bits))
        self.back = self.forth[::-1]
        self.distances = [1 << k for k in range(mp.bit_length() - 1)]

    def bit(self, axis):
        return 1 if axis == "core" else 2 << (self.bits - 1 - int(axis[1:]))

    def masks(self, order):
        found = [0]
        for axis in order + ("core",):
            found = found + [m | self.bit(axis) for m in found]
        return found

    def dp_index(self):
        place = lax.axis_index("core")
        for axis in self.forth:
            place = place + self.bit(axis) * lax.axis_index(axis)
        return place


class Part:
    def __init__(self, tree, low, count, place):
        self.tree, self.low, self.count, self.place = tree, low, count, place


def hold(*values):
    return lax.optimization_barrier(values)


def mp_double(values, distance):
    return jnp.concatenate([values, mp_swap(values, distance)])


def mp_direct(plan, own, sent):
    return [own] + [mp_swap(sent(j), j) for j in range(1, plan.mp)]


def two_trees(pieces, rows):
    return (
        jnp.concatenate([p[None, :rows] for p in pieces]),
        jnp.concatenate([p[None, rows:] for p in pieces]),
    )


def send_pair(plan, pair, k):
    return swap(pair[0], plan.forth[k]), swap(pair[1], plan.back[k])


def send_cores(pair):
    return tuple(swap(v, "core") for v in pair)


def join_pair(pair, got):
    return tuple(jnp.concatenate([v, g]) for v, g in zip(pair, got))


def as_quarters(pair, got, cores, got_cores):
    return tuple(zip(pair, got, cores, got_cores))


def as_trees(plan, cores):
    return {"a": (cores[0], plan.forth), "b": (cores[1], plan.back)}


def line_pairs(plan):
    return [(1, 2), (2, 1)], [(0, 1), (3, 2)], [(1, 0), (2, 3)]


def mp_middle(plan, values):
    if plan.mp != 4:
        return mp_swap(values, 2)
    return lax.ppermute(values, "mp", line_pairs(plan)[0])


def mp_outward(plan, got):
    if plan.mp != 4:
        return got
    return lax.ppermute(got, "mp", line_pairs(plan)[2])


def from_line(plan, across, far, j):
    if plan.mp != 4:
        return across[j - 2]
    me = lax.axis_index("mp")
    return jnp.where((me == 0) | (me == 3), far[j - 2], across[3 - j])


def mp_inward(plan, state):
    kept, sent = state
    if plan.mp != 4:
        return state
    got = lax.ppermute(sent, "mp", line_pairs(plan)[1])
    return kept, add_low(sent, got[::-1])


def mp_across(plan, state):
    kept, sent = state
    if plan.mp != 4:
        return mp_halve(state, 2)
    got = lax.ppermute(sent, "mp", line_pairs(plan)[0])
    return add_low(kept[:1], got[1:]), add_low(kept[1:], got[:1])


def natural_tree(plan, halves, order):
    values = jnp.concatenate(halves)
    values = values.reshape((plan.dp, values.shape[0] // plan.dp) + values.shape[1:])
    back = [0] * plan.dp
    for k, mask in enumerate(plan.masks(order)):
        back[mask] = k
    places = jnp.take(jnp.array(back), jnp.arange(plan.dp) ^ plan.dp_index())
    return jnp.take(values, places, axis=0)


def assemble(plan, trees, parts):
    found = []
    for part in parts:
        halves, order = trees[part.tree]
        natural = natural_tree(plan, halves, order)
        found.append(natural[:, :, part.low : part.low + part.count])
    whole = jnp.concatenate(found, axis=2).transpose(1, 0, 2, 3)
    return whole.reshape(whole.shape[0], -1, whole.shape[-1])


def by_distance(plan, matrices, segments, order):
    places = jnp.array(plan.masks(order)) ^ plan.dp_index()
    found = []
    for name, part in segments:
        blocks = matrices[name]
        blocks = blocks.reshape(blocks.shape[0], plan.dp, -1, blocks.shape[-1])
        blocks = jnp.take(blocks, places, axis=1).transpose(1, 0, 2, 3)
        found.append(blocks[:, :, part.place : part.place + part.count])
    whole = jnp.concatenate(found, axis=2)
    whole = whole.reshape((-1,) + whole.shape[2:])
    return whole[: whole.shape[0] // 2], whole[whole.shape[0] // 2 :]


def add_low(first, second):
    return (first.astype(F32) + second.astype(F32)).astype(BF)


def shrink_send(halves, axes):
    return tuple(swap(sent, axis) for (_, sent), axis in zip(halves, axes))


def shrink_add(halves, found):
    sums = []
    for (kept, _), got in zip(halves, found):
        half = got.shape[0] // 2
        sums.append((add_low(kept[:half], got[:half]), add_low(kept[half:], got[half:])))
    return tuple(sums)


def join_trees(halves):
    return tuple(jnp.concatenate([h[k] for h in halves], axis=1) for k in range(2))


def mp_halve(state, distance):
    kept, sent = state
    got = mp_swap(sent, distance)
    half = got.shape[0] // 2
    return add_low(kept[:half], got[:half]), add_low(kept[half:], got[half:])


def mp_scatter(plan, state):
    kept, sent = state
    pieces = [kept[0]]
    for j in range(1, plan.mp):
        values = kept if j < plan.mp // 2 else sent
        pieces.append(mp_swap(values[j % (plan.mp // 2)], j))
    return pieces


def mp_last(state):
    kept, sent = state
    return kept[0].astype(F32), mp_swap(sent[0], 1).astype(F32)


def norm_parts(values):
    center = values - jnp.mean(values, axis=-1, keepdims=True)
    spread = jnp.mean(center * center, axis=-1, keepdims=True)
    inverse = lax.rsqrt(spread + NORM_EPS)
    return center * inverse, inverse


def norm_backward(grad_out, normed, inverse, gain):
    scaled = grad_out * gain
    inner = (
        scaled
        - jnp.mean(scaled, axis=-1, keepdims=True)
        - normed * jnp.mean(scaled * normed, axis=-1, keepdims=True)
    )
    return inner * inverse


def column_sum(values):
    return jnp.sum(values.astype(F32), axis=0, keepdims=True)


def halves_of(values, items):
    split = values.reshape(items, 2 * NQ, values.shape[-1])
    parts = split[:, :NQ], split[:, NQ:]
    return tuple(p.reshape(items * NQ, values.shape[-1]) for p in parts)


def join_halves(query, caption, items):
    width = query.shape[-1]
    parts = [v.reshape(items, NQ, width) for v in (query, caption)]
    return jnp.concatenate(parts, axis=1).reshape(items * 2 * NQ, width)


def wide(first, second):
    return jnp.concatenate([first, second], axis=1)


def after(values, width):
    return jnp.concatenate([jnp.zeros_like(values), values], axis=1)


def before(values, width):
    return jnp.concatenate([values, jnp.zeros_like(values)], axis=1)


def head_lanes(width):
    lane = lax.broadcasted_iota(jnp.int32, (1, width), 1)
    return [lane // HEAD_DIM == h for h in range(width // HEAD_DIM)]


def only(values, lanes):
    return jnp.where(lanes, values, jnp.zeros_like(values))


def softmax(scores):
    expo = jnp.exp(scores - jnp.max(scores, axis=-1, keepdims=True))
    return expo * (1.0 / jnp.sum(expo, axis=-1, keepdims=True))


def fetch(plan, refs, parts, trees, target, sem):
    if trees is None:
        pltpu.make_async_copy(refs[0], target, sem).start()
        return
    place = plan.dp_index()
    block = sum(p.count for p in parts)
    for part in parts:
        found, order = trees[part.tree]
        for k, mask in enumerate(plan.masks(order)):
            quarter, index = divmod(k, plan.dp // len(found))
            begin = pl.multiple_of((place ^ mask) * block + part.place, 16)
            pieces = refs[found[quarter]].at[pl.ds(index * plan.mp, plan.mp)]
            pltpu.make_async_copy(
                pieces.at[:, pl.ds(part.low, part.count), :],
                target.at[:, pl.ds(begin, part.count), :],
                sem,
            ).start()


def fetch_whole(matrix, target, sem):
    pltpu.make_async_copy(matrix, target, sem).start()


def settle(target, sem):
    pltpu.make_async_copy(target, target, sem).wait()


def spread(plan, source, parts, outs, sem):
    if parts is None:
        pltpu.make_async_copy(source, outs, sem).start()
        return
    place = plan.dp_index()
    block = sum(p.count for p in parts)
    for part in parts:
        halves, order = outs[part.tree]
        for k, mask in enumerate(plan.masks(order)):
            half, index = divmod(k, plan.dp // 2)
            begin = pl.multiple_of((place ^ mask) * block + part.place, 16)
            pieces = halves[half].at[pl.ds(index * plan.mp, plan.mp)]
            pltpu.make_async_copy(
                source.at[:, pl.ds(begin, part.count), :],
                pieces.at[:, pl.ds(part.low, part.count), :],
                sem,
            ).start()


class Weights:
    def __init__(self, plan, trees, matrices):
        self.plan, self.matrices = plan, matrices
        self.direct = all(p.count % 16 == 0 for parts in matrices.values() for p in parts)
        if self.direct:
            self.trees = trees
        else:
            self.whole = {n: assemble(plan, trees, parts) for n, parts in matrices.items()}

    def operands(self, names):
        arrays, found = [], {}
        if not self.direct:
            for name in names:
                found[name] = (len(arrays), self.matrices[name], None)
                arrays.append(self.whole[name])
            return arrays, found
        seen = {}
        for name in names:
            for part in self.matrices[name]:
                if part.tree not in seen:
                    halves, order = self.trees[part.tree]
                    seen[part.tree] = (range(len(arrays), len(arrays) + len(halves)), order)
                    arrays.extend(halves)
            found[name] = (0, self.matrices[name], seen)
        return arrays, found


def gather_operands(sets):
    arrays, starts = [], {}
    for weights, names in sets:
        more, found = weights.operands(names)
        base = len(arrays)
        for name, (place, parts, trees) in found.items():
            starts[name] = functools.partial(
                lambda refs, target, sem, base, place, parts, trees, plan: fetch(
                    plan, refs[base + place :], parts, trees, target, sem
                )
                if trees is None
                else fetch(plan, refs[base:], parts, trees, target, sem),
                base=base,
                place=place,
                parts=parts,
                trees=trees,
                plan=weights.plan,
            )
        arrays.extend(more)
    return arrays, starts


class Gradients:
    def __init__(self, plan, trees, matrices, over):
        self.plan, self.trees, self.matrices, self.over = plan, trees, matrices, over
        self.direct = all(p.count % 16 == 0 for parts, _ in matrices.values() for p in parts)

    def shapes(self):
        found = []
        if self.direct:
            for _, rows, columns in self.trees.values():
                shape = (self.plan.dp // 2 * self.over, rows, columns)
                found += [jax.ShapeDtypeStruct(shape, BF)] * 2
            return found
        for parts, rows in self.matrices.values():
            columns = self.trees[parts[0].tree][2]
            found.append(jax.ShapeDtypeStruct((self.over, rows, columns), BF))
        return found

    def write(self, name, source, refs, sem):
        parts = self.matrices[name][0]
        if self.direct:
            outs = {
                tree: (refs[2 * k : 2 * k + 2], order)
                for k, (tree, (order, _, _)) in enumerate(self.trees.items())
            }
            spread(self.plan, source, parts, outs, sem)
        else:
            spread(self.plan, source, None, refs[list(self.matrices).index(name)], sem)

    def halves(self, arrays):
        if self.direct:
            return {t: tuple(arrays[2 * k : 2 * k + 2]) for k, t in enumerate(self.trees)}
        named = dict(zip(self.matrices, arrays))
        found = {}
        for tree, (order, _, _) in self.trees.items():
            segments = [
                (name, part)
                for name, (parts, _) in self.matrices.items()
                for part in parts
                if part.tree == tree
            ]
            segments.sort(key=lambda s: s[1].low)
            found[tree] = by_distance(self.plan, named, segments, order)
        return found


def call(kernel, ins, places, outs, out_places, scratch, limit):
    return pl.pallas_call(
        kernel,
        out_shape=outs,
        in_specs=[pl.BlockSpec(memory_space=p) for p in places],
        out_specs=[pl.BlockSpec(memory_space=p) for p in out_places],
        scratch_shapes=scratch,
        compiler_params=pltpu.CompilerParams(vmem_limit_bytes=limit * MIB),
        cost_estimate=pl.CostEstimate(flops=1000, bytes_accessed=1000, transcendentals=0),
    )(*ins)


ANY, HBM, VMEM, SMEM = pl.ANY, pltpu.HBM, pltpu.VMEM, pltpu.SMEM
DMA = pltpu.SemaphoreType.DMA


def self_mask(plan, lengths, me):
    count = plan.rows
    row = lax.broadcasted_iota(jnp.int32, (count, count), 0)
    col = lax.broadcasted_iota(jnp.int32, (count, count), 1)
    span = 2 * NQ
    limit = jnp.zeros((count, count), jnp.int32)
    for i in range(plan.items):
        limit = jnp.where(col // span == i, lengths[me * plan.items + i], limit)
    inside = col % span
    valid = (row // span == col // span) & ((inside < NQ) | (inside - NQ < limit))
    return jnp.where(valid, 0.0, MASKED).astype(F32)


def load_tokens(plan, hidden, target, sem):
    me = lax.axis_index("mp")
    return pltpu.make_async_copy(hidden.at[pl.ds(me * plan.items, plan.items)], target, sem)


def distance_shapes(plan):
    both = jax.ShapeDtypeStruct((plan.half, 2 * plan.width), BF)
    return [jax.ShapeDtypeStruct((plan.half, plan.width), BF), both, both]


def put_distance(refs, j, values):
    width = values.shape[1]
    if j == 0:
        refs[0][...] = values
    elif j == 1:
        refs[1][...] = before(values, width)
    else:
        refs[2][:, (j - 2) * width : (j - 1) * width] = values


def get_distance(refs, j, span=slice(None)):
    width = refs[0].shape[1]
    if j == 0:
        return refs[0][span, :]
    if j == 2:
        return refs[2][span, :width]
    return refs[1][span, :width] if j == 1 else refs[1][span, width:]


def self_forward(plan, lengths, hidden, vec, heads, sets):
    arrays, starts = gather_operands(sets)
    count = len(arrays)
    mp, rows, half, width, items = plan.mp, plan.rows, plan.half, plan.width, plan.items

    def kernel(lengths, hidden, vec, heads, *rest):
        refs = rest[:count]
        qk_out, v_out, context_out, z_out = rest[count : count + 4]
        cross = rest[count + 4 : count + 7]
        wholes = rest[count + 7 : count + 10]
        tokens, w_qk, w_vc, w_oo, sems = rest[count + 10 :]
        me = lax.axis_index("mp")
        loaded = load_tokens(plan, hidden, tokens, sems.at[0])
        loaded.start()
        starts["qk"](refs, w_qk, sems.at[1])
        starts["vc"](refs, w_vc, sems.at[2])
        starts["oo"](refs, w_oo, sems.at[3])
        mask = self_mask(plan, lengths, me)
        lanes = head_lanes(width)
        loaded.wait()
        x = tokens[...].reshape(rows, D)
        total = x.astype(F32) + vec[0:1, :]
        kept = []
        for k, matrix in enumerate((w_qk, w_vc, w_oo)):
            settle(matrix, sems.at[1 + k])
            kept.append(pltpu.make_async_copy(matrix, wholes[k], sems.at[4 + k]))
            kept[-1].start()
        for j in range(mp):
            both = (dot(x, w_qk[j]) + heads[j, 0:1, :]).astype(BF)
            qk_out[j] = both
            q, k = both[:, :width], both[:, width:]
            v = (dot(x, w_vc[j]) + heads[j, 1:2, :]).astype(BF)[:, :width]
            v_out[j] = v
            context = jnp.zeros((rows, width), F32)
            for lane in lanes:
                probs = softmax(dot_t(only(q, lane), k) * SCALE + mask)
                context = context + only(dot(probs.astype(BF), v), lane)
            context = context.astype(BF)
            context_out[j] = context
            total = total + dot_t(before(context, width), w_oo[j])
        z_out[...] = total
        normed, _ = norm_parts(total)
        u = halves_of(normed * vec[4:5, :] + vec[5:6, :], items)[0].astype(BF)
        for j in range(mp):
            maps = (dot(u, w_vc[j]) + heads[j, 1:2, :]).astype(BF)
            put_distance(cross, j, maps[:, width:])
        for copy in kept:
            copy.wait()

    whole = jax.ShapeDtypeStruct((mp, D, 2 * width), BF)
    outs = [
        jax.ShapeDtypeStruct((mp, rows, 2 * width), BF),
        jax.ShapeDtypeStruct((mp, rows, width), BF),
        jax.ShapeDtypeStruct((mp, rows, width), BF),
        jax.ShapeDtypeStruct((rows, D), F32),
        *distance_shapes(plan),
        whole,
        whole,
        whole,
    ]
    found = call(
        kernel,
        (lengths, hidden, vec, heads, *arrays),
        [SMEM, HBM, VMEM, VMEM] + [ANY] * count,
        outs,
        [VMEM] * 7 + [HBM] * 3,
        [
            pltpu.VMEM((items, 2 * NQ, D), BF),
            *[pltpu.VMEM((mp, D, 2 * width), BF)] * 3,
            DMA((7,)),
        ],
        28,
    )
    return (*found[:4], found[4:7], found[7:])


def load_images(images, held, sems):
    count = images.shape[0]
    cut = -(-count // 4)
    found = []
    for k in range(0, count, cut):
        span = pl.ds(k, min(cut, count - k))
        found.append(pltpu.make_async_copy(images.at[span], held.at[span], sems.at[k // cut]))
        found[-1].start()
    return found, cut


def image_maps(plan, images, bias, maps):
    items, keys, features = images.shape
    width = plan.width
    padded = -(-keys // 128) * 128

    def kernel(images, bias, maps, out, held, w_kv, sems, w_sem):
        weights = pltpu.make_async_copy(maps, w_kv, w_sem.at[0])
        weights.start()
        loaded, cut = load_images(images, held, sems)
        weights.wait()
        for n, copy in enumerate(loaded):
            copy.wait()

            def step(i, carry):
                both = (dot(held[i], w_kv[...]) + bias[2:3, :]).astype(BF)
                out[i, 0:keys, :] = both
                out[i, keys:padded, :] = jnp.zeros((padded - keys, 2 * width), BF)
                return carry

            lax.fori_loop(n * cut, min(items, (n + 1) * cut), step, 0)

    return call(
        kernel,
        (images, bias, maps),
        [ANY, VMEM, ANY],
        [jax.ShapeDtypeStruct((items, padded, 2 * width), BF)],
        [VMEM],
        [
            pltpu.VMEM((items, keys, features), BF),
            pltpu.VMEM((features, 2 * width), BF),
            DMA((4,)),
            DMA((1,)),
        ],
        28,
    )[0]


def key_mask(plan, keys, padded):
    lane = lax.broadcasted_iota(jnp.int32, (1, padded), 1)
    return jnp.where(lane < keys, 0.0, MASKED).astype(F32)


def spread_heads(values, lanes):
    return jnp.concatenate([only(values, lane) for lane in lanes], axis=0)


def gather_heads(values, lanes):
    total = None
    for h, lane in enumerate(lanes):
        part = only(values[h * NQ : (h + 1) * NQ], lane)
        total = part if total is None else total + part
    return total


def cross_attend(plan, keys, queries, kv):
    mp, half, width, items = plan.mp, plan.half, plan.width, plan.items
    padded = kv.shape[1]

    def kernel(*refs):
        queries, kv, contexts = refs[:3], refs[3], refs[4:]
        me = lax.axis_index("mp")
        lanes = head_lanes(width)
        mask = key_mask(plan, keys, padded)
        for j in range(mp):
            rows = []
            for i in range(items):
                q = spread_heads(get_distance(queries, j, slice(i * NQ, (i + 1) * NQ)), lanes)
                both = kv[(me ^ j) * items + i]
                probs = softmax(dot_t(q, both[:, :width]) * SCALE + mask)
                rows.append(gather_heads(dot(probs.astype(BF), both[:, width:]), lanes))
            put_distance(contexts, j, jnp.concatenate(rows, axis=0).astype(BF))

    return call(
        kernel,
        (*queries, kv),
        [VMEM] * 4,
        distance_shapes(plan),
        [VMEM] * 3,
        [],
        24,
    )


def cross_output(plan, vec, z_first, contexts, whole_oo):
    mp, half, width, items = plan.mp, plan.half, plan.width, plan.items

    def kernel(vec, z_first, *rest):
        contexts, whole_oo = rest[:3], rest[3]
        z_out, kept, given, w_oo, sems = rest[4:]
        me = lax.axis_index("mp")
        fetch_whole(whole_oo, w_oo, sems.at[0])
        normed, _ = norm_parts(z_first[...])
        query, caption = halves_of(normed * vec[4:5, :] + vec[5:6, :], items)
        total = query + vec[1:2, :]
        settle(w_oo, sems.at[0])
        for j in range(mp):
            total = total + dot_t(after(get_distance(contexts, j), width), w_oo[j])
        z_out[...] = total
        normed, _ = norm_parts(total)
        second = normed * vec[6:7, :] + vec[7:8, :]
        low = (me & 1) == 0
        kept[...] = jnp.where(low, second, caption)
        given[...] = jnp.where(low, caption, second).astype(BF)

    return call(
        kernel,
        (vec, z_first, *contexts, whole_oo),
        [VMEM] * 5 + [HBM],
        [
            jax.ShapeDtypeStruct((half, D), F32),
            jax.ShapeDtypeStruct((half, D), F32),
            jax.ShapeDtypeStruct((half, D), BF),
        ],
        [VMEM] * 3,
        [pltpu.VMEM((mp, D, 2 * width), BF), DMA((1,))],
        16,
    )


def feed_forward(plan, vec, heads, kept, got, cotangent, sets, gradients):
    arrays, starts = gather_operands(sets)
    count = len(arrays)
    mp, half, items = plan.mp, plan.half, plan.items
    hidden_width = F // mp
    shapes = gradients.shapes()

    def kernel(vec, heads, kept, got, cotangent, *rest):
        refs, rest = rest[:count], rest[count:]
        layer, kept_back, given_back, sums, bias_sums = rest[:5]
        grad_out = rest[5 : 5 + len(shapes)]
        top, w_up, w_down, slope, act, up_grad, down_grad, w_sems, sems = rest[5 + len(shapes) :]
        me = lax.axis_index("mp")
        group = me & 1
        starts["up"](refs, w_up, w_sems.at[0])
        starts["down"](refs, w_down, w_sems.at[1])
        tops = []
        for s in range(2):
            first = (me ^ s) * items
            tops.append(
                pltpu.make_async_copy(
                    cotangent.at[
                        pl.ds(first, items), pl.ds(pl.multiple_of(group * NQ, NQ), NQ), :
                    ],
                    top.at[s],
                    sems.at[2 + s],
                )
            )
            tops[-1].start()
        x = jnp.concatenate([kept[...], got[...].astype(F32)], axis=0)
        low = x.astype(BF)
        low_t = low.T
        total = x + vec[pl.ds(2 + group, 1), :]
        settle(w_up, w_sems.at[0])
        for z in range(mp):
            bias = wide(
                heads[z, pl.ds(3 + 2 * group, 1), :], heads[z, pl.ds(4 + 2 * group, 1), :]
            )
            pre = dot(low, w_up[z]) + bias
            cdf = 0.5 + 0.5 * lax.erf(pre * (0.5**0.5))
            value = (pre * cdf).astype(BF)
            act[z] = value
            slope[z] = cdf + pre * jnp.exp(-0.5 * pre * pre) * (1.0 / math.sqrt(2.0 * math.pi))
            if z == 0:
                settle(w_down, w_sems.at[1])
            total = total + dot_t(value, w_down[z])
        normed, inverse = norm_parts(total)
        gain = vec[pl.ds(8 + 2 * group, 1), :]
        third = normed * gain + vec[pl.ds(9 + 2 * group, 1), :]
        layer[...] = third.astype(BF).reshape(2, items, NQ, D)
        for t in tops:
            t.wait()
        grad = top[...].reshape(2 * half, D).astype(F32)
        back = norm_backward(grad, normed, inverse, gain)
        branch = back.astype(BF)
        sums[0:1, :] = column_sum(branch)
        sums[1:2, :] = column_sum(grad * normed)
        sums[2:3, :] = column_sum(grad)
        branch_t = branch.T
        for z in range(mp):
            down_grad[z] = dot(branch_t, act[z]).astype(BF)
        gradients.write("down", down_grad, grad_out, sems.at[0])
        for z in range(mp):
            pull = (dot(branch, w_down[z]) * slope[z]).astype(BF)
            bias_sums[pl.ds(me ^ z, 1), :] = column_sum(pull)
            up_grad[z] = dot(low_t, pull).astype(BF)
            back = back + dot_t(pull, w_up[z])
        gradients.write("up", up_grad, grad_out, sems.at[1])
        kept_back[...] = back[:half]
        given_back[...] = back[half:].astype(BF)
        settle(down_grad, sems.at[0])
        settle(up_grad, sems.at[1])

    outs = [
        jax.ShapeDtypeStruct((2, items, NQ, D), BF),
        jax.ShapeDtypeStruct((half, D), F32),
        jax.ShapeDtypeStruct((half, D), BF),
        jax.ShapeDtypeStruct((3, D), F32),
        jax.ShapeDtypeStruct((mp, hidden_width), F32),
        *shapes,
    ]
    found = call(
        kernel,
        (vec, heads, kept, got, cotangent, *arrays),
        [VMEM] * 4 + [HBM] + [ANY] * count,
        outs,
        [VMEM] * 5 + [HBM] * len(shapes),
        [
            pltpu.VMEM((2, items, NQ, D), BF),
            pltpu.VMEM((mp, D, hidden_width), BF),
            pltpu.VMEM((mp, D, hidden_width), BF),
            pltpu.VMEM((mp, 2 * half, hidden_width), F32),
            pltpu.VMEM((mp, 2 * half, hidden_width), BF),
            pltpu.VMEM((mp, D, hidden_width), BF),
            pltpu.VMEM((mp, D, hidden_width), BF),
            DMA((2,)),
            DMA((4,)),
        ],
        48,
    )
    return (*found[:5], gradients.halves(found[5:]))


def cross_output_backward(plan, vec, z_second, kept, got, whole_oo):
    mp, half, width = plan.mp, plan.half, plan.width

    def kernel(vec, z_second, kept, got, whole_oo, *rest):
        back_out, branch_out, caption, sums = rest[:4]
        context_back = rest[4:7]
        w_oo, sems = rest[7:]
        low = (lax.axis_index("mp") & 1) == 0
        fetch_whole(whole_oo, w_oo, sems.at[0])
        other = got[...].astype(F32)
        grad = jnp.where(low, kept[...], other)
        caption[...] = jnp.where(low, other, kept[...])
        normed, inverse = norm_parts(z_second[...])
        back = norm_backward(grad, normed, inverse, vec[6:7, :])
        branch = back.astype(BF)
        back_out[...] = back
        branch_out[...] = branch
        sums[0:1, :] = column_sum(branch)
        sums[1:2, :] = column_sum(grad * normed)
        sums[2:3, :] = column_sum(grad)
        settle(w_oo, sems.at[0])
        for j in range(mp):
            put_distance(context_back, j, dot(branch, w_oo[j]).astype(BF)[:, width:])

    found = call(
        kernel,
        (vec, z_second, kept, got, whole_oo),
        [VMEM] * 4 + [HBM],
        [
            jax.ShapeDtypeStruct((half, D), F32),
            jax.ShapeDtypeStruct((half, D), BF),
            jax.ShapeDtypeStruct((half, D), F32),
            jax.ShapeDtypeStruct((3, D), F32),
            *distance_shapes(plan),
        ],
        [VMEM] * 7,
        [pltpu.VMEM((mp, D, 2 * width), BF), DMA((1,))],
        16,
    )
    return (*found[:4], found[4:])


def cross_attend_backward(plan, keys, queries, context_back, kv):
    mp, half, width, items = plan.mp, plan.half, plan.width, plan.items
    padded = kv.shape[1]

    def kernel(*refs):
        queries, context_back, kv = refs[:3], refs[3:6], refs[6]
        kv_back, value_sum, query_back = refs[7], refs[8], refs[9:]
        me = lax.axis_index("mp")
        lanes = head_lanes(width)
        mask = key_mask(plan, keys, padded)
        total = jnp.zeros((1, width), F32)
        for j in range(mp):
            rows = []
            for i in range(items):
                span = slice(i * NQ, (i + 1) * NQ)
                item = (me ^ j) * items + i
                q = spread_heads(get_distance(queries, j, span), lanes)
                g = spread_heads(get_distance(context_back, j, span), lanes)
                both = kv[item]
                k, v = both[:, :width], both[:, width:]
                probs = softmax(dot_t(q, k) * SCALE + mask)
                pulled = dot_t(g, v)
                scored = probs * (pulled - jnp.sum(probs * pulled, axis=-1, keepdims=True))
                scored = scored.astype(BF)
                value_back = t_dot(probs.astype(BF), g).astype(BF)
                key_back = (t_dot(scored, q) * SCALE).astype(BF)
                kv_back[item] = wide(key_back, value_back)
                total = total + column_sum(value_back)
                rows.append(gather_heads(dot(scored, k), lanes) * SCALE)
            put_distance(query_back, j, jnp.concatenate(rows, axis=0).astype(BF))
        value_sum[...] = total

    found = call(
        kernel,
        (*queries, *context_back, kv),
        [VMEM] * 7,
        [
            jax.ShapeDtypeStruct((mp * items, padded, 2 * width), BF),
            jax.ShapeDtypeStruct((1, width), F32),
            *distance_shapes(plan),
        ],
        [VMEM] * 5,
        [],
        28,
    )
    return found[0], found[1], found[2:]


def put_columns(target, row, found, me, width):
    for z in range(len(found)):
        total = jnp.zeros((1, width), F32)
        for j, values in enumerate(found):
            total = jnp.where((me ^ j) == z, values, total)
        target[row : row + 1, z * width : (z + 1) * width] = total


def cross_input_backward(plan, vec, z_first, back, caption, query_back, whole_vc):
    mp, rows, half, width, items = plan.mp, plan.rows, plan.half, plan.width, plan.items

    def kernel(vec, z_first, back, caption, *rest):
        query_back, whole_vc = rest[:3], rest[3]
        first_back, sums, w_vc, sems = rest[4:]
        me = lax.axis_index("mp")
        fetch_whole(whole_vc, w_vc, sems.at[0])
        total = back[...]
        found = [column_sum(get_distance(query_back, j)) for j in range(mp)]
        put_columns(sums, 3, found, me, width)
        settle(w_vc, sems.at[0])
        for j in range(mp):
            total = total + dot_t(after(get_distance(query_back, j), width), w_vc[j])
        first_grad = join_halves(total, caption[...], items)
        normed, inverse = norm_parts(z_first[...])
        first = norm_backward(first_grad, normed, inverse, vec[4:5, :])
        first_back[...] = first
        sums[0:1, :] = column_sum(first_grad * normed)
        sums[1:2, :] = column_sum(first_grad)
        sums[2:3, :] = column_sum(first.astype(BF))

    return call(
        kernel,
        (vec, z_first, back, caption, *query_back, whole_vc),
        [VMEM] * 7 + [HBM],
        [
            jax.ShapeDtypeStruct((rows, D), F32),
            jax.ShapeDtypeStruct((4, D), F32),
        ],
        [VMEM] * 2,
        [pltpu.VMEM((mp, D, 2 * width), BF), DMA((1,))],
        20,
    )


def image_gradient(plan, images, kv_back):
    items, keys, features = images.shape
    width = plan.width
    even = keys // 128 * 128

    def kernel(images, kv_back, out, held, turned, sems):
        loaded, cut = load_images(images, held, sems)
        total = jnp.zeros((2 * width, features), F32)
        for i in range(items):
            turned[i] = kv_back[i, 0:even, :].T
        for i in range(items):
            if i % cut == 0:
                loaded[i // cut].wait()
            total = total + dot(turned[i], held[i, 0:even, :])
        if keys > even:
            left = jnp.concatenate([held[i, even:keys, :] for i in range(items)], axis=0)
            right = jnp.concatenate([kv_back[i, even:keys, :] for i in range(items)], axis=0)
            total = total + t_dot(right, left)
        out[...] = total.astype(BF).T

    return call(
        kernel,
        (images, kv_back),
        [HBM, VMEM],
        [jax.ShapeDtypeStruct((features, 2 * width), BF)],
        [VMEM],
        [
            pltpu.VMEM((items, keys, features), BF),
            pltpu.VMEM((items, 2 * width, even), BF),
            DMA((4,)),
        ],
        40,
    )[0]


def self_backward(plan, lengths, saved, found_sums, wholes):
    mp, rows, width = plan.mp, plan.rows, plan.width
    count = len(saved) + len(found_sums)
    vectors_rows = 16 + 2 * mp * (F // mp // D)

    def kernel(lengths, *rest):
        vec, first_back, qk_all, v_all = rest[:4]
        first_sums, cross_sums, third_sums, bias_sums, value_sum = rest[4:count]
        wholes, rest = rest[count : count + 3], rest[count + 3 :]
        token_back, vectors, maps_back, value_maps = rest[:4]
        w_qk, w_vc, w_oo, w_sems = rest[4:]
        me = lax.axis_index("mp")
        for k, target in enumerate((w_qk, w_vc, w_oo)):
            fetch_whole(wholes[k], target, w_sems.at[k])
        mask = self_mask(plan, lengths, me)
        lanes = head_lanes(width)
        group = me & 1
        vectors[...] = jnp.zeros((vectors_rows, D), F32)
        vectors[0:1, :] = first_sums[2:3, :]
        vectors[1:2, :] = cross_sums[0:1, :]
        vectors[pl.ds(2 + group, 1), :] = third_sums[0:1, :]
        vectors[4:6, :] = first_sums[0:2, :]
        vectors[6:8, :] = cross_sums[1:3, :]
        vectors[pl.ds(8 + 2 * group, 1), :] = third_sums[1:2, :]
        vectors[pl.ds(9 + 2 * group, 1), :] = third_sums[2:3, :]
        vectors[14:15, :] = first_sums[3:4, :]
        for z in range(mp):
            span = slice(z * width, (z + 1) * width)
            vectors[15:16, span] = jnp.where(me == z, value_sum[...], 0.0)
        for g in range(2):
            vectors[16 + g * mp : 16 + (g + 1) * mp, :] = jnp.where(
                group == g, bias_sums[...], 0.0
            )
        total = first_back[...]
        self_branch = total.astype(BF)
        settle(w_oo, w_sems.at[2])
        query_sums, value_sums = [], []
        for z in range(mp):
            pulled = dot(self_branch, w_oo[z]).astype(BF)[:, :width]
            q, k, v = qk_all[z][:, :width], qk_all[z][:, width:], v_all[z]
            query_grad = jnp.zeros((rows, width), F32)
            key_grad = jnp.zeros((rows, width), F32)
            value_grad = jnp.zeros((rows, width), F32)
            for lane in lanes:
                q_h, g_h = only(q, lane), only(pulled, lane)
                probs = softmax(dot_t(q_h, k) * SCALE + mask)
                wanted = dot_t(g_h, v)
                scored = probs * (wanted - jnp.sum(probs * wanted, axis=-1, keepdims=True))
                scored = scored.astype(BF)
                value_grad = value_grad + t_dot(probs.astype(BF), g_h)
                query_grad = query_grad + only(dot(scored, k), lane)
                key_grad = key_grad + t_dot(scored, q_h)
            query_grad = (query_grad * SCALE).astype(BF)
            value_grad = value_grad.astype(BF)
            query_sums.append(column_sum(query_grad))
            value_sums.append(column_sum(value_grad))
            both = wide(query_grad, (key_grad * SCALE).astype(BF))
            maps_back[z] = both
            value_maps[z] = value_grad
            if z == 0:
                settle(w_qk, w_sems.at[0])
                settle(w_vc, w_sems.at[1])
            total = total + dot_t(both, w_qk[z]) + dot_t(before(value_grad, width), w_vc[z])
        put_columns(vectors, 12, query_sums, me, width)
        put_columns(vectors, 13, value_sums, me, width)
        token_back[...] = total.astype(BF)

    return call(
        kernel,
        (lengths, *saved, *found_sums, *wholes),
        [SMEM] + [VMEM] * count + [HBM] * 3,
        [
            jax.ShapeDtypeStruct((rows, D), BF),
            jax.ShapeDtypeStruct((vectors_rows, D), F32),
            jax.ShapeDtypeStruct((mp, rows, 2 * width), BF),
            jax.ShapeDtypeStruct((mp, rows, width), BF),
        ],
        [VMEM] * 4,
        [pltpu.VMEM((mp, D, 2 * width), BF)] * 3 + [DMA((3,))],
        56,
    )


def output_gradient(plan, first_back, branch, context_all, contexts, gradients):
    mp, width = plan.mp, plan.width
    shapes = gradients.shapes()

    def kernel(first_back, branch, context_all, *rest):
        cross_context, grad_out = rest[:3], rest[3 : 3 + len(shapes)]
        g_oo, sems = rest[3 + len(shapes) :]
        branches_t = jnp.concatenate([first_back[...].astype(BF), branch[...]], axis=0).T
        for z in range(mp):
            contexts = jnp.concatenate(
                [
                    before(context_all[z], width),
                    after(get_distance(cross_context, z), width),
                ],
                axis=0,
            )
            g_oo[z] = dot(branches_t, contexts).astype(BF)
        gradients.write("oo", g_oo, grad_out, sems.at[0])
        settle(g_oo, sems.at[0])

    found = call(
        kernel,
        (first_back, branch, context_all, *contexts),
        [VMEM] * 6,
        shapes,
        [HBM] * len(shapes),
        [pltpu.VMEM((mp, D, 2 * width), BF), DMA((1,))],
        24,
    )
    return gradients.halves(found)


def self_gradient(plan, hidden, saved, gradients):
    mp, rows, half, width, items = plan.mp, plan.rows, plan.half, plan.width, plan.items
    shapes = gradients.shapes()
    count = len(saved)

    def kernel(hidden, *rest):
        vec, z_first, maps_back, value_maps = rest[:4]
        query_back = rest[4:7]
        grad_out = rest[count : count + len(shapes)]
        tokens, g_qk, g_vc, sems = rest[count + len(shapes) :]
        loaded = load_tokens(plan, hidden, tokens, sems.at[0])
        loaded.start()
        normed, _ = norm_parts(z_first[...])
        u = halves_of(normed * vec[4:5, :] + vec[5:6, :], items)[0].astype(BF)
        loaded.wait()
        inputs_t = jnp.concatenate([tokens[...].reshape(rows, D), u], axis=0).T
        for z in range(mp):
            g_qk[z] = dot(inputs_t[:, :rows], maps_back[z]).astype(BF)
        gradients.write("qk", g_qk, grad_out, sems.at[1])
        for z in range(mp):
            maps = jnp.concatenate(
                [before(value_maps[z], width), after(get_distance(query_back, z), width)], axis=0
            )
            g_vc[z] = dot(inputs_t, maps).astype(BF)
        gradients.write("vc", g_vc, grad_out, sems.at[2])
        settle(g_qk, sems.at[1])
        settle(g_vc, sems.at[2])

    found = call(
        kernel,
        (hidden, *saved),
        [HBM] + [VMEM] * count,
        shapes,
        [HBM] * len(shapes),
        [pltpu.VMEM((items, 2 * NQ, D), BF)]
        + [pltpu.VMEM((mp, D, 2 * width), BF)] * 2
        + [DMA((3,))],
        24,
    )
    return gradients.halves(found)


def place_layer(plan, two, across, far):
    mp, items = plan.mp, plan.items

    def kernel(two, across, far, out):
        me = lax.axis_index("mp")
        for j in range(mp):
            source = me ^ j
            values = two[j] if j < 2 else from_line(plan, across, far, j)
            for s in range(2):
                out[
                    pl.ds((source ^ s) * items, items),
                    pl.ds(pl.multiple_of((source & 1) * NQ, NQ), NQ),
                    :,
                ] = values[s]

    return call(
        kernel,
        (two, across, far),
        [VMEM] * 3,
        [jax.ShapeDtypeStruct((mp * items, 2 * NQ, D), BF)],
        [VMEM],
        [],
        16,
    )[0]


def place_gradient(plan, own, near, across_own, across_near, far_own, far_near):
    mp, items = plan.mp, plan.items

    def kernel(own, near, across_own, across_near, far_own, far_near, out):
        me = lax.axis_index("mp")
        end = (me == 0) | (me == mp - 1)
        found = [
            own[...],
            near[...],
            jnp.where(end, far_own[...], across_near[...]),
            jnp.where(end, far_near[...], across_own[...]),
        ]
        for j, values in enumerate(found):
            values = values.astype(F32).reshape(items, 2 * NQ, D)
            out[pl.ds((me ^ j) * items, items)] = values

    return call(
        kernel,
        (own, near, across_own, across_near, far_own, far_near),
        [VMEM] * 6,
        [jax.ShapeDtypeStruct((mp * items, 2 * NQ, D), F32)],
        [VMEM],
        [],
        24,
    )[0]


RATES = {
    "attn_in": 2.0 / math.sqrt(D),
    "attn_out": 2.0 / math.sqrt(max(D // 8, 1)),
    "cross_kv": 2.0 / math.sqrt(E),
    "ffn_up": 2.0 / math.sqrt(D),
    "ffn_down": 2.0 / math.sqrt(F),
    "vector": 0.3,
}


def adam_update(weight, first, second, grad, rate):
    first_new = BETA_ONE * first + (1.0 - BETA_ONE) * grad
    second_new = BETA_TWO * second + (1.0 - BETA_TWO) * grad * grad
    first_hat = first_new / (1.0 - BETA_ONE**STEP_COUNT)
    second_hat = second_new / (1.0 - BETA_TWO**STEP_COUNT)
    weight_new = weight - rate * (
        first_hat / (jnp.sqrt(second_hat) + ADAM_EPS) + WEIGHT_DECAY * weight
    )
    return (first_new, second_new, weight_new)


def update_into(held, outs, place, grad, rate):
    found = adam_update(held[0][place], held[1][place], held[2][place], grad, rate)
    for out, values in zip(outs, found):
        out[place] = values


def bring(sources, targets, sems):
    copies = [
        pltpu.make_async_copy(s, t, sems.at[k]) for k, (s, t) in enumerate(zip(sources, targets))
    ]
    for c in copies:
        c.start()
    return copies


def ffn_step(mine, theirs, up, down):
    rows = up[0].shape[1]

    def kernel(*refs):
        mine, theirs, sources, outs = refs[0], refs[1], refs[2:8], refs[8:14]
        held, sems = refs[14:20], refs[20]
        copies = bring(sources, held, sems)
        up, down = held[:3], held[3:]
        low = (lax.axis_index("mp") & 1) == 0
        own, other = mine[...].astype(F32), theirs[...].astype(F32)
        for copy in copies:
            copy.wait()
        for g in range(2):
            grad = jnp.where(low, own, other) if g == 0 else jnp.where(low, other, own)
            update_into(up, outs[:3], g, grad[:rows], RATES["ffn_up"])
            update_into(down, outs[3:], g, grad[rows:], RATES["ffn_down"])

    shapes = [jax.ShapeDtypeStruct(v.shape, F32) for v in up + down]
    return call(
        kernel,
        (mine, theirs, *up, *down),
        [VMEM] * 2 + [HBM] * 6,
        shapes,
        [VMEM] * 6,
        [pltpu.VMEM(v.shape, F32) for v in up + down] + [DMA((6,))],
        32,
    )


def other_steps(plan, pieces, kv_total, attn_in, out_turned, kv):
    width = plan.width
    rows = attn_in[0].shape[1]
    total = sum(p.astype(F32) for p in pieces)

    def columns(values):
        return jnp.stack([values[:, :width], values[:, width:]])

    in_grad = jnp.concatenate([columns(total[:rows]), columns(total[rows : 2 * rows])])
    found = adam_update(*attn_in, in_grad, RATES["attn_in"])
    turned = adam_update(*out_turned, columns(total[2 * rows :]), RATES["attn_out"])
    image = adam_update(*kv, columns(kv_total.astype(F32)), RATES["cross_kv"])
    return (*found, *(v.transpose(0, 2, 1) for v in turned), *image)


def vector_steps(plan, vectors, rep_, head, bias):
    me = lax.axis_index("mp")
    width, hidden_width = head[0].shape[1], bias[0].shape[1]
    head_grad = lax.dynamic_slice_in_dim(vectors[12:16], me * width, width, 1)
    bias_grad = lax.dynamic_slice_in_dim(
        vectors[16:].reshape(2, -1), me * hidden_width, hidden_width, 1
    )
    found = []
    for held, grad in ((rep_, vectors[:12]), (head, head_grad), (bias, bias_grad)):
        found.extend(adam_update(*held, grad, RATES["vector"]))
    return found


def local(
    bits,
    hidden,
    images,
    caption_len,
    cotangent,
    attn_in,
    attn_in_first,
    attn_in_second,
    attn_out,
    attn_out_first,
    attn_out_second,
    cross_key_value_maps,
    cross_kv_first,
    cross_kv_second,
    ffn_up,
    ffn_up_first,
    ffn_up_second,
    ffn_down,
    ffn_down_first,
    ffn_down_second,
    vec_rep,
    vec_rep_first,
    vec_rep_second,
    query_value_bias_rows,
    vec_head_first,
    vec_head_second,
    bias_up,
    bias_up_first,
    bias_up_second,
):
    mp = lax.axis_size("mp")
    me = lax.axis_index("mp")
    plan = Plan(bits, mp, hidden.shape[0] // mp, 2 ** (bits + 1))
    forth, back = plan.forth, plan.back
    low = (me & 1) == 0
    keys = images.shape[1]
    attn_rows, kv_rows, ffn_rows = attn_in.shape[1], cross_key_value_maps.shape[1], ffn_up.shape[1]
    oo_first = attn_rows // 32 * 16 or attn_rows // 2
    oo_second = attn_rows - oo_first

    def side(values):
        return jnp.concatenate([values[0], values[1]], axis=1)

    none = jnp.zeros_like(query_value_bias_rows[0])
    bias_rows = query_value_bias_rows
    packed = jnp.concatenate(
        [
            jnp.concatenate([bias_rows[0], none])[None],
            jnp.concatenate([bias_rows[1], bias_rows[2]])[None],
            jnp.concatenate([none, bias_rows[3]])[None],
            bias_up.reshape(-1, 2 * plan.width),
            jnp.zeros((1, 2 * plan.width), F32),
        ]
    )

    def three(values):
        found = []
        for _ in range(3):
            part = lax.reduce_precision(values, 8, 7)
            found.append(part.astype(BF))
            values = values - part
        return jnp.concatenate(found)

    low_in = attn_in.astype(BF)
    low_oo = side(attn_out.astype(BF).transpose(0, 2, 1))
    low_kv = side(cross_key_value_maps.astype(BF))
    attn_first, attn_second = attn_rows + oo_first, attn_rows + oo_second
    first_shard = jnp.concatenate(
        [
            side(low_in[:2]),
            low_oo[:oo_first],
            side(low_in[2:]),
            low_oo[oo_first:],
            three(packed),
        ]
    )
    group = me & 1
    low_ffn = jnp.concatenate([ffn_up.astype(BF), ffn_down.astype(BF).transpose(0, 2, 1)], axis=1)
    third_own = lax.dynamic_index_in_dim(low_ffn, group, 0, keepdims=False)
    third_other = lax.dynamic_index_in_dim(low_ffn, 1 - group, 0, keepdims=False)
    early, last = range(plan.bits - 1), range(plan.bits - 1, plan.bits)

    wide_columns, hidden_columns = 2 * plan.width, F // mp
    attn_parts = {
        "qk": [Part("a", 0, attn_rows, 0)],
        "vc": [Part("b", 0, attn_rows, 0)],
        "oo": [Part("a", attn_rows, oo_first, 0), Part("b", attn_rows, oo_second, oo_first)],
    }
    attn_gradients = Gradients(
        plan,
        {"a": (forth, attn_rows, wide_columns), "b": (back, attn_rows, wide_columns)},
        {"qk": (attn_parts["qk"], D), "vc": (attn_parts["vc"], D)},
        mp,
    )
    out_gradients = Gradients(
        plan,
        {"a": (forth, oo_first, wide_columns), "b": (back, oo_second, wide_columns)},
        {"oo": ([Part("a", 0, oo_first, 0), Part("b", 0, oo_second, oo_first)], D)},
        mp,
    )
    ffn_gradients = Gradients(
        plan,
        {"a": (forth, ffn_rows, hidden_columns), "b": (back, ffn_rows, hidden_columns)},
        {"up": ([Part("a", 0, ffn_rows, 0)], D), "down": ([Part("b", 0, ffn_rows, 0)], D)},
        mp,
    )

    first = mp_direct(plan, first_shard, lambda j: first_shard)
    maps = lax.all_gather(low_kv, forth + ("core",), axis=0, tiled=True)
    images = with_layout_constraint(images, Layout(major_to_minor=(0, 1, 2)))
    out_turned = tuple(
        v.transpose(0, 2, 1) for v in (attn_out, attn_out_first, attn_out_second)
    )
    first, images, third_own, third_other, out_turned = hold(
        first, images, third_own, third_other, out_turned
    )
    packed_rows = packed.shape[0]
    heads = jnp.stack([p[attn_first + attn_second :].astype(F32) for p in first])
    heads = heads.reshape(mp, 3, packed_rows, heads.shape[-1]).sum(axis=1)
    first = (
        jnp.stack([p[:attn_first] for p in first]),
        jnp.stack([p[attn_first : attn_first + attn_second] for p in first]),
    )
    near = mp_swap(third_other, 1)
    for k in early:
        got = send_pair(plan, first, k)
        if k < plan.bits - 2:
            first = join_pair(first, got)
    got, near = hold(got, near)
    first = join_pair(first, got)
    third = jnp.stack([third_own, near])
    got = send_pair(plan, first, plan.bits - 1)
    first_cores = send_cores(first)
    for distance in plan.distances[1:]:
        if distance > 2:
            third = mp_double(third, distance)
    far_up = mp_swap(third[:, :ffn_rows], 2)
    kv_all = image_maps(plan, images, packed, maps)
    got, first_cores, kv_all, far_up = hold(got, first_cores, kv_all, far_up)
    got_cores = send_cores(got)
    far_down = mp_swap(third[:, ffn_rows:], 2)

    def before_last(values, order):
        for axis in order[:-2]:
            values = jnp.concatenate([values, swap(values, axis)])
        return values, swap(values, order[-2])

    up, up_got = before_last(jnp.concatenate([third[:, :ffn_rows], far_up]), forth)
    (got_cores,) = hold(got_cores)
    attn_set = Weights(
        plan, as_trees(plan, as_quarters(first, got, first_cores, got_cores)), attn_parts
    )
    qk_all, v_all, context_all, z_first, cross, wholes = self_forward(
        plan, caption_len, hidden, vec_rep, heads, [(attn_set, ["qk", "vc", "oo"])]
    )
    whole_qk, whole_vc, whole_oo = wholes

    def exchange(values):
        own, near, others = values
        got = mp_swap(others, 2)
        lane = lax.broadcasted_iota(jnp.int32, got.shape, 1)
        passed = mp_swap(jnp.where(lane < plan.width, near, got), 1)
        return own, passed, got

    far_down, cross, up_got = hold(far_down, cross, up_got)
    up = jnp.concatenate([up, up_got])
    down, down_got = before_last(jnp.concatenate([third[:, ffn_rows:], far_down]), back)
    queries = exchange(cross)
    (queries,) = hold(queries)
    contexts = cross_attend(plan, keys, queries, kv_all)
    contexts, down_got = hold(contexts, down_got)
    down = jnp.concatenate([down, down_got])
    half = up.shape[0] // 2
    up_last, down_last = swap(up[:half], forth[-1]), swap(down[:half], back[-1])
    contexts = exchange(contexts)
    contexts, down, up, up_last, down_last = hold(contexts, down, up, up_last, down_last)
    up_last = jnp.concatenate([up_last, swap(up[half:], forth[-1])])
    down_last = jnp.concatenate([down_last, swap(down[half:], back[-1])])
    up_core, down_core = send_cores((up, down))
    z_second, kept, given = cross_output(plan, vec_rep, z_first, contexts, whole_oo)
    kept, given = hold(kept, given)
    ffn_got = mp_swap(given, 1)
    up_last, down_last, up_core, down_core, ffn_got, kept = hold(
        up_last, down_last, up_core, down_core, ffn_got, kept
    )
    up_last_core, down_last_core = send_cores((up_last, down_last))
    up_last_core, down_last_core, ffn_got, kept = hold(
        up_last_core, down_last_core, ffn_got, kept
    )
    ffn_set = Weights(
        plan,
        as_trees(
            plan,
            (
                (up, up_last, up_core, up_last_core),
                (down, down_last, down_core, down_last_core),
            ),
        ),
        {"up": [Part("a", 0, ffn_rows, 0)], "down": [Part("b", 0, ffn_rows, 0)]},
    )
    layer, kept_back, given_back, third_sums, bias_sums, ffn_halves = feed_forward(
        plan,
        vec_rep,
        heads,
        kept,
        ffn_got,
        cotangent,
        [(ffn_set, ["up", "down"])],
        ffn_gradients,
    )
    cores = ("core", "core")
    ffn_state = ffn_halves["a"], ffn_halves["b"]
    got_back = mp_swap(given_back, 1)
    got = shrink_send(ffn_state, cores)
    got_back, got, kept_back, layer = hold(got_back, got, kept_back, layer)
    layer_near = mp_swap(layer, 1)
    ffn_state = shrink_add(ffn_state, got)
    for k in range(plan.bits - 1, 1, -1):
        ffn_state = shrink_add(ffn_state, shrink_send(ffn_state, (forth[k], back[k])))
    got = shrink_send(ffn_state, (forth[1], back[1]))
    cross_back, branch, caption_back, cross_sums, context_back = cross_output_backward(
        plan, vec_rep, z_second, kept_back, got_back, whole_oo
    )
    (context_back,) = hold(context_back)
    context_back = exchange(context_back)
    context_back, layer_near = hold(context_back, layer_near)
    layer_two = jnp.stack([layer, layer_near])
    layer_across = mp_middle(plan, layer_two)
    kv_back, value_sum, query_back = cross_attend_backward(
        plan, keys, queries, context_back, kv_all
    )
    query_back, got = hold(query_back, got)
    ffn_state = shrink_add(ffn_state, got)
    got = shrink_send(ffn_state, (forth[0], back[0]))
    kv_grad = image_gradient(plan, images, kv_back)
    query_back = exchange(query_back)
    query_back, got, layer_across, kv_grad = hold(query_back, got, layer_across, kv_grad)
    kv_total = lax.psum_scatter(
        kv_grad, forth + ("core",), scatter_dimension=0, tiled=True
    )
    ffn_state = join_trees(shrink_add(ffn_state, got))
    for distance in plan.distances[:1:-1]:
        ffn_state = mp_halve(ffn_state, distance)
    first_back, first_sums = cross_input_backward(
        plan, vec_rep, z_first, cross_back, caption_back, query_back, whole_vc
    )
    out_halves = output_gradient(plan, first_back, branch, context_all, contexts, out_gradients)
    ffn_state, first_back, out_halves = hold(ffn_state, first_back, out_halves)
    middle = ffn_rows if ffn_state[1].shape[0] == 2 else 0
    ffn_got_up = mp_swap(ffn_state[1][:, :middle], 2)
    layer_far = mp_outward(plan, layer_across)
    out_state = out_halves["a"], out_halves["b"]
    out_got = shrink_send(out_state, cores)
    token_back, vectors, maps_back, value_maps = self_backward(
        plan,
        caption_len,
        (vec_rep, first_back, qk_all, v_all),
        (first_sums, cross_sums, third_sums, bias_sums, value_sum),
        wholes,
    )
    token_back, maps_back, vectors, ffn_got_up, out_got = hold(
        token_back, maps_back, vectors, ffn_got_up, out_got
    )
    across_own = mp_middle(plan, token_back)
    near = mp_swap(token_back, 1)
    out_state = shrink_add(out_state, out_got)
    for k in range(plan.bits - 1, 1, -1):
        out_state = shrink_add(out_state, shrink_send(out_state, (forth[k], back[k])))
    out_got = shrink_send(out_state, (forth[1], back[1]))
    attn_halves = self_gradient(
        plan,
        hidden,
        (vec_rep, z_first, maps_back, value_maps, *query_back),
        attn_gradients,
    )
    across_own, layer_far, near, attn_halves, out_got = hold(
        across_own, layer_far, near, attn_halves, out_got
    )
    attn_state = attn_halves["a"], attn_halves["b"]
    attn_got = shrink_send(attn_state, cores)
    ffn_got_down = mp_swap(ffn_state[1][:, middle:], 2)
    out_state = shrink_add(out_state, out_got)
    out_got = shrink_send(out_state, (forth[0], back[0]))
    attn_got, out_got, ffn_got_down, vectors = hold(attn_got, out_got, ffn_got_down, vectors)
    across_near = mp_middle(plan, near)
    far_own = mp_outward(plan, across_own)
    attn_state = shrink_add(attn_state, attn_got)
    for k in range(plan.bits - 1, 1, -1):
        attn_state = shrink_add(attn_state, shrink_send(attn_state, (forth[k], back[k])))
    attn_got = shrink_send(attn_state, (forth[1], back[1]))
    out_state = shrink_add(out_state, out_got)
    vector_got = mp_swap(vectors, 1)
    attn_got, across_near, far_own, vector_got = hold(
        attn_got, across_near, far_own, vector_got
    )
    vectors = vectors + vector_got
    for distance in plan.distances[2:]:
        vectors = vectors + mp_swap(vectors, distance)
    vector_got = mp_swap(vectors, 2)
    attn_state = shrink_add(attn_state, attn_got)
    attn_got = shrink_send(attn_state, (forth[0], back[0]))
    far_near = mp_outward(plan, across_near)
    ffn_got = jnp.concatenate([ffn_got_up, ffn_got_down], axis=1)
    half = ffn_got.shape[0] // 2
    ffn_state = (
        add_low(ffn_state[0][:half], ffn_got[:half]),
        add_low(ffn_state[0][half:], ffn_got[half:]),
    )
    theirs = mp_swap(ffn_state[1][0], 1)
    attn_got, vector_got, theirs, far_near = hold(attn_got, vector_got, theirs, far_near)
    attn_state = shrink_add(attn_state, attn_got)
    pieces = mp_scatter(plan, join_trees(attn_state + out_state))
    vectors = vectors + vector_got
    for axis in forth:
        vectors = vectors + swap(vectors, axis)
    grad_hidden = place_gradient(
        plan, token_back, near, across_own, across_near, far_own, far_near
    )
    layer_out = place_layer(plan, layer_two, layer_across, layer_far)
    turn = (0, 2, 1)
    ffn_results = ffn_step(
        ffn_state[0][0],
        theirs,
        (ffn_up, ffn_up_first, ffn_up_second),
        tuple(v.transpose(turn) for v in (ffn_down, ffn_down_first, ffn_down_second)),
    )
    vectors, grad_hidden, layer_out, ffn_results = hold(
        vectors, grad_hidden, layer_out, ffn_results
    )
    vectors = vectors + swap(vectors, "core")
    results = other_steps(
        plan,
        pieces,
        kv_total,
        (attn_in, attn_in_first, attn_in_second),
        out_turned,
        (cross_key_value_maps, cross_kv_first, cross_kv_second),
    )
    vector_results = vector_steps(
        plan,
        vectors,
        (vec_rep, vec_rep_first, vec_rep_second),
        (query_value_bias_rows, vec_head_first, vec_head_second),
        (bias_up, bias_up_first, bias_up_second),
    )
    return (
        layer_out,
        grad_hidden,
        *results,
        *ffn_results[:3],
        *(v.transpose(turn) for v in ffn_results[3:]),
        *vector_results,
    )


def solution(mesh):
    dp, mp = mesh.devices.shape
    bits = (dp // 2).bit_length() - 1
    names = tuple(f"b{k}" for k in range(bits)) + ("core",)
    fine = Mesh(mesh.devices.reshape((2,) * (bits + 1) + (mp,)), names + ("mp",))
    split = P(names)
    inward = P(None, names, "mp")
    outward = P(None, "mp", names)
    head = P(None, "mp")
    stored = (inward,) * 3 + (outward,) * 3 + (inward,) * 6 + (outward,) * 3 + (P(),) * 3 + (head,) * 6
    return jax.shard_map(
        functools.partial(local, bits),
        mesh=fine,
        in_specs=(split,) * 4 + stored,
        out_specs=(split,) * 2 + stored,
        check_vma=False,
    )
```

```python
import functools
import math

import jax
import jax.numpy as jnp
from jax import lax
from jax.experimental import pallas as pl
from jax.experimental.layout import Layout, with_layout_constraint
from jax.experimental.pallas import tpu as pltpu
from jax.sharding import Mesh
from jax.sharding import PartitionSpec as P

D = 768
HEAD_DIM = 64
F = 3072
E = 1408
NQ = 32
STEP_COUNT = 10

NORM_EPS = 1e-06
BETA_ONE = 0.9
BETA_TWO = 0.999
ADAM_EPS = 1e-08
WEIGHT_DECAY = 0.01
MASKED = -1000000000.0

BF = jnp.bfloat16
F32 = jnp.float32
SCALE = HEAD_DIM ** (-0.5)
MIB = 1 << 20


def dot(a, b):
    return lax.dot_general(a, b, (((1,), (0,)), ((), ())), preferred_element_type=F32)


def dot_t(a, b):
    return lax.dot_general(a, b, (((1,), (1,)), ((), ())), preferred_element_type=F32)


def t_dot(a, b):
    return lax.dot_general(a, b, (((0,), (0,)), ((), ())), preferred_element_type=F32)


def swap(values, axis):
    return lax.ppermute(values, axis, [(0, 1), (1, 0)])


def mp_swap(values, distance):
    count = lax.axis_size("mp")
    return lax.ppermute(values, "mp", [(i, i ^ distance) for i in range(count)])


class Plan:
    def __init__(self, bits, mp, items, dp):
        self.bits = bits
        self.mp = mp
        self.dp = dp
        self.items = items
        self.rows = items * 2 * NQ
        self.half = items * NQ
        self.width = D // mp
        self.forth = tuple(f"b{k}" for k in range(bits))
        self.back = self.forth[::-1]
        self.distances = [1 << k for k in range(mp.bit_length() - 1)]

    def bit(self, axis):
        return 1 if axis == "core" else 2 << (self.bits - 1 - int(axis[1:]))

    def masks(self, order):
        found = [0]
        for axis in order + ("core",):
            found = found + [m | self.bit(axis) for m in found]
        return found

    def dp_index(self):
        place = lax.axis_index("core")
        for axis in self.forth:
            place = place + self.bit(axis) * lax.axis_index(axis)
        return place


class Part:
    def __init__(self, tree, low, count, place):
        self.tree, self.low, self.count, self.place = tree, low, count, place


def hold(*values):
    return lax.optimization_barrier(values)


def mp_double(values, distance):
    return jnp.concatenate([values, mp_swap(values, distance)])


def mp_direct(plan, own, sent):
    return [own] + [mp_swap(sent(j), j) for j in range(1, plan.mp)]


def two_trees(pieces, rows):
    return (
        jnp.concatenate([p[None, :rows] for p in pieces]),
        jnp.concatenate([p[None, rows:] for p in pieces]),
    )


def send_pair(plan, pair, k):
    return swap(pair[0], plan.forth[k]), swap(pair[1], plan.back[k])


def send_cores(pair):
    return tuple(swap(v, "core") for v in pair)


def join_pair(pair, got):
    return tuple(jnp.concatenate([v, g]) for v, g in zip(pair, got))


def as_quarters(pair, got, cores, got_cores):
    return tuple(zip(pair, got, cores, got_cores))


def as_trees(plan, cores):
    return {"a": (cores[0], plan.forth), "b": (cores[1], plan.back)}


def line_pairs(plan):
    return [(1, 2), (2, 1)], [(0, 1), (3, 2)], [(1, 0), (2, 3)]


def mp_middle(plan, values):
    if plan.mp != 4:
        return mp_swap(values, 2)
    return lax.ppermute(values, "mp", line_pairs(plan)[0])


def mp_outward(plan, got):
    if plan.mp != 4:
        return got
    return lax.ppermute(got, "mp", line_pairs(plan)[2])


def from_line(plan, across, far, j):
    if plan.mp != 4:
        return across[j - 2]
    me = lax.axis_index("mp")
    return jnp.where((me == 0) | (me == 3), far[j - 2], across[3 - j])


def mp_inward(plan, state):
    kept, sent = state
    if plan.mp != 4:
        return state
    got = lax.ppermute(sent, "mp", line_pairs(plan)[1])
    return kept, add_low(sent, got[::-1])


def mp_across(plan, state):
    kept, sent = state
    if plan.mp != 4:
        return mp_halve(state, 2)
    got = lax.ppermute(sent, "mp", line_pairs(plan)[0])
    return add_low(kept[:1], got[1:]), add_low(kept[1:], got[:1])


def natural_tree(plan, halves, order):
    values = jnp.concatenate(halves)
    values = values.reshape((plan.dp, values.shape[0] // plan.dp) + values.shape[1:])
    back = [0] * plan.dp
    for k, mask in enumerate(plan.masks(order)):
        back[mask] = k
    places = jnp.take(jnp.array(back), jnp.arange(plan.dp) ^ plan.dp_index())
    return jnp.take(values, places, axis=0)


def assemble(plan, trees, parts):
    found = []
    for part in parts:
        halves, order = trees[part.tree]
        natural = natural_tree(plan, halves, order)
        found.append(natural[:, :, part.low : part.low + part.count])
    whole = jnp.concatenate(found, axis=2).transpose(1, 0, 2, 3)
    return whole.reshape(whole.shape[0], -1, whole.shape[-1])


def by_distance(plan, matrices, segments, order):
    places = jnp.array(plan.masks(order)) ^ plan.dp_index()
    found = []
    for name, part in segments:
        blocks = matrices[name]
        blocks = blocks.reshape(blocks.shape[0], plan.dp, -1, blocks.shape[-1])
        blocks = jnp.take(blocks, places, axis=1).transpose(1, 0, 2, 3)
        found.append(blocks[:, :, part.place : part.place + part.count])
    whole = jnp.concatenate(found, axis=2)
    whole = whole.reshape((-1,) + whole.shape[2:])
    return whole[: whole.shape[0] // 2], whole[whole.shape[0] // 2 :]


def add_low(first, second):
    return (first.astype(F32) + second.astype(F32)).astype(BF)


def shrink_send(halves, axes):
    return tuple(swap(sent, axis) for (_, sent), axis in zip(halves, axes))


def shrink_add(halves, found):
    sums = []
    for (kept, _), got in zip(halves, found):
        half = got.shape[0] // 2
        sums.append((add_low(kept[:half], got[:half]), add_low(kept[half:], got[half:])))
    return tuple(sums)


def join_trees(halves):
    return tuple(jnp.concatenate([h[k] for h in halves], axis=1) for k in range(2))


def mp_halve(state, distance):
    kept, sent = state
    got = mp_swap(sent, distance)
    half = got.shape[0] // 2
    return add_low(kept[:half], got[:half]), add_low(kept[half:], got[half:])


def mp_scatter(plan, state):
    kept, sent = state
    pieces = [kept[0]]
    for j in range(1, plan.mp):
        values = kept if j < plan.mp // 2 else sent
        pieces.append(mp_swap(values[j % (plan.mp // 2)], j))
    return pieces


def mp_last(state):
    kept, sent = state
    return kept[0].astype(F32), mp_swap(sent[0], 1).astype(F32)


def norm_parts(values):
    center = values - jnp.mean(values, axis=-1, keepdims=True)
    spread = jnp.mean(center * center, axis=-1, keepdims=True)
    inverse = lax.rsqrt(spread + NORM_EPS)
    return center * inverse, inverse


def norm_backward(grad_out, normed, inverse, gain):
    scaled = grad_out * gain
    inner = (
        scaled
        - jnp.mean(scaled, axis=-1, keepdims=True)
        - normed * jnp.mean(scaled * normed, axis=-1, keepdims=True)
    )
    return inner * inverse


def column_sum(values):
    return jnp.sum(values.astype(F32), axis=0, keepdims=True)


def halves_of(values, items):
    split = values.reshape(items, 2 * NQ, values.shape[-1])
    parts = split[:, :NQ], split[:, NQ:]
    return tuple(p.reshape(items * NQ, values.shape[-1]) for p in parts)


def join_halves(query, caption, items):
    width = query.shape[-1]
    parts = [v.reshape(items, NQ, width) for v in (query, caption)]
    return jnp.concatenate(parts, axis=1).reshape(items * 2 * NQ, width)


def wide(first, second):
    return jnp.concatenate([first, second], axis=1)


def after(values, width):
    return jnp.concatenate([jnp.zeros_like(values), values], axis=1)


def before(values, width):
    return jnp.concatenate([values, jnp.zeros_like(values)], axis=1)


def head_lanes(width):
    lane = lax.broadcasted_iota(jnp.int32, (1, width), 1)
    return [lane // HEAD_DIM == h for h in range(width // HEAD_DIM)]


def only(values, lanes):
    return jnp.where(lanes, values, jnp.zeros_like(values))


def softmax(scores):
    expo = jnp.exp(scores - jnp.max(scores, axis=-1, keepdims=True))
    return expo * (1.0 / jnp.sum(expo, axis=-1, keepdims=True))


def fetch(plan, refs, parts, trees, target, sem):
    if trees is None:
        pltpu.make_async_copy(refs[0], target, sem).start()
        return
    place = plan.dp_index()
    block = sum(p.count for p in parts)
    for part in parts:
        found, order = trees[part.tree]
        for k, mask in enumerate(plan.masks(order)):
            quarter, index = divmod(k, plan.dp // len(found))
            begin = pl.multiple_of((place ^ mask) * block + part.place, 16)
            pieces = refs[found[quarter]].at[pl.ds(index * plan.mp, plan.mp)]
            pltpu.make_async_copy(
                pieces.at[:, pl.ds(part.low, part.count), :],
                target.at[:, pl.ds(begin, part.count), :],
                sem,
            ).start()


def fetch_whole(matrix, target, sem):
    pltpu.make_async_copy(matrix, target, sem).start()


def settle(target, sem):
    pltpu.make_async_copy(target, target, sem).wait()


def spread(plan, source, parts, outs, sem):
    if parts is None:
        pltpu.make_async_copy(source, outs, sem).start()
        return
    place = plan.dp_index()
    block = sum(p.count for p in parts)
    for part in parts:
        halves, order = outs[part.tree]
        for k, mask in enumerate(plan.masks(order)):
            half, index = divmod(k, plan.dp // 2)
            begin = pl.multiple_of((place ^ mask) * block + part.place, 16)
            pieces = halves[half].at[pl.ds(index * plan.mp, plan.mp)]
            pltpu.make_async_copy(
                source.at[:, pl.ds(begin, part.count), :],
                pieces.at[:, pl.ds(part.low, part.count), :],
                sem,
            ).start()


class Weights:
    def __init__(self, plan, trees, matrices):
        self.plan, self.matrices = plan, matrices
        self.direct = all(p.count % 16 == 0 for parts in matrices.values() for p in parts)
        if self.direct:
            self.trees = trees
        else:
            self.whole = {n: assemble(plan, trees, parts) for n, parts in matrices.items()}

    def operands(self, names):
        arrays, found = [], {}
        if not self.direct:
            for name in names:
                found[name] = (len(arrays), self.matrices[name], None)
                arrays.append(self.whole[name])
            return arrays, found
        seen = {}
        for name in names:
            for part in self.matrices[name]:
                if part.tree not in seen:
                    halves, order = self.trees[part.tree]
                    seen[part.tree] = (range(len(arrays), len(arrays) + len(halves)), order)
                    arrays.extend(halves)
            found[name] = (0, self.matrices[name], seen)
        return arrays, found


def gather_operands(sets):
    arrays, starts = [], {}
    for weights, names in sets:
        more, found = weights.operands(names)
        base = len(arrays)
        for name, (place, parts, trees) in found.items():
            starts[name] = functools.partial(
                lambda refs, target, sem, base, place, parts, trees, plan: fetch(
                    plan, refs[base + place :], parts, trees, target, sem
                )
                if trees is None
                else fetch(plan, refs[base:], parts, trees, target, sem),
                base=base,
                place=place,
                parts=parts,
                trees=trees,
                plan=weights.plan,
            )
        arrays.extend(more)
    return arrays, starts


class Gradients:
    def __init__(self, plan, trees, matrices, over):
        self.plan, self.trees, self.matrices, self.over = plan, trees, matrices, over
        self.direct = all(p.count % 16 == 0 for parts, _ in matrices.values() for p in parts)

    def shapes(self):
        found = []
        if self.direct:
            for _, rows, columns in self.trees.values():
                shape = (self.plan.dp // 2 * self.over, rows, columns)
                found += [jax.ShapeDtypeStruct(shape, BF)] * 2
            return found
        for parts, rows in self.matrices.values():
            columns = self.trees[parts[0].tree][2]
            found.append(jax.ShapeDtypeStruct((self.over, rows, columns), BF))
        return found

    def write(self, name, source, refs, sem):
        parts = self.matrices[name][0]
        if self.direct:
            outs = {
                tree: (refs[2 * k : 2 * k + 2], order)
                for k, (tree, (order, _, _)) in enumerate(self.trees.items())
            }
            spread(self.plan, source, parts, outs, sem)
        else:
            spread(self.plan, source, None, refs[list(self.matrices).index(name)], sem)

    def halves(self, arrays):
        if self.direct:
            return {t: tuple(arrays[2 * k : 2 * k + 2]) for k, t in enumerate(self.trees)}
        named = dict(zip(self.matrices, arrays))
        found = {}
        for tree, (order, _, _) in self.trees.items():
            segments = [
                (name, part)
                for name, (parts, _) in self.matrices.items()
                for part in parts
                if part.tree == tree
            ]
            segments.sort(key=lambda s: s[1].low)
            found[tree] = by_distance(self.plan, named, segments, order)
        return found


def call(kernel, ins, places, outs, out_places, scratch, limit):
    return pl.pallas_call(
        kernel,
        out_shape=outs,
        in_specs=[pl.BlockSpec(memory_space=p) for p in places],
        out_specs=[pl.BlockSpec(memory_space=p) for p in out_places],
        scratch_shapes=scratch,
        compiler_params=pltpu.CompilerParams(vmem_limit_bytes=limit * MIB),
        cost_estimate=pl.CostEstimate(flops=1000, bytes_accessed=1000, transcendentals=0),
    )(*ins)


ANY, HBM, VMEM, SMEM = pl.ANY, pltpu.HBM, pltpu.VMEM, pltpu.SMEM
DMA = pltpu.SemaphoreType.DMA


def self_mask(plan, lengths, me):
    count = plan.rows
    row = lax.broadcasted_iota(jnp.int32, (count, count), 0)
    col = lax.broadcasted_iota(jnp.int32, (count, count), 1)
    span = 2 * NQ
    limit = jnp.zeros((count, count), jnp.int32)
    for i in range(plan.items):
        limit = jnp.where(col // span == i, lengths[me * plan.items + i], limit)
    inside = col % span
    valid = (row // span == col // span) & ((inside < NQ) | (inside - NQ < limit))
    return jnp.where(valid, 0.0, MASKED).astype(F32)


def load_tokens(plan, hidden, target, sem):
    me = lax.axis_index("mp")
    return pltpu.make_async_copy(hidden.at[pl.ds(me * plan.items, plan.items)], target, sem)


def distance_shapes(plan):
    both = jax.ShapeDtypeStruct((plan.half, 2 * plan.width), BF)
    return [jax.ShapeDtypeStruct((plan.half, plan.width), BF), both, both]


def put_distance(refs, j, values):
    width = values.shape[1]
    if j == 0:
        refs[0][...] = values
    elif j == 1:
        refs[1][...] = before(values, width)
    else:
        refs[2][:, (j - 2) * width : (j - 1) * width] = values


def get_distance(refs, j, span=slice(None)):
    width = refs[0].shape[1]
    if j == 0:
        return refs[0][span, :]
    if j == 2:
        return refs[2][span, :width]
    return refs[1][span, :width] if j == 1 else refs[1][span, width:]


def self_forward(plan, lengths, hidden, vec, heads, sets):
    arrays, starts = gather_operands(sets)
    count = len(arrays)
    mp, rows, half, width, items = plan.mp, plan.rows, plan.half, plan.width, plan.items

    def kernel(lengths, hidden, vec, heads, *rest):
        refs = rest[:count]
        qk_out, v_out, context_out, z_out = rest[count : count + 4]
        cross = rest[count + 4 : count + 7]
        wholes = rest[count + 7 : count + 10]
        tokens, w_qk, w_vc, w_oo, sems = rest[count + 10 :]
        me = lax.axis_index("mp")
        loaded = load_tokens(plan, hidden, tokens, sems.at[0])
        loaded.start()
        starts["qk"](refs, w_qk, sems.at[1])
        starts["vc"](refs, w_vc, sems.at[2])
        starts["oo"](refs, w_oo, sems.at[3])
        mask = self_mask(plan, lengths, me)
        lanes = head_lanes(width)
        loaded.wait()
        x = tokens[...].reshape(rows, D)
        total = x.astype(F32) + vec[0:1, :]
        kept = []
        for k, matrix in enumerate((w_qk, w_vc, w_oo)):
            settle(matrix, sems.at[1 + k])
            kept.append(pltpu.make_async_copy(matrix, wholes[k], sems.at[4 + k]))
            kept[-1].start()
        for j in range(mp):
            both = (dot(x, w_qk[j]) + heads[j, 0:1, :]).astype(BF)
            qk_out[j] = both
            q, k = both[:, :width], both[:, width:]
            v = (dot(x, w_vc[j]) + heads[j, 1:2, :]).astype(BF)[:, :width]
            v_out[j] = v
            context = jnp.zeros((rows, width), F32)
            for lane in lanes:
                probs = softmax(dot_t(only(q, lane), k) * SCALE + mask)
                context = context + only(dot(probs.astype(BF), v), lane)
            context = context.astype(BF)
            context_out[j] = context
            total = total + dot_t(before(context, width), w_oo[j])
        z_out[...] = total
        normed, _ = norm_parts(total)
        u = halves_of(normed * vec[4:5, :] + vec[5:6, :], items)[0].astype(BF)
        for j in range(mp):
            maps = (dot(u, w_vc[j]) + heads[j, 1:2, :]).astype(BF)
            put_distance(cross, j, maps[:, width:])
        for copy in kept:
            copy.wait()

    whole = jax.ShapeDtypeStruct((mp, D, 2 * width), BF)
    outs = [
        jax.ShapeDtypeStruct((mp, rows, 2 * width), BF),
        jax.ShapeDtypeStruct((mp, rows, width), BF),
        jax.ShapeDtypeStruct((mp, rows, width), BF),
        jax.ShapeDtypeStruct((rows, D), F32),
        *distance_shapes(plan),
        whole,
        whole,
        whole,
    ]
    found = call(
        kernel,
        (lengths, hidden, vec, heads, *arrays),
        [SMEM, HBM, VMEM, VMEM] + [ANY] * count,
        outs,
        [VMEM] * 7 + [HBM] * 3,
        [
            pltpu.VMEM((items, 2 * NQ, D), BF),
            *[pltpu.VMEM((mp, D, 2 * width), BF)] * 3,
            DMA((7,)),
        ],
        28,
    )
    return (*found[:4], found[4:7], found[7:])


def load_images(images, held, sems):
    count = images.shape[0]
    cut = -(-count // 4)
    found = []
    for k in range(0, count, cut):
        span = pl.ds(k, min(cut, count - k))
        found.append(pltpu.make_async_copy(images.at[span], held.at[span], sems.at[k // cut]))
        found[-1].start()
    return found, cut


def image_maps(plan, images, bias, maps):
    items, keys, features = images.shape
    width = plan.width
    padded = -(-keys // 128) * 128

    def kernel(images, bias, maps, out, held, w_kv, sems, w_sem):
        weights = pltpu.make_async_copy(maps, w_kv, w_sem.at[0])
        weights.start()
        loaded, cut = load_images(images, held, sems)
        weights.wait()
        for n, copy in enumerate(loaded):
            copy.wait()

            def step(i, carry):
                both = (dot(held[i], w_kv[...]) + bias[2:3, :]).astype(BF)
                out[i, 0:keys, :] = both
                out[i, keys:padded, :] = jnp.zeros((padded - keys, 2 * width), BF)
                return carry

            lax.fori_loop(n * cut, min(items, (n + 1) * cut), step, 0)

    return call(
        kernel,
        (images, bias, maps),
        [ANY, VMEM, ANY],
        [jax.ShapeDtypeStruct((items, padded, 2 * width), BF)],
        [VMEM],
        [
            pltpu.VMEM((items, keys, features), BF),
            pltpu.VMEM((features, 2 * width), BF),
            DMA((4,)),
            DMA((1,)),
        ],
        28,
    )[0]


def key_mask(plan, keys, padded):
    lane = lax.broadcasted_iota(jnp.int32, (1, padded), 1)
    return jnp.where(lane < keys, 0.0, MASKED).astype(F32)


def spread_heads(values, lanes):
    return jnp.concatenate([only(values, lane) for lane in lanes], axis=0)


def gather_heads(values, lanes):
    total = None
    for h, lane in enumerate(lanes):
        part = only(values[h * NQ : (h + 1) * NQ], lane)
        total = part if total is None else total + part
    return total


def cross_attend(plan, keys, queries, kv):
    mp, half, width, items = plan.mp, plan.half, plan.width, plan.items
    padded = kv.shape[1]

    def kernel(*refs):
        queries, kv, contexts = refs[:3], refs[3], refs[4:]
        me = lax.axis_index("mp")
        lanes = head_lanes(width)
        mask = key_mask(plan, keys, padded)
        for j in range(mp):
            rows = []
            for i in range(items):
                q = spread_heads(get_distance(queries, j, slice(i * NQ, (i + 1) * NQ)), lanes)
                both = kv[(me ^ j) * items + i]
                probs = softmax(dot_t(q, both[:, :width]) * SCALE + mask)
                rows.append(gather_heads(dot(probs.astype(BF), both[:, width:]), lanes))
            put_distance(contexts, j, jnp.concatenate(rows, axis=0).astype(BF))

    return call(
        kernel,
        (*queries, kv),
        [VMEM] * 4,
        distance_shapes(plan),
        [VMEM] * 3,
        [],
        24,
    )


def cross_output(plan, vec, z_first, contexts, whole_oo):
    mp, half, width, items = plan.mp, plan.half, plan.width, plan.items

    def kernel(vec, z_first, *rest):
        contexts, whole_oo = rest[:3], rest[3]
        z_out, kept, given, w_oo, sems = rest[4:]
        me = lax.axis_index("mp")
        fetch_whole(whole_oo, w_oo, sems.at[0])
        normed, _ = norm_parts(z_first[...])
        query, caption = halves_of(normed * vec[4:5, :] + vec[5:6, :], items)
        total = query + vec[1:2, :]
        settle(w_oo, sems.at[0])
        for j in range(mp):
            total = total + dot_t(after(get_distance(contexts, j), width), w_oo[j])
        z_out[...] = total
        normed, _ = norm_parts(total)
        second = normed * vec[6:7, :] + vec[7:8, :]
        low = (me & 1) == 0
        kept[...] = jnp.where(low, second, caption)
        given[...] = jnp.where(low, caption, second).astype(BF)

    return call(
        kernel,
        (vec, z_first, *contexts, whole_oo),
        [VMEM] * 5 + [HBM],
        [
            jax.ShapeDtypeStruct((half, D), F32),
            jax.ShapeDtypeStruct((half, D), F32),
            jax.ShapeDtypeStruct((half, D), BF),
        ],
        [VMEM] * 3,
        [pltpu.VMEM((mp, D, 2 * width), BF), DMA((1,))],
        16,
    )


def feed_forward(plan, vec, heads, kept, got, cotangent, sets, gradients):
    arrays, starts = gather_operands(sets)
    count = len(arrays)
    mp, half, items = plan.mp, plan.half, plan.items
    hidden_width = F // mp
    shapes = gradients.shapes()

    def kernel(vec, heads, kept, got, cotangent, *rest):
        refs, rest = rest[:count], rest[count:]
        layer, kept_back, given_back, sums, bias_sums = rest[:5]
        grad_out = rest[5 : 5 + len(shapes)]
        top, w_up, w_down, slope, act, up_grad, down_grad, w_sems, sems = rest[5 + len(shapes) :]
        me = lax.axis_index("mp")
        group = me & 1
        starts["up"](refs, w_up, w_sems.at[0])
        starts["down"](refs, w_down, w_sems.at[1])
        tops = []
        for s in range(2):
            first = (me ^ s) * items
            tops.append(
                pltpu.make_async_copy(
                    cotangent.at[
                        pl.ds(first, items), pl.ds(pl.multiple_of(group * NQ, NQ), NQ), :
                    ],
                    top.at[s],
                    sems.at[2 + s],
                )
            )
            tops[-1].start()
        x = jnp.concatenate([kept[...], got[...].astype(F32)], axis=0)
        low = x.astype(BF)
        low_t = low.T
        total = x + vec[pl.ds(2 + group, 1), :]
        settle(w_up, w_sems.at[0])
        for z in range(mp):
            bias = wide(
                heads[z, pl.ds(3 + 2 * group, 1), :], heads[z, pl.ds(4 + 2 * group, 1), :]
            )
            pre = dot(low, w_up[z]) + bias
            cdf = 0.5 + 0.5 * lax.erf(pre * (0.5**0.5))
            value = (pre * cdf).astype(BF)
            act[z] = value
            slope[z] = cdf + pre * jnp.exp(-0.5 * pre * pre) * (1.0 / math.sqrt(2.0 * math.pi))
            if z == 0:
                settle(w_down, w_sems.at[1])
            total = total + dot_t(value, w_down[z])
        normed, inverse = norm_parts(total)
        gain = vec[pl.ds(8 + 2 * group, 1), :]
        third = normed * gain + vec[pl.ds(9 + 2 * group, 1), :]
        layer[...] = third.astype(BF).reshape(2, items, NQ, D)
        for t in tops:
            t.wait()
        grad = top[...].reshape(2 * half, D).astype(F32)
        back = norm_backward(grad, normed, inverse, gain)
        branch = back.astype(BF)
        sums[0:1, :] = column_sum(branch)
        sums[1:2, :] = column_sum(grad * normed)
        sums[2:3, :] = column_sum(grad)
        branch_t = branch.T
        for z in range(mp):
            down_grad[z] = dot(branch_t, act[z]).astype(BF)
        gradients.write("down", down_grad, grad_out, sems.at[0])
        for z in range(mp):
            pull = (dot(branch, w_down[z]) * slope[z]).astype(BF)
            bias_sums[pl.ds(me ^ z, 1), :] = column_sum(pull)
            up_grad[z] = dot(low_t, pull).astype(BF)
            back = back + dot_t(pull, w_up[z])
        gradients.write("up", up_grad, grad_out, sems.at[1])
        kept_back[...] = back[:half]
        given_back[...] = back[half:].astype(BF)
        settle(down_grad, sems.at[0])
        settle(up_grad, sems.at[1])

    outs = [
        jax.ShapeDtypeStruct((2, items, NQ, D), BF),
        jax.ShapeDtypeStruct((half, D), F32),
        jax.ShapeDtypeStruct((half, D), BF),
        jax.ShapeDtypeStruct((3, D), F32),
        jax.ShapeDtypeStruct((mp, hidden_width), F32),
        *shapes,
    ]
    found = call(
        kernel,
        (vec, heads, kept, got, cotangent, *arrays),
        [VMEM] * 4 + [HBM] + [ANY] * count,
        outs,
        [VMEM] * 5 + [HBM] * len(shapes),
        [
            pltpu.VMEM((2, items, NQ, D), BF),
            pltpu.VMEM((mp, D, hidden_width), BF),
            pltpu.VMEM((mp, D, hidden_width), BF),
            pltpu.VMEM((mp, 2 * half, hidden_width), F32),
            pltpu.VMEM((mp, 2 * half, hidden_width), BF),
            pltpu.VMEM((mp, D, hidden_width), BF),
            pltpu.VMEM((mp, D, hidden_width), BF),
            DMA((2,)),
            DMA((4,)),
        ],
        48,
    )
    return (*found[:5], gradients.halves(found[5:]))


def cross_output_backward(plan, vec, z_second, kept, got, whole_oo):
    mp, half, width = plan.mp, plan.half, plan.width

    def kernel(vec, z_second, kept, got, whole_oo, *rest):
        back_out, branch_out, caption, sums = rest[:4]
        context_back = rest[4:7]
        w_oo, sems = rest[7:]
        low = (lax.axis_index("mp") & 1) == 0
        fetch_whole(whole_oo, w_oo, sems.at[0])
        other = got[...].astype(F32)
        grad = jnp.where(low, kept[...], other)
        caption[...] = jnp.where(low, other, kept[...])
        normed, inverse = norm_parts(z_second[...])
        back = norm_backward(grad, normed, inverse, vec[6:7, :])
        branch = back.astype(BF)
        back_out[...] = back
        branch_out[...] = branch
        sums[0:1, :] = column_sum(branch)
        sums[1:2, :] = column_sum(grad * normed)
        sums[2:3, :] = column_sum(grad)
        settle(w_oo, sems.at[0])
        for j in range(mp):
            put_distance(context_back, j, dot(branch, w_oo[j]).astype(BF)[:, width:])

    found = call(
        kernel,
        (vec, z_second, kept, got, whole_oo),
        [VMEM] * 4 + [HBM],
        [
            jax.ShapeDtypeStruct((half, D), F32),
            jax.ShapeDtypeStruct((half, D), BF),
            jax.ShapeDtypeStruct((half, D), F32),
            jax.ShapeDtypeStruct((3, D), F32),
            *distance_shapes(plan),
        ],
        [VMEM] * 7,
        [pltpu.VMEM((mp, D, 2 * width), BF), DMA((1,))],
        16,
    )
    return (*found[:4], found[4:])


def cross_attend_backward(plan, keys, queries, context_back, kv):
    mp, half, width, items = plan.mp, plan.half, plan.width, plan.items
    padded = kv.shape[1]

    def kernel(*refs):
        queries, context_back, kv = refs[:3], refs[3:6], refs[6]
        kv_back, value_sum, query_back = refs[7], refs[8], refs[9:]
        me = lax.axis_index("mp")
        lanes = head_lanes(width)
        mask = key_mask(plan, keys, padded)
        total = jnp.zeros((1, width), F32)
        for j in range(mp):
            rows = []
            for i in range(items):
                span = slice(i * NQ, (i + 1) * NQ)
                item = (me ^ j) * items + i
                q = spread_heads(get_distance(queries, j, span), lanes)
                g = spread_heads(get_distance(context_back, j, span), lanes)
                both = kv[item]
                k, v = both[:, :width], both[:, width:]
                probs = softmax(dot_t(q, k) * SCALE + mask)
                pulled = dot_t(g, v)
                scored = probs * (pulled - jnp.sum(probs * pulled, axis=-1, keepdims=True))
                scored = scored.astype(BF)
                value_back = t_dot(probs.astype(BF), g).astype(BF)
                key_back = (t_dot(scored, q) * SCALE).astype(BF)
                kv_back[item] = wide(key_back, value_back)
                total = total + column_sum(value_back)
                rows.append(gather_heads(dot(scored, k), lanes) * SCALE)
            put_distance(query_back, j, jnp.concatenate(rows, axis=0).astype(BF))
        value_sum[...] = total

    found = call(
        kernel,
        (*queries, *context_back, kv),
        [VMEM] * 7,
        [
            jax.ShapeDtypeStruct((mp * items, padded, 2 * width), BF),
            jax.ShapeDtypeStruct((1, width), F32),
            *distance_shapes(plan),
        ],
        [VMEM] * 5,
        [],
        28,
    )
    return found[0], found[1], found[2:]


def put_columns(target, row, found, me, width):
    for z in range(len(found)):
        total = jnp.zeros((1, width), F32)
        for j, values in enumerate(found):
            total = jnp.where((me ^ j) == z, values, total)
        target[row : row + 1, z * width : (z + 1) * width] = total


def cross_input_backward(plan, vec, z_first, back, caption, query_back, whole_vc):
    mp, rows, half, width, items = plan.mp, plan.rows, plan.half, plan.width, plan.items

    def kernel(vec, z_first, back, caption, *rest):
        query_back, whole_vc = rest[:3], rest[3]
        first_back, sums, w_vc, sems = rest[4:]
        me = lax.axis_index("mp")
        fetch_whole(whole_vc, w_vc, sems.at[0])
        total = back[...]
        found = [column_sum(get_distance(query_back, j)) for j in range(mp)]
        put_columns(sums, 3, found, me, width)
        settle(w_vc, sems.at[0])
        for j in range(mp):
            total = total + dot_t(after(get_distance(query_back, j), width), w_vc[j])
        first_grad = join_halves(total, caption[...], items)
        normed, inverse = norm_parts(z_first[...])
        first = norm_backward(first_grad, normed, inverse, vec[4:5, :])
        first_back[...] = first
        sums[0:1, :] = column_sum(first_grad * normed)
        sums[1:2, :] = column_sum(first_grad)
        sums[2:3, :] = column_sum(first.astype(BF))

    return call(
        kernel,
        (vec, z_first, back, caption, *query_back, whole_vc),
        [VMEM] * 7 + [HBM],
        [
            jax.ShapeDtypeStruct((rows, D), F32),
            jax.ShapeDtypeStruct((4, D), F32),
        ],
        [VMEM] * 2,
        [pltpu.VMEM((mp, D, 2 * width), BF), DMA((1,))],
        20,
    )


def image_gradient(plan, images, kv_back):
    items, keys, features = images.shape
    width = plan.width
    even = keys // 128 * 128

    def kernel(images, kv_back, out, held, turned, sems):
        loaded, cut = load_images(images, held, sems)
        total = jnp.zeros((2 * width, features), F32)
        for i in range(items):
            turned[i] = kv_back[i, 0:even, :].T
        for i in range(items):
            if i % cut == 0:
                loaded[i // cut].wait()
            total = total + dot(turned[i], held[i, 0:even, :])
        if keys > even:
            left = jnp.concatenate([held[i, even:keys, :] for i in range(items)], axis=0)
            right = jnp.concatenate([kv_back[i, even:keys, :] for i in range(items)], axis=0)
            total = total + t_dot(right, left)
        out[...] = total.astype(BF).T

    return call(
        kernel,
        (images, kv_back),
        [HBM, VMEM],
        [jax.ShapeDtypeStruct((features, 2 * width), BF)],
        [VMEM],
        [
            pltpu.VMEM((items, keys, features), BF),
            pltpu.VMEM((items, 2 * width, even), BF),
            DMA((4,)),
        ],
        40,
    )[0]


def self_backward(plan, lengths, saved, found_sums, wholes):
    mp, rows, width = plan.mp, plan.rows, plan.width
    count = len(saved) + len(found_sums)
    vectors_rows = 16 + 2 * mp * (F // mp // D)

    def kernel(lengths, *rest):
        vec, first_back, qk_all, v_all = rest[:4]
        first_sums, cross_sums, third_sums, bias_sums, value_sum = rest[4:count]
        wholes, rest = rest[count : count + 3], rest[count + 3 :]
        token_back, vectors, maps_back, value_maps = rest[:4]
        w_qk, w_vc, w_oo, w_sems = rest[4:]
        me = lax.axis_index("mp")
        for k, target in enumerate((w_qk, w_vc, w_oo)):
            fetch_whole(wholes[k], target, w_sems.at[k])
        mask = self_mask(plan, lengths, me)
        lanes = head_lanes(width)
        group = me & 1
        vectors[...] = jnp.zeros((vectors_rows, D), F32)
        vectors[0:1, :] = first_sums[2:3, :]
        vectors[1:2, :] = cross_sums[0:1, :]
        vectors[pl.ds(2 + group, 1), :] = third_sums[0:1, :]
        vectors[4:6, :] = first_sums[0:2, :]
        vectors[6:8, :] = cross_sums[1:3, :]
        vectors[pl.ds(8 + 2 * group, 1), :] = third_sums[1:2, :]
        vectors[pl.ds(9 + 2 * group, 1), :] = third_sums[2:3, :]
        vectors[14:15, :] = first_sums[3:4, :]
        for z in range(mp):
            span = slice(z * width, (z + 1) * width)
            vectors[15:16, span] = jnp.where(me == z, value_sum[...], 0.0)
        for g in range(2):
            vectors[16 + g * mp : 16 + (g + 1) * mp, :] = jnp.where(
                group == g, bias_sums[...], 0.0
            )
        total = first_back[...]
        self_branch = total.astype(BF)
        settle(w_oo, w_sems.at[2])
        query_sums, value_sums = [], []
        for z in range(mp):
            pulled = dot(self_branch, w_oo[z]).astype(BF)[:, :width]
            q, k, v = qk_all[z][:, :width], qk_all[z][:, width:], v_all[z]
            query_grad = jnp.zeros((rows, width), F32)
            key_grad = jnp.zeros((rows, width), F32)
            value_grad = jnp.zeros((rows, width), F32)
            for lane in lanes:
                q_h, g_h = only(q, lane), only(pulled, lane)
                probs = softmax(dot_t(q_h, k) * SCALE + mask)
                wanted = dot_t(g_h, v)
                scored = probs * (wanted - jnp.sum(probs * wanted, axis=-1, keepdims=True))
                scored = scored.astype(BF)
                value_grad = value_grad + t_dot(probs.astype(BF), g_h)
                query_grad = query_grad + only(dot(scored, k), lane)
                key_grad = key_grad + t_dot(scored, q_h)
            query_grad = (query_grad * SCALE).astype(BF)
            value_grad = value_grad.astype(BF)
            query_sums.append(column_sum(query_grad))
            value_sums.append(column_sum(value_grad))
            both = wide(query_grad, (key_grad * SCALE).astype(BF))
            maps_back[z] = both
            value_maps[z] = value_grad
            if z == 0:
                settle(w_qk, w_sems.at[0])
                settle(w_vc, w_sems.at[1])
            total = total + dot_t(both, w_qk[z]) + dot_t(before(value_grad, width), w_vc[z])
        put_columns(vectors, 12, query_sums, me, width)
        put_columns(vectors, 13, value_sums, me, width)
        token_back[...] = total.astype(BF)

    return call(
        kernel,
        (lengths, *saved, *found_sums, *wholes),
        [SMEM] + [VMEM] * count + [HBM] * 3,
        [
            jax.ShapeDtypeStruct((rows, D), BF),
            jax.ShapeDtypeStruct((vectors_rows, D), F32),
            jax.ShapeDtypeStruct((mp, rows, 2 * width), BF),
            jax.ShapeDtypeStruct((mp, rows, width), BF),
        ],
        [VMEM] * 4,
        [pltpu.VMEM((mp, D, 2 * width), BF)] * 3 + [DMA((3,))],
        56,
    )


def output_gradient(plan, first_back, branch, context_all, contexts, gradients):
    mp, width = plan.mp, plan.width
    shapes = gradients.shapes()

    def kernel(first_back, branch, context_all, *rest):
        cross_context, grad_out = rest[:3], rest[3 : 3 + len(shapes)]
        g_oo, sems = rest[3 + len(shapes) :]
        branches_t = jnp.concatenate([first_back[...].astype(BF), branch[...]], axis=0).T
        for z in range(mp):
            contexts = jnp.concatenate(
                [
                    before(context_all[z], width),
                    after(get_distance(cross_context, z), width),
                ],
                axis=0,
            )
            g_oo[z] = dot(branches_t, contexts).astype(BF)
        gradients.write("oo", g_oo, grad_out, sems.at[0])
        settle(g_oo, sems.at[0])

    found = call(
        kernel,
        (first_back, branch, context_all, *contexts),
        [VMEM] * 6,
        shapes,
        [HBM] * len(shapes),
        [pltpu.VMEM((mp, D, 2 * width), BF), DMA((1,))],
        24,
    )
    return gradients.halves(found)


def self_gradient(plan, hidden, saved, gradients):
    mp, rows, half, width, items = plan.mp, plan.rows, plan.half, plan.width, plan.items
    shapes = gradients.shapes()
    count = len(saved)

    def kernel(hidden, *rest):
        vec, z_first, maps_back, value_maps = rest[:4]
        query_back = rest[4:7]
        grad_out = rest[count : count + len(shapes)]
        tokens, g_qk, g_vc, sems = rest[count + len(shapes) :]
        loaded = load_tokens(plan, hidden, tokens, sems.at[0])
        loaded.start()
        normed, _ = norm_parts(z_first[...])
        u = halves_of(normed * vec[4:5, :] + vec[5:6, :], items)[0].astype(BF)
        loaded.wait()
        inputs_t = jnp.concatenate([tokens[...].reshape(rows, D), u], axis=0).T
        for z in range(mp):
            g_qk[z] = dot(inputs_t[:, :rows], maps_back[z]).astype(BF)
        gradients.write("qk", g_qk, grad_out, sems.at[1])
        for z in range(mp):
            maps = jnp.concatenate(
                [before(value_maps[z], width), after(get_distance(query_back, z), width)], axis=0
            )
            g_vc[z] = dot(inputs_t, maps).astype(BF)
        gradients.write("vc", g_vc, grad_out, sems.at[2])
        settle(g_qk, sems.at[1])
        settle(g_vc, sems.at[2])

    found = call(
        kernel,
        (hidden, *saved),
        [HBM] + [VMEM] * count,
        shapes,
        [HBM] * len(shapes),
        [pltpu.VMEM((items, 2 * NQ, D), BF)]
        + [pltpu.VMEM((mp, D, 2 * width), BF)] * 2
        + [DMA((3,))],
        24,
    )
    return gradients.halves(found)


def place_layer(plan, two, across, far):
    mp, items = plan.mp, plan.items

    def kernel(two, across, far, out):
        me = lax.axis_index("mp")
        for j in range(mp):
            source = me ^ j
            values = two[j] if j < 2 else from_line(plan, across, far, j)
            for s in range(2):
                out[
                    pl.ds((source ^ s) * items, items),
                    pl.ds(pl.multiple_of((source & 1) * NQ, NQ), NQ),
                    :,
                ] = values[s]

    return call(
        kernel,
        (two, across, far),
        [VMEM] * 3,
        [jax.ShapeDtypeStruct((mp * items, 2 * NQ, D), BF)],
        [VMEM],
        [],
        16,
    )[0]


def place_gradient(plan, own, near, across_own, across_near, far_own, far_near):
    mp, items = plan.mp, plan.items

    def kernel(own, near, across_own, across_near, far_own, far_near, out):
        me = lax.axis_index("mp")
        end = (me == 0) | (me == mp - 1)
        found = [
            own[...],
            near[...],
            jnp.where(end, far_own[...], across_near[...]),
            jnp.where(end, far_near[...], across_own[...]),
        ]
        for j, values in enumerate(found):
            values = values.astype(F32).reshape(items, 2 * NQ, D)
            out[pl.ds((me ^ j) * items, items)] = values

    return call(
        kernel,
        (own, near, across_own, across_near, far_own, far_near),
        [VMEM] * 6,
        [jax.ShapeDtypeStruct((mp * items, 2 * NQ, D), F32)],
        [VMEM],
        [],
        24,
    )[0]


RATES = {
    "attn_in": 2.0 / math.sqrt(D),
    "attn_out": 2.0 / math.sqrt(max(D // 8, 1)),
    "cross_kv": 2.0 / math.sqrt(E),
    "ffn_up": 2.0 / math.sqrt(D),
    "ffn_down": 2.0 / math.sqrt(F),
    "vector": 0.3,
}


def adam_update(weight, first, second, grad, rate):
    first_new = BETA_ONE * first + (1.0 - BETA_ONE) * grad
    second_new = BETA_TWO * second + (1.0 - BETA_TWO) * grad * grad
    first_hat = first_new / (1.0 - BETA_ONE**STEP_COUNT)
    second_hat = second_new / (1.0 - BETA_TWO**STEP_COUNT)
    weight_new = weight - rate * (
        first_hat / (jnp.sqrt(second_hat) + ADAM_EPS) + WEIGHT_DECAY * weight
    )
    return (first_new, second_new, weight_new)


def update_into(held, outs, place, grad, rate):
    found = adam_update(held[0][place], held[1][place], held[2][place], grad, rate)
    for out, values in zip(outs, found):
        out[place] = values


def bring(sources, targets, sems):
    copies = [
        pltpu.make_async_copy(s, t, sems.at[k]) for k, (s, t) in enumerate(zip(sources, targets))
    ]
    for c in copies:
        c.start()
    return copies


def ffn_step(mine, theirs, up, down):
    rows = up[0].shape[1]

    def kernel(*refs):
        mine, theirs, sources, outs = refs[0], refs[1], refs[2:8], refs[8:14]
        held, sems = refs[14:20], refs[20]
        copies = bring(sources, held, sems)
        up, down = held[:3], held[3:]
        low = (lax.axis_index("mp") & 1) == 0
        own, other = mine[...].astype(F32), theirs[...].astype(F32)
        for copy in copies:
            copy.wait()
        for g in range(2):
            grad = jnp.where(low, own, other) if g == 0 else jnp.where(low, other, own)
            update_into(up, outs[:3], g, grad[:rows], RATES["ffn_up"])
            update_into(down, outs[3:], g, grad[rows:], RATES["ffn_down"])

    shapes = [jax.ShapeDtypeStruct(v.shape, F32) for v in up + down]
    return call(
        kernel,
        (mine, theirs, *up, *down),
        [VMEM] * 2 + [HBM] * 6,
        shapes,
        [VMEM] * 6,
        [pltpu.VMEM(v.shape, F32) for v in up + down] + [DMA((6,))],
        32,
    )


def other_steps(plan, pieces, kv_total, attn_in, out_turned, kv):
    width = plan.width
    rows = attn_in[0].shape[1]
    total = sum(p.astype(F32) for p in pieces)

    def columns(values):
        return jnp.stack([values[:, :width], values[:, width:]])

    in_grad = jnp.concatenate([columns(total[:rows]), columns(total[rows : 2 * rows])])
    found = adam_update(*attn_in, in_grad, RATES["attn_in"])
    turned = adam_update(*out_turned, columns(total[2 * rows :]), RATES["attn_out"])
    image = adam_update(*kv, columns(kv_total.astype(F32)), RATES["cross_kv"])
    return (*found, *(v.transpose(0, 2, 1) for v in turned), *image)


def vector_steps(plan, vectors, rep_, head, bias):
    me = lax.axis_index("mp")
    width, hidden_width = head[0].shape[1], bias[0].shape[1]
    head_grad = lax.dynamic_slice_in_dim(vectors[12:16], me * width, width, 1)
    bias_grad = lax.dynamic_slice_in_dim(
        vectors[16:].reshape(2, -1), me * hidden_width, hidden_width, 1
    )
    found = []
    for held, grad in ((rep_, vectors[:12]), (head, head_grad), (bias, bias_grad)):
        found.extend(adam_update(*held, grad, RATES["vector"]))
    return found


def local(
    bits,
    hidden,
    images,
    caption_len,
    cotangent,
    attn_in,
    attn_in_first,
    attn_in_second,
    attn_out,
    attn_out_first,
    attn_out_second,
    cross_key_value_maps,
    cross_kv_first,
    cross_kv_second,
    ffn_up,
    ffn_up_first,
    ffn_up_second,
    ffn_down,
    ffn_down_first,
    ffn_down_second,
    vec_rep,
    vec_rep_first,
    vec_rep_second,
    query_value_bias_rows,
    vec_head_first,
    vec_head_second,
    bias_up,
    bias_up_first,
    bias_up_second,
):
    mp = lax.axis_size("mp")
    me = lax.axis_index("mp")
    plan = Plan(bits, mp, hidden.shape[0] // mp, 2 ** (bits + 1))
    forth, back = plan.forth, plan.back
    low = (me & 1) == 0
    keys = images.shape[1]
    attn_rows, kv_rows, ffn_rows = attn_in.shape[1], cross_key_value_maps.shape[1], ffn_up.shape[1]
    oo_first = attn_rows // 32 * 16 or attn_rows // 2
    oo_second = attn_rows - oo_first

    def side(values):
        return jnp.concatenate([values[0], values[1]], axis=1)

    none = jnp.zeros_like(query_value_bias_rows[0])
    bias_rows = query_value_bias_rows
    packed = jnp.concatenate(
        [
            jnp.concatenate([bias_rows[0], none])[None],
            jnp.concatenate([bias_rows[1], bias_rows[2]])[None],
            jnp.concatenate([none, bias_rows[3]])[None],
            bias_up.reshape(-1, 2 * plan.width),
            jnp.zeros((1, 2 * plan.width), F32),
        ]
    )

    def three(values):
        found = []
        for _ in range(3):
            part = lax.reduce_precision(values, 8, 7)
            found.append(part.astype(BF))
            values = values - part
        return jnp.concatenate(found)

    low_in = attn_in.astype(BF)
    low_oo = side(attn_out.astype(BF).transpose(0, 2, 1))
    low_kv = side(cross_key_value_maps.astype(BF))
    attn_first, attn_second = attn_rows + oo_first, attn_rows + oo_second
    first_shard = jnp.concatenate(
        [
            side(low_in[:2]),
            low_oo[:oo_first],
            side(low_in[2:]),
            low_oo[oo_first:],
            three(packed),
        ]
    )
    group = me & 1
    low_ffn = jnp.concatenate([ffn_up.astype(BF), ffn_down.astype(BF).transpose(0, 2, 1)], axis=1)
    third_own = lax.dynamic_index_in_dim(low_ffn, group, 0, keepdims=False)
    third_other = lax.dynamic_index_in_dim(low_ffn, 1 - group, 0, keepdims=False)
    early, last = range(plan.bits - 1), range(plan.bits - 1, plan.bits)

    wide_columns, hidden_columns = 2 * plan.width, F // mp
    attn_parts = {
        "qk": [Part("a", 0, attn_rows, 0)],
        "vc": [Part("b", 0, attn_rows, 0)],
        "oo": [Part("a", attn_rows, oo_first, 0), Part("b", attn_rows, oo_second, oo_first)],
    }
    attn_gradients = Gradients(
        plan,
        {"a": (forth, attn_rows, wide_columns), "b": (back, attn_rows, wide_columns)},
        {"qk": (attn_parts["qk"], D), "vc": (attn_parts["vc"], D)},
        mp,
    )
    out_gradients = Gradients(
        plan,
        {"a": (forth, oo_first, wide_columns), "b": (back, oo_second, wide_columns)},
        {"oo": ([Part("a", 0, oo_first, 0), Part("b", 0, oo_second, oo_first)], D)},
        mp,
    )
    ffn_gradients = Gradients(
        plan,
        {"a": (forth, ffn_rows, hidden_columns), "b": (back, ffn_rows, hidden_columns)},
        {"up": ([Part("a", 0, ffn_rows, 0)], D), "down": ([Part("b", 0, ffn_rows, 0)], D)},
        mp,
    )

    first = mp_direct(plan, first_shard, lambda j: first_shard)
    maps = lax.all_gather(low_kv, forth + ("core",), axis=0, tiled=True)
    images = with_layout_constraint(images, Layout(major_to_minor=(0, 1, 2)))
    out_turned = tuple(
        v.transpose(0, 2, 1) for v in (attn_out, attn_out_first, attn_out_second)
    )
    first, images, third_own, third_other, out_turned = hold(
        first, images, third_own, third_other, out_turned
    )
    packed_rows = packed.shape[0]
    heads = jnp.stack([p[attn_first + attn_second :].astype(F32) for p in first])
    heads = heads.reshape(mp, 3, packed_rows, heads.shape[-1]).sum(axis=1)
    first = (
        jnp.stack([p[:attn_first] for p in first]),
        jnp.stack([p[attn_first : attn_first + attn_second] for p in first]),
    )
    near = mp_swap(third_other, 1)
    for k in early:
        got = send_pair(plan, first, k)
        if k < plan.bits - 2:
            first = join_pair(first, got)
    got, near = hold(got, near)
    first = join_pair(first, got)
    third = jnp.stack([third_own, near])
    got = send_pair(plan, first, plan.bits - 1)
    first_cores = send_cores(first)
    for distance in plan.distances[1:]:
        if distance > 2:
            third = mp_double(third, distance)
    far_up = mp_swap(third[:, :ffn_rows], 2)
    kv_all = image_maps(plan, images, packed, maps)
    got, first_cores, kv_all, far_up = hold(got, first_cores, kv_all, far_up)
    got_cores = send_cores(got)
    far_down = mp_swap(third[:, ffn_rows:], 2)

    def before_last(values, order):
        for axis in order[:-2]:
            values = jnp.concatenate([values, swap(values, axis)])
        return values, swap(values, order[-2])

    up, up_got = before_last(jnp.concatenate([third[:, :ffn_rows], far_up]), forth)
    (got_cores,) = hold(got_cores)
    attn_set = Weights(
        plan, as_trees(plan, as_quarters(first, got, first_cores, got_cores)), attn_parts
    )
    qk_all, v_all, context_all, z_first, cross, wholes = self_forward(
        plan, caption_len, hidden, vec_rep, heads, [(attn_set, ["qk", "vc", "oo"])]
    )
    whole_qk, whole_vc, whole_oo = wholes

    def exchange(values):
        return exchange_rest(values, mp_swap(values[2], 2))

    def exchange_rest(values, got):
        own, near, _ = values
        lane = lax.broadcasted_iota(jnp.int32, got.shape, 1)
        passed = mp_swap(jnp.where(lane < plan.width, near, got), 1)
        return own, passed, got

    far_down, cross, up_got = hold(far_down, cross, up_got)
    up = jnp.concatenate([up, up_got])
    down, down_got = before_last(jnp.concatenate([third[:, ffn_rows:], far_down]), back)
    queries = exchange(cross)
    (queries,) = hold(queries)
    contexts = cross_attend(plan, keys, queries, kv_all)
    contexts, down_got = hold(contexts, down_got)
    down = jnp.concatenate([down, down_got])
    half = up.shape[0] // 2
    up_last, down_last = swap(up[:half], forth[-1]), swap(down[:half], back[-1])
    context_got = mp_swap(contexts[2], 2)
    contexts, context_got, down, up, up_last, down_last = hold(
        contexts, context_got, down, up, up_last, down_last
    )
    contexts = exchange_rest(contexts, context_got)
    up_last = jnp.concatenate([up_last, swap(up[half:], forth[-1])])
    down_last = jnp.concatenate([down_last, swap(down[half:], back[-1])])
    (contexts,) = hold(contexts)
    up_core, down_core = send_cores((up, down))
    z_second, kept, given = cross_output(plan, vec_rep, z_first, contexts, whole_oo)
    kept, given = hold(kept, given)
    ffn_got = mp_swap(given, 1)
    up_last, down_last, up_core, down_core, ffn_got, kept = hold(
        up_last, down_last, up_core, down_core, ffn_got, kept
    )
    up_last_core, down_last_core = send_cores((up_last, down_last))
    up_last_core, down_last_core, ffn_got, kept = hold(
        up_last_core, down_last_core, ffn_got, kept
    )
    ffn_set = Weights(
        plan,
        as_trees(
            plan,
            (
                (up, up_last, up_core, up_last_core),
                (down, down_last, down_core, down_last_core),
            ),
        ),
        {"up": [Part("a", 0, ffn_rows, 0)], "down": [Part("b", 0, ffn_rows, 0)]},
    )
    layer, kept_back, given_back, third_sums, bias_sums, ffn_halves = feed_forward(
        plan,
        vec_rep,
        heads,
        kept,
        ffn_got,
        cotangent,
        [(ffn_set, ["up", "down"])],
        ffn_gradients,
    )
    cores = ("core", "core")
    ffn_state = ffn_halves["a"], ffn_halves["b"]
    got_back = mp_swap(given_back, 1)
    got = shrink_send(ffn_state, cores)
    got_back, got, kept_back, layer = hold(got_back, got, kept_back, layer)
    layer_near = mp_swap(layer, 1)
    ffn_state = shrink_add(ffn_state, got)
    for k in range(plan.bits - 1, 1, -1):
        ffn_state = shrink_add(ffn_state, shrink_send(ffn_state, (forth[k], back[k])))
    got = shrink_send(ffn_state, (forth[1], back[1]))
    cross_back, branch, caption_back, cross_sums, context_back = cross_output_backward(
        plan, vec_rep, z_second, kept_back, got_back, whole_oo
    )
    (context_back,) = hold(context_back)
    context_back = exchange(context_back)
    context_back, layer_near = hold(context_back, layer_near)
    layer_two = jnp.stack([layer, layer_near])
    layer_across = mp_middle(plan, layer_two)
    kv_back, value_sum, query_back = cross_attend_backward(
        plan, keys, queries, context_back, kv_all
    )
    query_back, got = hold(query_back, got)
    ffn_state = shrink_add(ffn_state, got)
    got = shrink_send(ffn_state, (forth[0], back[0]))
    kv_grad = image_gradient(plan, images, kv_back)
    query_back = exchange(query_back)
    query_back, got, layer_across, kv_grad = hold(query_back, got, layer_across, kv_grad)
    kv_total = lax.psum_scatter(
        kv_grad, forth + ("core",), scatter_dimension=0, tiled=True
    )
    ffn_state = join_trees(shrink_add(ffn_state, got))
    for distance in plan.distances[:1:-1]:
        ffn_state = mp_halve(ffn_state, distance)
    first_back, first_sums = cross_input_backward(
        plan, vec_rep, z_first, cross_back, caption_back, query_back, whole_vc
    )
    out_halves = output_gradient(plan, first_back, branch, context_all, contexts, out_gradients)
    ffn_state, first_back, out_halves = hold(ffn_state, first_back, out_halves)
    middle = ffn_rows if ffn_state[1].shape[0] == 2 else 0
    ffn_got_up = mp_swap(ffn_state[1][:, :middle], 2)
    layer_far = mp_outward(plan, layer_across)
    out_state = out_halves["a"], out_halves["b"]
    out_got = shrink_send(out_state, cores)
    token_back, vectors, maps_back, value_maps = self_backward(
        plan,
        caption_len,
        (vec_rep, first_back, qk_all, v_all),
        (first_sums, cross_sums, third_sums, bias_sums, value_sum),
        wholes,
    )
    token_back, maps_back, vectors, ffn_got_up, out_got, layer_far = hold(
        token_back, maps_back, vectors, ffn_got_up, out_got, layer_far
    )
    middle_down = (ffn_state[1].shape[1] + middle) // 2
    ffn_got_down = mp_swap(ffn_state[1][:, middle:middle_down], 2)
    across_own = mp_middle(plan, token_back)
    near = mp_swap(token_back, 1)
    out_state = shrink_add(out_state, out_got)
    for k in range(plan.bits - 1, 1, -1):
        out_state = shrink_add(out_state, shrink_send(out_state, (forth[k], back[k])))
    out_got = shrink_send(out_state, (forth[1], back[1]))
    attn_halves = self_gradient(
        plan,
        hidden,
        (vec_rep, z_first, maps_back, value_maps, *query_back),
        attn_gradients,
    )
    across_own, near, attn_halves, out_got, ffn_got_down = hold(
        across_own, near, attn_halves, out_got, ffn_got_down
    )
    attn_state = attn_halves["a"], attn_halves["b"]
    attn_got = shrink_send(attn_state, cores)
    ffn_got_rest = mp_swap(ffn_state[1][:, middle_down:], 2)
    out_state = shrink_add(out_state, out_got)
    out_got = shrink_send(out_state, (forth[0], back[0]))
    attn_got, out_got, ffn_got_rest, vectors = hold(attn_got, out_got, ffn_got_rest, vectors)
    across_near = mp_middle(plan, near)
    far_own = mp_outward(plan, across_own)
    attn_state = shrink_add(attn_state, attn_got)
    for k in range(plan.bits - 1, 1, -1):
        attn_state = shrink_add(attn_state, shrink_send(attn_state, (forth[k], back[k])))
    attn_got = shrink_send(attn_state, (forth[1], back[1]))
    out_state = shrink_add(out_state, out_got)
    vector_got = mp_swap(vectors, 1)
    attn_got, across_near, far_own, vector_got = hold(
        attn_got, across_near, far_own, vector_got
    )
    vectors = vectors + vector_got
    for distance in plan.distances[2:]:
        vectors = vectors + mp_swap(vectors, distance)
    vector_got = mp_swap(vectors, 2)
    attn_state = shrink_add(attn_state, attn_got)
    attn_got = shrink_send(attn_state, (forth[0], back[0]))
    far_near = mp_outward(plan, across_near)
    ffn_got = jnp.concatenate([ffn_got_up, ffn_got_down, ffn_got_rest], axis=1)
    half = ffn_got.shape[0] // 2
    ffn_state = (
        add_low(ffn_state[0][:half], ffn_got[:half]),
        add_low(ffn_state[0][half:], ffn_got[half:]),
    )
    theirs = mp_swap(ffn_state[1][0], 1)
    attn_got, vector_got, theirs, far_near = hold(attn_got, vector_got, theirs, far_near)
    attn_state = shrink_add(attn_state, attn_got)
    pieces = mp_scatter(plan, join_trees(attn_state + out_state))
    vectors = vectors + vector_got
    for axis in forth:
        vectors = vectors + swap(vectors, axis)
    grad_hidden = place_gradient(
        plan, token_back, near, across_own, across_near, far_own, far_near
    )
    layer_out = place_layer(plan, layer_two, layer_across, layer_far)
    turn = (0, 2, 1)
    ffn_results = ffn_step(
        ffn_state[0][0],
        theirs,
        (ffn_up, ffn_up_first, ffn_up_second),
        tuple(v.transpose(turn) for v in (ffn_down, ffn_down_first, ffn_down_second)),
    )
    vectors, grad_hidden, layer_out, ffn_results = hold(
        vectors, grad_hidden, layer_out, ffn_results
    )
    vectors = vectors + swap(vectors, "core")
    results = other_steps(
        plan,
        pieces,
        kv_total,
        (attn_in, attn_in_first, attn_in_second),
        out_turned,
        (cross_key_value_maps, cross_kv_first, cross_kv_second),
    )
    vector_results = vector_steps(
        plan,
        vectors,
        (vec_rep, vec_rep_first, vec_rep_second),
        (query_value_bias_rows, vec_head_first, vec_head_second),
        (bias_up, bias_up_first, bias_up_second),
    )
    return (
        layer_out,
        grad_hidden,
        *results,
        *ffn_results[:3],
        *(v.transpose(turn) for v in ffn_results[3:]),
        *vector_results,
    )


def solution(mesh):
    dp, mp = mesh.devices.shape
    bits = (dp // 2).bit_length() - 1
    names = tuple(f"b{k}" for k in range(bits)) + ("core",)
    fine = Mesh(mesh.devices.reshape((2,) * (bits + 1) + (mp,)), names + ("mp",))
    split = P(names)
    inward = P(None, names, "mp")
    outward = P(None, "mp", names)
    head = P(None, "mp")
    stored = (inward,) * 3 + (outward,) * 3 + (inward,) * 6 + (outward,) * 3 + (P(),) * 3 + (head,) * 6
    return jax.shard_map(
        functools.partial(local, bits),
        mesh=fine,
        in_specs=(split,) * 4 + stored,
        out_specs=(split,) * 2 + stored,
        check_vma=False,
    )
```

```python
import functools
import math

import jax
import jax.numpy as jnp
from jax import lax
from jax.experimental import pallas as pl
from jax.experimental.layout import Layout, with_layout_constraint
from jax.experimental.pallas import tpu as pltpu
from jax.sharding import Mesh
from jax.sharding import PartitionSpec as P

D = 768
HEAD_DIM = 64
F = 3072
E = 1408
NQ = 32
STEP_COUNT = 10

NORM_EPS = 1e-06
BETA_ONE = 0.9
BETA_TWO = 0.999
ADAM_EPS = 1e-08
WEIGHT_DECAY = 0.01
MASKED = -1000000000.0

BF = jnp.bfloat16
F32 = jnp.float32
SCALE = HEAD_DIM ** (-0.5)
MIB = 1 << 20


def dot(a, b):
    return lax.dot_general(a, b, (((1,), (0,)), ((), ())), preferred_element_type=F32)


def dot_t(a, b):
    return lax.dot_general(a, b, (((1,), (1,)), ((), ())), preferred_element_type=F32)


def t_dot(a, b):
    return lax.dot_general(a, b, (((0,), (0,)), ((), ())), preferred_element_type=F32)


def swap(values, axis):
    return lax.ppermute(values, axis, [(0, 1), (1, 0)])


def mp_swap(values, distance):
    count = lax.axis_size("mp")
    return lax.ppermute(values, "mp", [(i, i ^ distance) for i in range(count)])


class Plan:
    def __init__(self, bits, mp, items, dp):
        self.bits = bits
        self.mp = mp
        self.dp = dp
        self.items = items
        self.rows = items * 2 * NQ
        self.half = items * NQ
        self.width = D // mp
        self.forth = tuple(f"b{k}" for k in range(bits))
        self.back = self.forth[::-1]
        self.distances = [1 << k for k in range(mp.bit_length() - 1)]

    def bit(self, axis):
        return 1 if axis == "core" else 2 << (self.bits - 1 - int(axis[1:]))

    def masks(self, order):
        found = [0]
        for axis in order + ("core",):
            found = found + [m | self.bit(axis) for m in found]
        return found

    def dp_index(self):
        place = lax.axis_index("core")
        for axis in self.forth:
            place = place + self.bit(axis) * lax.axis_index(axis)
        return place


class Part:
    def __init__(self, tree, low, count, place):
        self.tree, self.low, self.count, self.place = tree, low, count, place


def hold(*values):
    return lax.optimization_barrier(values)


def mp_double(values, distance):
    return jnp.concatenate([values, mp_swap(values, distance)])


def mp_direct(plan, own, sent):
    return [own] + [mp_swap(sent(j), j) for j in range(1, plan.mp)]


def two_trees(pieces, rows):
    return (
        jnp.concatenate([p[None, :rows] for p in pieces]),
        jnp.concatenate([p[None, rows:] for p in pieces]),
    )


def send_pair(plan, pair, k):
    return swap(pair[0], plan.forth[k]), swap(pair[1], plan.back[k])


def send_cores(pair):
    return tuple(swap(v, "core") for v in pair)


def join_pair(pair, got):
    return tuple(jnp.concatenate([v, g]) for v, g in zip(pair, got))


def as_quarters(pair, got, cores, got_cores):
    return tuple(zip(pair, got, cores, got_cores))


def as_trees(plan, cores):
    return {"a": (cores[0], plan.forth), "b": (cores[1], plan.back)}


def line_pairs(plan):
    return [(1, 2), (2, 1)], [(0, 1), (3, 2)], [(1, 0), (2, 3)]


def mp_middle(plan, values):
    if plan.mp != 4:
        return mp_swap(values, 2)
    return lax.ppermute(values, "mp", line_pairs(plan)[0])


def mp_outward(plan, got):
    if plan.mp != 4:
        return got
    return lax.ppermute(got, "mp", line_pairs(plan)[2])


def from_line(plan, across, far, j):
    if plan.mp != 4:
        return across[j - 2]
    me = lax.axis_index("mp")
    return jnp.where((me == 0) | (me == 3), far[j - 2], across[3 - j])


def mp_inward(plan, state):
    kept, sent = state
    if plan.mp != 4:
        return state
    got = lax.ppermute(sent, "mp", line_pairs(plan)[1])
    return kept, add_low(sent, got[::-1])


def mp_across(plan, state):
    kept, sent = state
    if plan.mp != 4:
        return mp_halve(state, 2)
    got = lax.ppermute(sent, "mp", line_pairs(plan)[0])
    return add_low(kept[:1], got[1:]), add_low(kept[1:], got[:1])


def natural_tree(plan, halves, order):
    values = jnp.concatenate(halves)
    values = values.reshape((plan.dp, values.shape[0] // plan.dp) + values.shape[1:])
    back = [0] * plan.dp
    for k, mask in enumerate(plan.masks(order)):
        back[mask] = k
    places = jnp.take(jnp.array(back), jnp.arange(plan.dp) ^ plan.dp_index())
    return jnp.take(values, places, axis=0)


def assemble(plan, trees, parts):
    found = []
    for part in parts:
        halves, order = trees[part.tree]
        natural = natural_tree(plan, halves, order)
        found.append(natural[:, :, part.low : part.low + part.count])
    whole = jnp.concatenate(found, axis=2).transpose(1, 0, 2, 3)
    return whole.reshape(whole.shape[0], -1, whole.shape[-1])


def by_distance(plan, matrices, segments, order):
    places = jnp.array(plan.masks(order)) ^ plan.dp_index()
    found = []
    for name, part in segments:
        blocks = matrices[name]
        blocks = blocks.reshape(blocks.shape[0], plan.dp, -1, blocks.shape[-1])
        blocks = jnp.take(blocks, places, axis=1).transpose(1, 0, 2, 3)
        found.append(blocks[:, :, part.place : part.place + part.count])
    whole = jnp.concatenate(found, axis=2)
    whole = whole.reshape((-1,) + whole.shape[2:])
    return whole[: whole.shape[0] // 2], whole[whole.shape[0] // 2 :]


def add_low(first, second):
    return (first.astype(F32) + second.astype(F32)).astype(BF)


def shrink_send(halves, axes):
    return tuple(swap(sent, axis) for (_, sent), axis in zip(halves, axes))


def shrink_add(halves, found):
    sums = []
    for (kept, _), got in zip(halves, found):
        half = got.shape[0] // 2
        sums.append((add_low(kept[:half], got[:half]), add_low(kept[half:], got[half:])))
    return tuple(sums)


def join_trees(halves):
    return tuple(jnp.concatenate([h[k] for h in halves], axis=1) for k in range(2))


def mp_halve(state, distance):
    kept, sent = state
    got = mp_swap(sent, distance)
    half = got.shape[0] // 2
    return add_low(kept[:half], got[:half]), add_low(kept[half:], got[half:])


def mp_scatter(plan, state):
    kept, sent = state
    pieces = [kept[0]]
    for j in range(1, plan.mp):
        values = kept if j < plan.mp // 2 else sent
        pieces.append(mp_swap(values[j % (plan.mp // 2)], j))
    return pieces


def mp_last(state):
    kept, sent = state
    return kept[0].astype(F32), mp_swap(sent[0], 1).astype(F32)


def norm_parts(values):
    center = values - jnp.mean(values, axis=-1, keepdims=True)
    spread = jnp.mean(center * center, axis=-1, keepdims=True)
    inverse = lax.rsqrt(spread + NORM_EPS)
    return center * inverse, inverse


def norm_backward(grad_out, normed, inverse, gain):
    scaled = grad_out * gain
    inner = (
        scaled
        - jnp.mean(scaled, axis=-1, keepdims=True)
        - normed * jnp.mean(scaled * normed, axis=-1, keepdims=True)
    )
    return inner * inverse


def column_sum(values):
    return jnp.sum(values.astype(F32), axis=0, keepdims=True)


def halves_of(values, items):
    split = values.reshape(items, 2 * NQ, values.shape[-1])
    parts = split[:, :NQ], split[:, NQ:]
    return tuple(p.reshape(items * NQ, values.shape[-1]) for p in parts)


def join_halves(query, caption, items):
    width = query.shape[-1]
    parts = [v.reshape(items, NQ, width) for v in (query, caption)]
    return jnp.concatenate(parts, axis=1).reshape(items * 2 * NQ, width)


def wide(first, second):
    return jnp.concatenate([first, second], axis=1)


def after(values, width):
    return jnp.concatenate([jnp.zeros_like(values), values], axis=1)


def before(values, width):
    return jnp.concatenate([values, jnp.zeros_like(values)], axis=1)


def head_lanes(width):
    lane = lax.broadcasted_iota(jnp.int32, (1, width), 1)
    return [lane // HEAD_DIM == h for h in range(width // HEAD_DIM)]


def only(values, lanes):
    return jnp.where(lanes, values, jnp.zeros_like(values))


def softmax(scores):
    expo = jnp.exp(scores - jnp.max(scores, axis=-1, keepdims=True))
    return expo * (1.0 / jnp.sum(expo, axis=-1, keepdims=True))


def fetch(plan, refs, parts, trees, target, sem):
    if trees is None:
        pltpu.make_async_copy(refs[0], target, sem).start()
        return
    place = plan.dp_index()
    block = sum(p.count for p in parts)
    for part in parts:
        found, order = trees[part.tree]
        for k, mask in enumerate(plan.masks(order)):
            quarter, index = divmod(k, plan.dp // len(found))
            begin = pl.multiple_of((place ^ mask) * block + part.place, 16)
            pieces = refs[found[quarter]].at[pl.ds(index * plan.mp, plan.mp)]
            pltpu.make_async_copy(
                pieces.at[:, pl.ds(part.low, part.count), :],
                target.at[:, pl.ds(begin, part.count), :],
                sem,
            ).start()


def fetch_whole(matrix, target, sem):
    pltpu.make_async_copy(matrix, target, sem).start()


def settle(target, sem):
    pltpu.make_async_copy(target, target, sem).wait()


def spread(plan, source, parts, outs, sem):
    if parts is None:
        pltpu.make_async_copy(source, outs, sem).start()
        return
    place = plan.dp_index()
    block = sum(p.count for p in parts)
    for part in parts:
        halves, order = outs[part.tree]
        for k, mask in enumerate(plan.masks(order)):
            half, index = divmod(k, plan.dp // 2)
            begin = pl.multiple_of((place ^ mask) * block + part.place, 16)
            pieces = halves[half].at[pl.ds(index * plan.mp, plan.mp)]
            pltpu.make_async_copy(
                source.at[:, pl.ds(begin, part.count), :],
                pieces.at[:, pl.ds(part.low, part.count), :],
                sem,
            ).start()


class Weights:
    def __init__(self, plan, trees, matrices):
        self.plan, self.matrices = plan, matrices
        self.direct = all(p.count % 16 == 0 for parts in matrices.values() for p in parts)
        if self.direct:
            self.trees = trees
        else:
            self.whole = {n: assemble(plan, trees, parts) for n, parts in matrices.items()}

    def operands(self, names):
        arrays, found = [], {}
        if not self.direct:
            for name in names:
                found[name] = (len(arrays), self.matrices[name], None)
                arrays.append(self.whole[name])
            return arrays, found
        seen = {}
        for name in names:
            for part in self.matrices[name]:
                if part.tree not in seen:
                    halves, order = self.trees[part.tree]
                    seen[part.tree] = (range(len(arrays), len(arrays) + len(halves)), order)
                    arrays.extend(halves)
            found[name] = (0, self.matrices[name], seen)
        return arrays, found


def gather_operands(sets):
    arrays, starts = [], {}
    for weights, names in sets:
        more, found = weights.operands(names)
        base = len(arrays)
        for name, (place, parts, trees) in found.items():
            starts[name] = functools.partial(
                lambda refs, target, sem, base, place, parts, trees, plan: fetch(
                    plan, refs[base + place :], parts, trees, target, sem
                )
                if trees is None
                else fetch(plan, refs[base:], parts, trees, target, sem),
                base=base,
                place=place,
                parts=parts,
                trees=trees,
                plan=weights.plan,
            )
        arrays.extend(more)
    return arrays, starts


class Gradients:
    def __init__(self, plan, trees, matrices, over):
        self.plan, self.trees, self.matrices, self.over = plan, trees, matrices, over
        self.direct = all(p.count % 16 == 0 for parts, _ in matrices.values() for p in parts)

    def shapes(self):
        found = []
        if self.direct:
            for _, rows, columns in self.trees.values():
                shape = (self.plan.dp // 2 * self.over, rows, columns)
                found += [jax.ShapeDtypeStruct(shape, BF)] * 2
            return found
        for parts, rows in self.matrices.values():
            columns = self.trees[parts[0].tree][2]
            found.append(jax.ShapeDtypeStruct((self.over, rows, columns), BF))
        return found

    def write(self, name, source, refs, sem):
        parts = self.matrices[name][0]
        if self.direct:
            outs = {
                tree: (refs[2 * k : 2 * k + 2], order)
                for k, (tree, (order, _, _)) in enumerate(self.trees.items())
            }
            spread(self.plan, source, parts, outs, sem)
        else:
            spread(self.plan, source, None, refs[list(self.matrices).index(name)], sem)

    def halves(self, arrays):
        if self.direct:
            return {t: tuple(arrays[2 * k : 2 * k + 2]) for k, t in enumerate(self.trees)}
        named = dict(zip(self.matrices, arrays))
        found = {}
        for tree, (order, _, _) in self.trees.items():
            segments = [
                (name, part)
                for name, (parts, _) in self.matrices.items()
                for part in parts
                if part.tree == tree
            ]
            segments.sort(key=lambda s: s[1].low)
            found[tree] = by_distance(self.plan, named, segments, order)
        return found


def call(kernel, ins, places, outs, out_places, scratch, limit):
    return pl.pallas_call(
        kernel,
        out_shape=outs,
        in_specs=[pl.BlockSpec(memory_space=p) for p in places],
        out_specs=[pl.BlockSpec(memory_space=p) for p in out_places],
        scratch_shapes=scratch,
        compiler_params=pltpu.CompilerParams(vmem_limit_bytes=limit * MIB),
        cost_estimate=pl.CostEstimate(flops=1000, bytes_accessed=1000, transcendentals=0),
    )(*ins)


ANY, HBM, VMEM, SMEM = pl.ANY, pltpu.HBM, pltpu.VMEM, pltpu.SMEM
DMA = pltpu.SemaphoreType.DMA


def self_mask(plan, lengths, me):
    count = plan.rows
    row = lax.broadcasted_iota(jnp.int32, (count, count), 0)
    col = lax.broadcasted_iota(jnp.int32, (count, count), 1)
    span = 2 * NQ
    limit = jnp.zeros((count, count), jnp.int32)
    for i in range(plan.items):
        limit = jnp.where(col // span == i, lengths[me * plan.items + i], limit)
    inside = col % span
    valid = (row // span == col // span) & ((inside < NQ) | (inside - NQ < limit))
    return jnp.where(valid, 0.0, MASKED).astype(F32)


def load_tokens(plan, hidden, target, sem):
    me = lax.axis_index("mp")
    return pltpu.make_async_copy(hidden.at[pl.ds(me * plan.items, plan.items)], target, sem)


def distance_shapes(plan):
    both = jax.ShapeDtypeStruct((plan.half, 2 * plan.width), BF)
    return [jax.ShapeDtypeStruct((plan.half, plan.width), BF), both, both]


def put_distance(refs, j, values):
    width = values.shape[1]
    if j == 0:
        refs[0][...] = values
    elif j == 1:
        refs[1][...] = before(values, width)
    else:
        refs[2][:, (j - 2) * width : (j - 1) * width] = values


def get_distance(refs, j, span=slice(None)):
    width = refs[0].shape[1]
    if j == 0:
        return refs[0][span, :]
    if j == 2:
        return refs[2][span, :width]
    return refs[1][span, :width] if j == 1 else refs[1][span, width:]


def self_forward(plan, lengths, hidden, vec, heads, sets):
    arrays, starts = gather_operands(sets)
    count = len(arrays)
    mp, rows, half, width, items = plan.mp, plan.rows, plan.half, plan.width, plan.items

    def kernel(lengths, hidden, vec, heads, *rest):
        refs = rest[:count]
        qk_out, v_out, context_out, z_out = rest[count : count + 4]
        cross = rest[count + 4 : count + 7]
        wholes = rest[count + 7 : count + 10]
        tokens, w_qk, w_vc, w_oo, sems = rest[count + 10 :]
        me = lax.axis_index("mp")
        loaded = load_tokens(plan, hidden, tokens, sems.at[0])
        loaded.start()
        starts["qk"](refs, w_qk, sems.at[1])
        starts["vc"](refs, w_vc, sems.at[2])
        starts["oo"](refs, w_oo, sems.at[3])
        mask = self_mask(plan, lengths, me)
        lanes = head_lanes(width)
        loaded.wait()
        x = tokens[...].reshape(rows, D)
        total = x.astype(F32) + vec[0:1, :]
        kept = []

        def arrive(k, matrix):
            settle(matrix, sems.at[1 + k])
            kept.append(pltpu.make_async_copy(matrix, wholes[k], sems.at[4 + k]))
            kept[-1].start()

        arrive(0, w_qk)
        for j in range(mp):
            both = (dot(x, w_qk[j]) + heads[j, 0:1, :]).astype(BF)
            qk_out[j] = both
            q, k = both[:, :width], both[:, width:]
            if j == 0:
                arrive(1, w_vc)
            v = (dot(x, w_vc[j]) + heads[j, 1:2, :]).astype(BF)[:, :width]
            v_out[j] = v
            context = jnp.zeros((rows, width), F32)
            for lane in lanes:
                probs = softmax(dot_t(only(q, lane), k) * SCALE + mask)
                context = context + only(dot(probs.astype(BF), v), lane)
            context = context.astype(BF)
            context_out[j] = context
            if j == 0:
                arrive(2, w_oo)
            total = total + dot_t(before(context, width), w_oo[j])
        z_out[...] = total
        normed, _ = norm_parts(total)
        u = halves_of(normed * vec[4:5, :] + vec[5:6, :], items)[0].astype(BF)
        for j in range(mp):
            maps = (dot(u, w_vc[j]) + heads[j, 1:2, :]).astype(BF)
            put_distance(cross, j, maps[:, width:])
        for copy in kept:
            copy.wait()

    whole = jax.ShapeDtypeStruct((mp, D, 2 * width), BF)
    outs = [
        jax.ShapeDtypeStruct((mp, rows, 2 * width), BF),
        jax.ShapeDtypeStruct((mp, rows, width), BF),
        jax.ShapeDtypeStruct((mp, rows, width), BF),
        jax.ShapeDtypeStruct((rows, D), F32),
        *distance_shapes(plan),
        whole,
        whole,
        whole,
    ]
    found = call(
        kernel,
        (lengths, hidden, vec, heads, *arrays),
        [SMEM, HBM, VMEM, VMEM] + [ANY] * count,
        outs,
        [VMEM] * 7 + [HBM] * 3,
        [
            pltpu.VMEM((items, 2 * NQ, D), BF),
            *[pltpu.VMEM((mp, D, 2 * width), BF)] * 3,
            DMA((7,)),
        ],
        28,
    )
    return (*found[:4], found[4:7], found[7:])


def load_images(images, held, sems):
    count = images.shape[0]
    cut = -(-count // 4)
    found = []
    for k in range(0, count, cut):
        span = pl.ds(k, min(cut, count - k))
        found.append(pltpu.make_async_copy(images.at[span], held.at[span], sems.at[k // cut]))
        found[-1].start()
    return found, cut


def image_maps(plan, images, bias, maps):
    items, keys, features = images.shape
    width = plan.width
    padded = -(-keys // 128) * 128

    def kernel(images, bias, maps, out, held, w_kv, sems, w_sem):
        weights = pltpu.make_async_copy(maps, w_kv, w_sem.at[0])
        weights.start()
        loaded, cut = load_images(images, held, sems)
        weights.wait()
        for n, copy in enumerate(loaded):
            copy.wait()

            def step(i, carry):
                both = (dot(held[i], w_kv[...]) + bias[2:3, :]).astype(BF)
                out[i, 0:keys, :] = both
                out[i, keys:padded, :] = jnp.zeros((padded - keys, 2 * width), BF)
                return carry

            lax.fori_loop(n * cut, min(items, (n + 1) * cut), step, 0)

    return call(
        kernel,
        (images, bias, maps),
        [ANY, VMEM, ANY],
        [jax.ShapeDtypeStruct((items, padded, 2 * width), BF)],
        [VMEM],
        [
            pltpu.VMEM((items, keys, features), BF),
            pltpu.VMEM((features, 2 * width), BF),
            DMA((4,)),
            DMA((1,)),
        ],
        28,
    )[0]


def key_mask(plan, keys, padded):
    lane = lax.broadcasted_iota(jnp.int32, (1, padded), 1)
    return jnp.where(lane < keys, 0.0, MASKED).astype(F32)


def spread_heads(values, lanes):
    return jnp.concatenate([only(values, lane) for lane in lanes], axis=0)


def gather_heads(values, lanes):
    total = None
    for h, lane in enumerate(lanes):
        part = only(values[h * NQ : (h + 1) * NQ], lane)
        total = part if total is None else total + part
    return total


def cross_attend(plan, keys, queries, kv):
    mp, half, width, items = plan.mp, plan.half, plan.width, plan.items
    padded = kv.shape[1]

    def kernel(*refs):
        queries, kv, contexts = refs[:3], refs[3], refs[4:]
        me = lax.axis_index("mp")
        lanes = head_lanes(width)
        mask = key_mask(plan, keys, padded)
        for j in range(mp):
            rows = []
            for i in range(items):
                q = spread_heads(get_distance(queries, j, slice(i * NQ, (i + 1) * NQ)), lanes)
                both = kv[(me ^ j) * items + i]
                probs = softmax(dot_t(q, both[:, :width]) * SCALE + mask)
                rows.append(gather_heads(dot(probs.astype(BF), both[:, width:]), lanes))
            put_distance(contexts, j, jnp.concatenate(rows, axis=0).astype(BF))

    return call(
        kernel,
        (*queries, kv),
        [VMEM] * 4,
        distance_shapes(plan),
        [VMEM] * 3,
        [],
        24,
    )


def cross_output(plan, vec, z_first, contexts, whole_oo):
    mp, half, width, items = plan.mp, plan.half, plan.width, plan.items

    def kernel(vec, z_first, *rest):
        contexts, whole_oo = rest[:3], rest[3]
        z_out, kept, given, w_oo, sems = rest[4:]
        me = lax.axis_index("mp")
        fetch_whole(whole_oo, w_oo, sems.at[0])
        normed, _ = norm_parts(z_first[...])
        query, caption = halves_of(normed * vec[4:5, :] + vec[5:6, :], items)
        total = query + vec[1:2, :]
        settle(w_oo, sems.at[0])
        for j in range(mp):
            total = total + dot_t(after(get_distance(contexts, j), width), w_oo[j])
        z_out[...] = total
        normed, _ = norm_parts(total)
        second = normed * vec[6:7, :] + vec[7:8, :]
        low = (me & 1) == 0
        kept[...] = jnp.where(low, second, caption)
        given[...] = jnp.where(low, caption, second).astype(BF)

    return call(
        kernel,
        (vec, z_first, *contexts, whole_oo),
        [VMEM] * 5 + [HBM],
        [
            jax.ShapeDtypeStruct((half, D), F32),
            jax.ShapeDtypeStruct((half, D), F32),
            jax.ShapeDtypeStruct((half, D), BF),
        ],
        [VMEM] * 3,
        [pltpu.VMEM((mp, D, 2 * width), BF), DMA((1,))],
        16,
    )


def feed_forward(plan, vec, heads, kept, got, cotangent, sets, gradients):
    arrays, starts = gather_operands(sets)
    count = len(arrays)
    mp, half, items = plan.mp, plan.half, plan.items
    hidden_width = F // mp
    shapes = gradients.shapes()

    def kernel(vec, heads, kept, got, cotangent, *rest):
        refs, rest = rest[:count], rest[count:]
        layer, kept_back, given_back, sums, bias_sums = rest[:5]
        grad_out = rest[5 : 5 + len(shapes)]
        top, w_up, w_down, slope, act, up_grad, down_grad, w_sems, sems = rest[5 + len(shapes) :]
        me = lax.axis_index("mp")
        group = me & 1
        starts["up"](refs, w_up, w_sems.at[0])
        starts["down"](refs, w_down, w_sems.at[1])
        tops = []
        for s in range(2):
            first = (me ^ s) * items
            tops.append(
                pltpu.make_async_copy(
                    cotangent.at[
                        pl.ds(first, items), pl.ds(pl.multiple_of(group * NQ, NQ), NQ), :
                    ],
                    top.at[s],
                    sems.at[2 + s],
                )
            )
            tops[-1].start()
        x = jnp.concatenate([kept[...], got[...].astype(F32)], axis=0)
        low = x.astype(BF)
        low_t = low.T
        total = x + vec[pl.ds(2 + group, 1), :]
        settle(w_up, w_sems.at[0])
        for z in range(mp):
            bias = wide(
                heads[z, pl.ds(3 + 2 * group, 1), :], heads[z, pl.ds(4 + 2 * group, 1), :]
            )
            pre = dot(low, w_up[z]) + bias
            cdf = 0.5 + 0.5 * lax.erf(pre * (0.5**0.5))
            value = (pre * cdf).astype(BF)
            act[z] = value
            slope[z] = cdf + pre * jnp.exp(-0.5 * pre * pre) * (1.0 / math.sqrt(2.0 * math.pi))
        settle(w_down, w_sems.at[1])
        for z in range(mp):
            total = total + dot_t(act[z], w_down[z])
        normed, inverse = norm_parts(total)
        gain = vec[pl.ds(8 + 2 * group, 1), :]
        third = normed * gain + vec[pl.ds(9 + 2 * group, 1), :]
        layer[...] = third.astype(BF).reshape(2, items, NQ, D)
        for t in tops:
            t.wait()
        grad = top[...].reshape(2 * half, D).astype(F32)
        back = norm_backward(grad, normed, inverse, gain)
        branch = back.astype(BF)
        sums[0:1, :] = column_sum(branch)
        sums[1:2, :] = column_sum(grad * normed)
        sums[2:3, :] = column_sum(grad)
        branch_t = branch.T
        for z in range(mp):
            down_grad[z] = dot(branch_t, act[z]).astype(BF)
        gradients.write("down", down_grad, grad_out, sems.at[0])
        for z in range(mp):
            pull = (dot(branch, w_down[z]) * slope[z]).astype(BF)
            bias_sums[pl.ds(me ^ z, 1), :] = column_sum(pull)
            up_grad[z] = dot(low_t, pull).astype(BF)
            back = back + dot_t(pull, w_up[z])
        gradients.write("up", up_grad, grad_out, sems.at[1])
        kept_back[...] = back[:half]
        given_back[...] = back[half:].astype(BF)
        settle(down_grad, sems.at[0])
        settle(up_grad, sems.at[1])

    outs = [
        jax.ShapeDtypeStruct((2, items, NQ, D), BF),
        jax.ShapeDtypeStruct((half, D), F32),
        jax.ShapeDtypeStruct((half, D), BF),
        jax.ShapeDtypeStruct((3, D), F32),
        jax.ShapeDtypeStruct((mp, hidden_width), F32),
        *shapes,
    ]
    found = call(
        kernel,
        (vec, heads, kept, got, cotangent, *arrays),
        [VMEM] * 4 + [HBM] + [ANY] * count,
        outs,
        [VMEM] * 5 + [HBM] * len(shapes),
        [
            pltpu.VMEM((2, items, NQ, D), BF),
            pltpu.VMEM((mp, D, hidden_width), BF),
            pltpu.VMEM((mp, D, hidden_width), BF),
            pltpu.VMEM((mp, 2 * half, hidden_width), F32),
            pltpu.VMEM((mp, 2 * half, hidden_width), BF),
            pltpu.VMEM((mp, D, hidden_width), BF),
            pltpu.VMEM((mp, D, hidden_width), BF),
            DMA((2,)),
            DMA((4,)),
        ],
        48,
    )
    return (*found[:5], gradients.halves(found[5:]))


def cross_output_backward(plan, vec, z_second, kept, got, whole_oo):
    mp, half, width = plan.mp, plan.half, plan.width

    def kernel(vec, z_second, kept, got, whole_oo, *rest):
        back_out, branch_out, caption, sums = rest[:4]
        context_back = rest[4:7]
        w_oo, sems = rest[7:]
        low = (lax.axis_index("mp") & 1) == 0
        fetch_whole(whole_oo, w_oo, sems.at[0])
        other = got[...].astype(F32)
        grad = jnp.where(low, kept[...], other)
        caption[...] = jnp.where(low, other, kept[...])
        normed, inverse = norm_parts(z_second[...])
        back = norm_backward(grad, normed, inverse, vec[6:7, :])
        branch = back.astype(BF)
        back_out[...] = back
        branch_out[...] = branch
        sums[0:1, :] = column_sum(branch)
        sums[1:2, :] = column_sum(grad * normed)
        sums[2:3, :] = column_sum(grad)
        settle(w_oo, sems.at[0])
        for j in range(mp):
            put_distance(context_back, j, dot(branch, w_oo[j]).astype(BF)[:, width:])

    found = call(
        kernel,
        (vec, z_second, kept, got, whole_oo),
        [VMEM] * 4 + [HBM],
        [
            jax.ShapeDtypeStruct((half, D), F32),
            jax.ShapeDtypeStruct((half, D), BF),
            jax.ShapeDtypeStruct((half, D), F32),
            jax.ShapeDtypeStruct((3, D), F32),
            *distance_shapes(plan),
        ],
        [VMEM] * 7,
        [pltpu.VMEM((mp, D, 2 * width), BF), DMA((1,))],
        16,
    )
    return (*found[:4], found[4:])


def cross_attend_backward(plan, keys, queries, context_back, kv):
    mp, half, width, items = plan.mp, plan.half, plan.width, plan.items
    padded = kv.shape[1]

    def kernel(*refs):
        queries, context_back, kv = refs[:3], refs[3:6], refs[6]
        kv_back, value_sum, query_back = refs[7], refs[8], refs[9:]
        me = lax.axis_index("mp")
        lanes = head_lanes(width)
        mask = key_mask(plan, keys, padded)
        total = jnp.zeros((1, width), F32)
        for j in range(mp):
            rows = []
            for i in range(items):
                span = slice(i * NQ, (i + 1) * NQ)
                item = (me ^ j) * items + i
                q = spread_heads(get_distance(queries, j, span), lanes)
                g = spread_heads(get_distance(context_back, j, span), lanes)
                both = kv[item]
                k, v = both[:, :width], both[:, width:]
                probs = softmax(dot_t(q, k) * SCALE + mask)
                pulled = dot_t(g, v)
                scored = probs * (pulled - jnp.sum(probs * pulled, axis=-1, keepdims=True))
                scored = scored.astype(BF)
                value_back = t_dot(probs.astype(BF), g).astype(BF)
                key_back = (t_dot(scored, q) * SCALE).astype(BF)
                kv_back[item] = wide(key_back, value_back)
                total = total + column_sum(value_back)
                rows.append(gather_heads(dot(scored, k), lanes) * SCALE)
            put_distance(query_back, j, jnp.concatenate(rows, axis=0).astype(BF))
        value_sum[...] = total

    found = call(
        kernel,
        (*queries, *context_back, kv),
        [VMEM] * 7,
        [
            jax.ShapeDtypeStruct((mp * items, padded, 2 * width), BF),
            jax.ShapeDtypeStruct((1, width), F32),
            *distance_shapes(plan),
        ],
        [VMEM] * 5,
        [],
        28,
    )
    return found[0], found[1], found[2:]


def put_columns(target, row, found, me, width):
    for z in range(len(found)):
        total = jnp.zeros((1, width), F32)
        for j, values in enumerate(found):
            total = jnp.where((me ^ j) == z, values, total)
        target[row : row + 1, z * width : (z + 1) * width] = total


def cross_input_backward(plan, vec, z_first, back, caption, query_back, whole_vc):
    mp, rows, half, width, items = plan.mp, plan.rows, plan.half, plan.width, plan.items

    def kernel(vec, z_first, back, caption, *rest):
        query_back, whole_vc = rest[:3], rest[3]
        first_back, sums, w_vc, sems = rest[4:]
        me = lax.axis_index("mp")
        fetch_whole(whole_vc, w_vc, sems.at[0])
        total = back[...]
        found = [column_sum(get_distance(query_back, j)) for j in range(mp)]
        put_columns(sums, 3, found, me, width)
        settle(w_vc, sems.at[0])
        for j in range(mp):
            total = total + dot_t(after(get_distance(query_back, j), width), w_vc[j])
        first_grad = join_halves(total, caption[...], items)
        normed, inverse = norm_parts(z_first[...])
        first = norm_backward(first_grad, normed, inverse, vec[4:5, :])
        first_back[...] = first
        sums[0:1, :] = column_sum(first_grad * normed)
        sums[1:2, :] = column_sum(first_grad)
        sums[2:3, :] = column_sum(first.astype(BF))

    return call(
        kernel,
        (vec, z_first, back, caption, *query_back, whole_vc),
        [VMEM] * 7 + [HBM],
        [
            jax.ShapeDtypeStruct((rows, D), F32),
            jax.ShapeDtypeStruct((4, D), F32),
        ],
        [VMEM] * 2,
        [pltpu.VMEM((mp, D, 2 * width), BF), DMA((1,))],
        20,
    )


def image_gradient(plan, images, kv_back):
    items, keys, features = images.shape
    width = plan.width
    even = keys // 128 * 128

    def kernel(images, kv_back, out, held, turned, sems):
        loaded, cut = load_images(images, held, sems)
        total = jnp.zeros((2 * width, features), F32)
        for i in range(items):
            turned[i] = kv_back[i, 0:even, :].T
        for i in range(items):
            if i % cut == 0:
                loaded[i // cut].wait()
            total = total + dot(turned[i], held[i, 0:even, :])
        if keys > even:
            left = jnp.concatenate([held[i, even:keys, :] for i in range(items)], axis=0)
            right = jnp.concatenate([kv_back[i, even:keys, :] for i in range(items)], axis=0)
            total = total + t_dot(right, left)
        out[...] = total.astype(BF).T

    return call(
        kernel,
        (images, kv_back),
        [HBM, VMEM],
        [jax.ShapeDtypeStruct((features, 2 * width), BF)],
        [VMEM],
        [
            pltpu.VMEM((items, keys, features), BF),
            pltpu.VMEM((items, 2 * width, even), BF),
            DMA((4,)),
        ],
        40,
    )[0]


def self_backward(plan, lengths, saved, found_sums, wholes):
    mp, rows, width = plan.mp, plan.rows, plan.width
    count = len(saved) + len(found_sums)
    vectors_rows = 16 + 2 * mp * (F // mp // D)

    def kernel(lengths, *rest):
        vec, first_back, qk_all, v_all = rest[:4]
        first_sums, cross_sums, third_sums, bias_sums, value_sum = rest[4:count]
        wholes, rest = rest[count : count + 3], rest[count + 3 :]
        token_back, vectors, maps_back, value_maps = rest[:4]
        w_qk, w_vc, w_oo, w_sems = rest[4:]
        me = lax.axis_index("mp")
        for k, target in ((2, w_oo), (0, w_qk), (1, w_vc)):
            fetch_whole(wholes[k], target, w_sems.at[k])
        mask = self_mask(plan, lengths, me)
        lanes = head_lanes(width)
        group = me & 1
        vectors[...] = jnp.zeros((vectors_rows, D), F32)
        vectors[0:1, :] = first_sums[2:3, :]
        vectors[1:2, :] = cross_sums[0:1, :]
        vectors[pl.ds(2 + group, 1), :] = third_sums[0:1, :]
        vectors[4:6, :] = first_sums[0:2, :]
        vectors[6:8, :] = cross_sums[1:3, :]
        vectors[pl.ds(8 + 2 * group, 1), :] = third_sums[1:2, :]
        vectors[pl.ds(9 + 2 * group, 1), :] = third_sums[2:3, :]
        vectors[14:15, :] = first_sums[3:4, :]
        for z in range(mp):
            span = slice(z * width, (z + 1) * width)
            vectors[15:16, span] = jnp.where(me == z, value_sum[...], 0.0)
        for g in range(2):
            vectors[16 + g * mp : 16 + (g + 1) * mp, :] = jnp.where(
                group == g, bias_sums[...], 0.0
            )
        total = first_back[...]
        self_branch = total.astype(BF)
        settle(w_oo, w_sems.at[2])
        query_sums, value_sums = [], []
        for z in range(mp):
            pulled = dot(self_branch, w_oo[z]).astype(BF)[:, :width]
            q, k, v = qk_all[z][:, :width], qk_all[z][:, width:], v_all[z]
            query_grad = jnp.zeros((rows, width), F32)
            key_grad = jnp.zeros((rows, width), F32)
            value_grad = jnp.zeros((rows, width), F32)
            for lane in lanes:
                q_h, g_h = only(q, lane), only(pulled, lane)
                probs = softmax(dot_t(q_h, k) * SCALE + mask)
                wanted = dot_t(g_h, v)
                scored = probs * (wanted - jnp.sum(probs * wanted, axis=-1, keepdims=True))
                scored = scored.astype(BF)
                value_grad = value_grad + t_dot(probs.astype(BF), g_h)
                query_grad = query_grad + only(dot(scored, k), lane)
                key_grad = key_grad + t_dot(scored, q_h)
            query_grad = (query_grad * SCALE).astype(BF)
            value_grad = value_grad.astype(BF)
            query_sums.append(column_sum(query_grad))
            value_sums.append(column_sum(value_grad))
            both = wide(query_grad, (key_grad * SCALE).astype(BF))
            maps_back[z] = both
            value_maps[z] = value_grad
            if z == 0:
                settle(w_qk, w_sems.at[0])
                settle(w_vc, w_sems.at[1])
            total = total + dot_t(both, w_qk[z]) + dot_t(before(value_grad, width), w_vc[z])
        put_columns(vectors, 12, query_sums, me, width)
        put_columns(vectors, 13, value_sums, me, width)
        token_back[...] = total.astype(BF)

    return call(
        kernel,
        (lengths, *saved, *found_sums, *wholes),
        [SMEM] + [VMEM] * count + [HBM] * 3,
        [
            jax.ShapeDtypeStruct((rows, D), BF),
            jax.ShapeDtypeStruct((vectors_rows, D), F32),
            jax.ShapeDtypeStruct((mp, rows, 2 * width), BF),
            jax.ShapeDtypeStruct((mp, rows, width), BF),
        ],
        [VMEM] * 4,
        [pltpu.VMEM((mp, D, 2 * width), BF)] * 3 + [DMA((3,))],
        56,
    )


def output_gradient(plan, first_back, branch, context_all, contexts, gradients):
    mp, width = plan.mp, plan.width
    shapes = gradients.shapes()

    def kernel(first_back, branch, context_all, *rest):
        cross_context, grad_out = rest[:3], rest[3 : 3 + len(shapes)]
        g_oo, sems = rest[3 + len(shapes) :]
        branches_t = jnp.concatenate([first_back[...].astype(BF), branch[...]], axis=0).T
        for z in range(mp):
            contexts = jnp.concatenate(
                [
                    before(context_all[z], width),
                    after(get_distance(cross_context, z), width),
                ],
                axis=0,
            )
            g_oo[z] = dot(branches_t, contexts).astype(BF)
        gradients.write("oo", g_oo, grad_out, sems.at[0])
        settle(g_oo, sems.at[0])

    found = call(
        kernel,
        (first_back, branch, context_all, *contexts),
        [VMEM] * 6,
        shapes,
        [HBM] * len(shapes),
        [pltpu.VMEM((mp, D, 2 * width), BF), DMA((1,))],
        24,
    )
    return gradients.halves(found)


def self_gradient(plan, hidden, saved, gradients):
    mp, rows, half, width, items = plan.mp, plan.rows, plan.half, plan.width, plan.items
    shapes = gradients.shapes()
    count = len(saved)

    def kernel(hidden, *rest):
        vec, z_first, maps_back, value_maps = rest[:4]
        query_back = rest[4:7]
        grad_out = rest[count : count + len(shapes)]
        tokens, g_qk, g_vc, sems = rest[count + len(shapes) :]
        loaded = load_tokens(plan, hidden, tokens, sems.at[0])
        loaded.start()
        normed, _ = norm_parts(z_first[...])
        u = halves_of(normed * vec[4:5, :] + vec[5:6, :], items)[0].astype(BF)
        loaded.wait()
        inputs_t = jnp.concatenate([tokens[...].reshape(rows, D), u], axis=0).T
        for z in range(mp):
            g_qk[z] = dot(inputs_t[:, :rows], maps_back[z]).astype(BF)
        gradients.write("qk", g_qk, grad_out, sems.at[1])
        for z in range(mp):
            maps = jnp.concatenate(
                [before(value_maps[z], width), after(get_distance(query_back, z), width)], axis=0
            )
            g_vc[z] = dot(inputs_t, maps).astype(BF)
        gradients.write("vc", g_vc, grad_out, sems.at[2])
        settle(g_qk, sems.at[1])
        settle(g_vc, sems.at[2])

    found = call(
        kernel,
        (hidden, *saved),
        [HBM] + [VMEM] * count,
        shapes,
        [HBM] * len(shapes),
        [pltpu.VMEM((items, 2 * NQ, D), BF)]
        + [pltpu.VMEM((mp, D, 2 * width), BF)] * 2
        + [DMA((3,))],
        24,
    )
    return gradients.halves(found)


def place_layer(plan, two, across, far):
    mp, items = plan.mp, plan.items

    def kernel(two, across, far, out):
        me = lax.axis_index("mp")
        for j in range(mp):
            source = me ^ j
            values = two[j] if j < 2 else from_line(plan, across, far, j)
            for s in range(2):
                out[
                    pl.ds((source ^ s) * items, items),
                    pl.ds(pl.multiple_of((source & 1) * NQ, NQ), NQ),
                    :,
                ] = values[s]

    return call(
        kernel,
        (two, across, far),
        [VMEM] * 3,
        [jax.ShapeDtypeStruct((mp * items, 2 * NQ, D), BF)],
        [VMEM],
        [],
        16,
    )[0]


def place_gradient(plan, own, near, across_own, across_near, far_own, far_near):
    mp, items = plan.mp, plan.items

    def kernel(own, near, across_own, across_near, far_own, far_near, out):
        me = lax.axis_index("mp")
        end = (me == 0) | (me == mp - 1)
        found = [
            own[...],
            near[...],
            jnp.where(end, far_own[...], across_near[...]),
            jnp.where(end, far_near[...], across_own[...]),
        ]
        for j, values in enumerate(found):
            values = values.astype(F32).reshape(items, 2 * NQ, D)
            out[pl.ds((me ^ j) * items, items)] = values

    return call(
        kernel,
        (own, near, across_own, across_near, far_own, far_near),
        [VMEM] * 6,
        [jax.ShapeDtypeStruct((mp * items, 2 * NQ, D), F32)],
        [VMEM],
        [],
        24,
    )[0]


RATES = {
    "attn_in": 2.0 / math.sqrt(D),
    "attn_out": 2.0 / math.sqrt(max(D // 8, 1)),
    "cross_kv": 2.0 / math.sqrt(E),
    "ffn_up": 2.0 / math.sqrt(D),
    "ffn_down": 2.0 / math.sqrt(F),
    "vector": 0.3,
}


def adam_update(weight, first, second, grad, rate):
    first_new = BETA_ONE * first + (1.0 - BETA_ONE) * grad
    second_new = BETA_TWO * second + (1.0 - BETA_TWO) * grad * grad
    first_hat = first_new / (1.0 - BETA_ONE**STEP_COUNT)
    second_hat = second_new / (1.0 - BETA_TWO**STEP_COUNT)
    weight_new = weight - rate * (
        first_hat / (jnp.sqrt(second_hat) + ADAM_EPS) + WEIGHT_DECAY * weight
    )
    return (first_new, second_new, weight_new)


def update_into(held, outs, place, grad, rate):
    found = adam_update(held[0][place], held[1][place], held[2][place], grad, rate)
    for out, values in zip(outs, found):
        out[place] = values


def bring(sources, targets, sems):
    copies = [
        pltpu.make_async_copy(s, t, sems.at[k]) for k, (s, t) in enumerate(zip(sources, targets))
    ]
    for c in copies:
        c.start()
    return copies


def ffn_step(mine, theirs, up, down):
    rows = up[0].shape[1]

    def kernel(*refs):
        mine, theirs, sources, outs = refs[0], refs[1], refs[2:8], refs[8:14]
        held, sems = refs[14:20], refs[20]
        copies = bring(sources, held, sems)
        up, down = held[:3], held[3:]
        low = (lax.axis_index("mp") & 1) == 0
        own, other = mine[...].astype(F32), theirs[...].astype(F32)
        for copy in copies:
            copy.wait()
        for g in range(2):
            grad = jnp.where(low, own, other) if g == 0 else jnp.where(low, other, own)
            update_into(up, outs[:3], g, grad[:rows], RATES["ffn_up"])
            update_into(down, outs[3:], g, grad[rows:], RATES["ffn_down"])

    shapes = [jax.ShapeDtypeStruct(v.shape, F32) for v in up + down]
    return call(
        kernel,
        (mine, theirs, *up, *down),
        [VMEM] * 2 + [HBM] * 6,
        shapes,
        [VMEM] * 6,
        [pltpu.VMEM(v.shape, F32) for v in up + down] + [DMA((6,))],
        32,
    )


def other_steps(plan, pieces, kv_total, attn_in, out_turned, kv):
    width = plan.width
    rows = attn_in[0].shape[1]
    total = sum(p.astype(F32) for p in pieces)

    def columns(values):
        return jnp.stack([values[:, :width], values[:, width:]])

    in_grad = jnp.concatenate([columns(total[:rows]), columns(total[rows : 2 * rows])])
    found = adam_update(*attn_in, in_grad, RATES["attn_in"])
    turned = adam_update(*out_turned, columns(total[2 * rows :]), RATES["attn_out"])
    image = adam_update(*kv, columns(kv_total.astype(F32)), RATES["cross_kv"])
    return (*found, *(v.transpose(0, 2, 1) for v in turned), *image)


def vector_steps(plan, vectors, rep_, head, bias):
    me = lax.axis_index("mp")
    width, hidden_width = head[0].shape[1], bias[0].shape[1]
    head_grad = lax.dynamic_slice_in_dim(vectors[12:16], me * width, width, 1)
    bias_grad = lax.dynamic_slice_in_dim(
        vectors[16:].reshape(2, -1), me * hidden_width, hidden_width, 1
    )
    found = []
    for held, grad in ((rep_, vectors[:12]), (head, head_grad), (bias, bias_grad)):
        found.extend(adam_update(*held, grad, RATES["vector"]))
    return found


def local(
    bits,
    hidden,
    images,
    caption_len,
    cotangent,
    attn_in,
    attn_in_first,
    attn_in_second,
    attn_out,
    attn_out_first,
    attn_out_second,
    cross_key_value_maps,
    cross_kv_first,
    cross_kv_second,
    ffn_up,
    ffn_up_first,
    ffn_up_second,
    ffn_down,
    ffn_down_first,
    ffn_down_second,
    vec_rep,
    vec_rep_first,
    vec_rep_second,
    query_value_bias_rows,
    vec_head_first,
    vec_head_second,
    bias_up,
    bias_up_first,
    bias_up_second,
):
    mp = lax.axis_size("mp")
    me = lax.axis_index("mp")
    plan = Plan(bits, mp, hidden.shape[0] // mp, 2 ** (bits + 1))
    forth, back = plan.forth, plan.back
    low = (me & 1) == 0
    keys = images.shape[1]
    attn_rows, kv_rows, ffn_rows = attn_in.shape[1], cross_key_value_maps.shape[1], ffn_up.shape[1]
    oo_first = attn_rows // 32 * 16 or attn_rows // 2
    oo_second = attn_rows - oo_first

    def side(values):
        return jnp.concatenate([values[0], values[1]], axis=1)

    none = jnp.zeros_like(query_value_bias_rows[0])
    bias_rows = query_value_bias_rows
    packed = jnp.concatenate(
        [
            jnp.concatenate([bias_rows[0], none])[None],
            jnp.concatenate([bias_rows[1], bias_rows[2]])[None],
            jnp.concatenate([none, bias_rows[3]])[None],
            bias_up.reshape(-1, 2 * plan.width),
            jnp.zeros((1, 2 * plan.width), F32),
        ]
    )

    def three(values):
        found = []
        for _ in range(3):
            part = lax.reduce_precision(values, 8, 7)
            found.append(part.astype(BF))
            values = values - part
        return jnp.concatenate(found)

    low_in = attn_in.astype(BF)
    low_oo = side(attn_out.astype(BF).transpose(0, 2, 1))
    low_kv = side(cross_key_value_maps.astype(BF))
    attn_first, attn_second = attn_rows + oo_first, attn_rows + oo_second
    first_shard = jnp.concatenate(
        [
            side(low_in[:2]),
            low_oo[:oo_first],
            side(low_in[2:]),
            low_oo[oo_first:],
            three(packed),
        ]
    )
    group = me & 1
    low_ffn = jnp.concatenate([ffn_up.astype(BF), ffn_down.astype(BF).transpose(0, 2, 1)], axis=1)
    third_own = lax.dynamic_index_in_dim(low_ffn, group, 0, keepdims=False)
    third_other = lax.dynamic_index_in_dim(low_ffn, 1 - group, 0, keepdims=False)
    early, last = range(plan.bits - 1), range(plan.bits - 1, plan.bits)

    wide_columns, hidden_columns = 2 * plan.width, F // mp
    attn_parts = {
        "qk": [Part("a", 0, attn_rows, 0)],
        "vc": [Part("b", 0, attn_rows, 0)],
        "oo": [Part("a", attn_rows, oo_first, 0), Part("b", attn_rows, oo_second, oo_first)],
    }
    attn_gradients = Gradients(
        plan,
        {"a": (forth, attn_rows, wide_columns), "b": (back, attn_rows, wide_columns)},
        {"qk": (attn_parts["qk"], D), "vc": (attn_parts["vc"], D)},
        mp,
    )
    out_gradients = Gradients(
        plan,
        {"a": (forth, oo_first, wide_columns), "b": (back, oo_second, wide_columns)},
        {"oo": ([Part("a", 0, oo_first, 0), Part("b", 0, oo_second, oo_first)], D)},
        mp,
    )
    ffn_gradients = Gradients(
        plan,
        {"a": (forth, ffn_rows, hidden_columns), "b": (back, ffn_rows, hidden_columns)},
        {"up": ([Part("a", 0, ffn_rows, 0)], D), "down": ([Part("b", 0, ffn_rows, 0)], D)},
        mp,
    )

    first = mp_direct(plan, first_shard, lambda j: first_shard)
    maps = lax.all_gather(low_kv, forth + ("core",), axis=0, tiled=True)
    images = with_layout_constraint(images, Layout(major_to_minor=(0, 1, 2)))
    out_turned = tuple(
        v.transpose(0, 2, 1) for v in (attn_out, attn_out_first, attn_out_second)
    )
    first, images, third_own, third_other, out_turned = hold(
        first, images, third_own, third_other, out_turned
    )
    packed_rows = packed.shape[0]
    heads = jnp.stack([p[attn_first + attn_second :].astype(F32) for p in first])
    heads = heads.reshape(mp, 3, packed_rows, heads.shape[-1]).sum(axis=1)
    first = (
        jnp.stack([p[:attn_first] for p in first]),
        jnp.stack([p[attn_first : attn_first + attn_second] for p in first]),
    )
    near = mp_swap(third_other, 1)
    for k in early:
        got = send_pair(plan, first, k)
        if k < plan.bits - 2:
            first = join_pair(first, got)
    got, near = hold(got, near)
    first = join_pair(first, got)
    third = jnp.stack([third_own, near])
    got = send_pair(plan, first, plan.bits - 1)
    first_cores = send_cores(first)
    for distance in plan.distances[1:]:
        if distance > 2:
            third = mp_double(third, distance)
    far_up = mp_swap(third[:, :ffn_rows], 2)
    kv_all = image_maps(plan, images, packed, maps)
    got, first_cores, kv_all, far_up = hold(got, first_cores, kv_all, far_up)
    got_cores = send_cores(got)
    far_down = mp_swap(third[:, ffn_rows:], 2)

    def before_last(values, order):
        for axis in order[:-2]:
            values = jnp.concatenate([values, swap(values, axis)])
        return values, swap(values, order[-2])

    up, up_got = before_last(jnp.concatenate([third[:, :ffn_rows], far_up]), forth)
    (got_cores,) = hold(got_cores)
    attn_set = Weights(
        plan, as_trees(plan, as_quarters(first, got, first_cores, got_cores)), attn_parts
    )
    qk_all, v_all, context_all, z_first, cross, wholes = self_forward(
        plan, caption_len, hidden, vec_rep, heads, [(attn_set, ["qk", "vc", "oo"])]
    )
    whole_qk, whole_vc, whole_oo = wholes

    def exchange(values):
        return exchange_rest(values, mp_swap(values[2], 2))

    def exchange_rest(values, got):
        own, near, _ = values
        lane = lax.broadcasted_iota(jnp.int32, got.shape, 1)
        passed = mp_swap(jnp.where(lane < plan.width, near, got), 1)
        return own, passed, got

    far_down, cross, up_got = hold(far_down, cross, up_got)
    up = jnp.concatenate([up, up_got])
    down, down_got = before_last(jnp.concatenate([third[:, ffn_rows:], far_down]), back)
    queries = exchange(cross)
    (queries,) = hold(queries)
    contexts = cross_attend(plan, keys, queries, kv_all)
    contexts, down_got = hold(contexts, down_got)
    down = jnp.concatenate([down, down_got])
    half = up.shape[0] // 2
    up_last, down_last = swap(up[:half], forth[-1]), swap(down[:half], back[-1])
    context_got = mp_swap(contexts[2], 2)
    contexts, context_got, down, up, up_last, down_last = hold(
        contexts, context_got, down, up, up_last, down_last
    )
    contexts = exchange_rest(contexts, context_got)
    up_last = jnp.concatenate([up_last, swap(up[half:], forth[-1])])
    down_last = jnp.concatenate([down_last, swap(down[half:], back[-1])])
    (contexts,) = hold(contexts)
    up_core, down_core = send_cores((up, down))
    z_second, kept, given = cross_output(plan, vec_rep, z_first, contexts, whole_oo)
    kept, given = hold(kept, given)
    ffn_got = mp_swap(given, 1)
    up_last, down_last, up_core, down_core, ffn_got, kept = hold(
        up_last, down_last, up_core, down_core, ffn_got, kept
    )
    up_last_core, down_last_core = send_cores((up_last, down_last))
    up_last_core, down_last_core, ffn_got, kept = hold(
        up_last_core, down_last_core, ffn_got, kept
    )
    ffn_set = Weights(
        plan,
        as_trees(
            plan,
            (
                (up, up_last, up_core, up_last_core),
                (down, down_last, down_core, down_last_core),
            ),
        ),
        {"up": [Part("a", 0, ffn_rows, 0)], "down": [Part("b", 0, ffn_rows, 0)]},
    )
    layer, kept_back, given_back, third_sums, bias_sums, ffn_halves = feed_forward(
        plan,
        vec_rep,
        heads,
        kept,
        ffn_got,
        cotangent,
        [(ffn_set, ["up", "down"])],
        ffn_gradients,
    )
    cores = ("core", "core")
    ffn_state = ffn_halves["a"], ffn_halves["b"]
    got_back = mp_swap(given_back, 1)
    got = shrink_send(ffn_state, cores)
    got_back, got, kept_back, layer = hold(got_back, got, kept_back, layer)
    layer_near = mp_swap(layer, 1)
    ffn_state = shrink_add(ffn_state, got)
    for k in range(plan.bits - 1, 1, -1):
        ffn_state = shrink_add(ffn_state, shrink_send(ffn_state, (forth[k], back[k])))
    got = shrink_send(ffn_state, (forth[1], back[1]))
    cross_back, branch, caption_back, cross_sums, context_back = cross_output_backward(
        plan, vec_rep, z_second, kept_back, got_back, whole_oo
    )
    (context_back,) = hold(context_back)
    context_back = exchange(context_back)
    context_back, layer_near = hold(context_back, layer_near)
    layer_two = jnp.stack([layer, layer_near])
    layer_across = mp_middle(plan, layer_two)
    kv_back, value_sum, query_back = cross_attend_backward(
        plan, keys, queries, context_back, kv_all
    )
    query_back, got = hold(query_back, got)
    ffn_state = shrink_add(ffn_state, got)
    got = shrink_send(ffn_state, (forth[0], back[0]))
    kv_grad = image_gradient(plan, images, kv_back)
    query_back = exchange(query_back)
    query_back, got, layer_across, kv_grad = hold(query_back, got, layer_across, kv_grad)
    kv_total = lax.psum_scatter(
        kv_grad, forth + ("core",), scatter_dimension=0, tiled=True
    )
    ffn_state = join_trees(shrink_add(ffn_state, got))
    for distance in plan.distances[:1:-1]:
        ffn_state = mp_halve(ffn_state, distance)
    first_back, first_sums = cross_input_backward(
        plan, vec_rep, z_first, cross_back, caption_back, query_back, whole_vc
    )
    out_halves = output_gradient(plan, first_back, branch, context_all, contexts, out_gradients)
    ffn_state, first_back, out_halves = hold(ffn_state, first_back, out_halves)
    middle = ffn_rows if ffn_state[1].shape[0] == 2 else 0
    ffn_got_up = mp_swap(ffn_state[1][:, :middle], 2)
    layer_far = mp_outward(plan, layer_across)
    out_state = out_halves["a"], out_halves["b"]
    out_got = shrink_send(out_state, cores)
    token_back, vectors, maps_back, value_maps = self_backward(
        plan,
        caption_len,
        (vec_rep, first_back, qk_all, v_all),
        (first_sums, cross_sums, third_sums, bias_sums, value_sum),
        wholes,
    )
    token_back, maps_back, vectors, ffn_got_up, out_got, layer_far = hold(
        token_back, maps_back, vectors, ffn_got_up, out_got, layer_far
    )
    middle_down = (ffn_state[1].shape[1] + middle) // 2
    ffn_got_down = mp_swap(ffn_state[1][:, middle:middle_down], 2)
    across_own = mp_middle(plan, token_back)
    near = mp_swap(token_back, 1)
    out_state = shrink_add(out_state, out_got)
    for k in range(plan.bits - 1, 1, -1):
        out_state = shrink_add(out_state, shrink_send(out_state, (forth[k], back[k])))
    out_got = shrink_send(out_state, (forth[1], back[1]))
    attn_halves = self_gradient(
        plan,
        hidden,
        (vec_rep, z_first, maps_back, value_maps, *query_back),
        attn_gradients,
    )
    across_own, near, attn_halves, out_got, ffn_got_down = hold(
        across_own, near, attn_halves, out_got, ffn_got_down
    )
    attn_state = attn_halves["a"], attn_halves["b"]
    attn_got = shrink_send(attn_state, cores)
    ffn_got_rest = mp_swap(ffn_state[1][:, middle_down:], 2)
    out_state = shrink_add(out_state, out_got)
    out_got = shrink_send(out_state, (forth[0], back[0]))
    attn_got, out_got, ffn_got_rest, vectors = hold(attn_got, out_got, ffn_got_rest, vectors)
    across_near = mp_middle(plan, near)
    far_own = mp_outward(plan, across_own)
    attn_state = shrink_add(attn_state, attn_got)
    for k in range(plan.bits - 1, 1, -1):
        attn_state = shrink_add(attn_state, shrink_send(attn_state, (forth[k], back[k])))
    attn_got = shrink_send(attn_state, (forth[1], back[1]))
    out_state = shrink_add(out_state, out_got)
    vector_got = mp_swap(vectors, 1)
    attn_got, across_near, far_own, vector_got = hold(
        attn_got, across_near, far_own, vector_got
    )
    vectors = vectors + vector_got
    for distance in plan.distances[2:]:
        vectors = vectors + mp_swap(vectors, distance)
    vector_got = mp_swap(vectors, 2)
    attn_state = shrink_add(attn_state, attn_got)
    attn_got = shrink_send(attn_state, (forth[0], back[0]))
    far_near = mp_outward(plan, across_near)
    ffn_got = jnp.concatenate([ffn_got_up, ffn_got_down, ffn_got_rest], axis=1)
    half = ffn_got.shape[0] // 2
    ffn_state = (
        add_low(ffn_state[0][:half], ffn_got[:half]),
        add_low(ffn_state[0][half:], ffn_got[half:]),
    )
    theirs = mp_swap(ffn_state[1][0], 1)
    attn_got, vector_got, theirs, far_near = hold(attn_got, vector_got, theirs, far_near)
    attn_state = shrink_add(attn_state, attn_got)
    pieces = mp_scatter(plan, join_trees(attn_state + out_state))
    vectors = vectors + vector_got
    for axis in forth:
        vectors = vectors + swap(vectors, axis)
    grad_hidden = place_gradient(
        plan, token_back, near, across_own, across_near, far_own, far_near
    )
    layer_out = place_layer(plan, layer_two, layer_across, layer_far)
    turn = (0, 2, 1)
    ffn_results = ffn_step(
        ffn_state[0][0],
        theirs,
        (ffn_up, ffn_up_first, ffn_up_second),
        tuple(v.transpose(turn) for v in (ffn_down, ffn_down_first, ffn_down_second)),
    )
    vectors, grad_hidden, layer_out, ffn_results = hold(
        vectors, grad_hidden, layer_out, ffn_results
    )
    vectors = vectors + swap(vectors, "core")
    results = other_steps(
        plan,
        pieces,
        kv_total,
        (attn_in, attn_in_first, attn_in_second),
        out_turned,
        (cross_key_value_maps, cross_kv_first, cross_kv_second),
    )
    vector_results = vector_steps(
        plan,
        vectors,
        (vec_rep, vec_rep_first, vec_rep_second),
        (query_value_bias_rows, vec_head_first, vec_head_second),
        (bias_up, bias_up_first, bias_up_second),
    )
    return (
        layer_out,
        grad_hidden,
        *results,
        *ffn_results[:3],
        *(v.transpose(turn) for v in ffn_results[3:]),
        *vector_results,
    )


def solution(mesh):
    dp, mp = mesh.devices.shape
    bits = (dp // 2).bit_length() - 1
    names = tuple(f"b{k}" for k in range(bits)) + ("core",)
    fine = Mesh(mesh.devices.reshape((2,) * (bits + 1) + (mp,)), names + ("mp",))
    split = P(names)
    inward = P(None, names, "mp")
    outward = P(None, "mp", names)
    head = P(None, "mp")
    stored = (inward,) * 3 + (outward,) * 3 + (inward,) * 6 + (outward,) * 3 + (P(),) * 3 + (head,) * 6
    return jax.shard_map(
        functools.partial(local, bits),
        mesh=fine,
        in_specs=(split,) * 4 + stored,
        out_specs=(split,) * 2 + stored,
        check_vma=False,
    )
```
